256 devices in a mesh: rows: 128 (over x, y, z), cols: 2 (over core).
Axes of the slice: x: 4, y: 4, z: 8, core: 2. Of those that a mesh axis runs over, the one named last changes fastest.
Arguments:
- whitening: float32 [49152, 384], P('rows'), as said below
- sensor_states: int32 [49152, 4], P('rows'), may hold values from 0 to 1023, as said below
- sensor_coefficients: float32 [49152, 4], P('rows'), may hold values from -5 to 5
- sensor_readings: float32 [49152], P('rows'), may hold values from -6 to 6
- conduit_endpoints: int32 [16384, 2], P('rows'), may hold values from 0 to 1023
- conductance: float32 [16384], P('rows'), may hold values from 0.2 to 1
- balance_right_side: float32 [16384], P('rows'), may hold values from -3 to 3
- prior_root_factor: float32 [1024, 1024], P('rows'), as said below
- prior_information: float32 [1024], P('rows'), may hold values from -6 to 6
- transition: float32 [1024, 1024], P('cols'), may hold values from -0.1875 to 0.1875
Outputs:
- r_post: float32 [1024, 1024], P('rows', 'cols')
- z_post: float32 [1024], P('cols')
- x_next: float32 [1024], P('cols')
The draws below stay inside these ranges and needn't reach their ends.
Inputs may be any that keep to these rules, and one draw needn't show every extreme that they name: `prior_root_factor`: upper triangular, with diagonal entries between 1.5 and 3. `whitening`: each aligned block of 384 rows is a lower triangular matrix with a positive diagonal. `sensor_states`: the 4 states of a row are consecutive, counted modulo 1024.
All inputs are finite; a program needn't handle non-finite values.
Results may differ from the reference program's by a relative error of at most 0.0003.
Values sent between devices are 32-bit elements; how exact they have to be, the bound alone decides.
A program may use at most 128 MiB of HBM per device.

```python
import math
import jax
import jax.numpy as jnp
from jax import lax

STATE_TOTAL = 1024
STATES_PER_ROW = 4
BLOCK_SENSOR_ROWS = 384
BR_DEV = 128
SENSOR_ROWS = 49152
BAL = 16384
N_ROWS = 128


def draw_prior_root_factor(key, part):
    diagonal_key, offdiagonal_key = jax.random.split(jax.random.fold_in(key, 11))
    row_position = lax.broadcasted_iota(jnp.int32, (STATE_TOTAL, STATE_TOTAL), 0)
    column_position = lax.broadcasted_iota(jnp.int32, (STATE_TOTAL, STATE_TOTAL), 1)
    diagonal_portion = jax.random.uniform(diagonal_key, (STATE_TOTAL, 1), jnp.float32, 1.5, 3.0)
    offdiagonal_portion = jax.random.normal(offdiagonal_key, (STATE_TOTAL, STATE_TOTAL), jnp.float32)
    offdiagonal_portion = offdiagonal_portion * (0.3 / math.sqrt(STATE_TOTAL))
    return jnp.where(row_position == column_position, diagonal_portion, jnp.where(column_position > row_position, offdiagonal_portion, 0.0))


def draw_whitening(key, part):
    diagonal_key, offdiagonal_key = jax.random.split(jax.random.fold_in(key, 23))
    row_position = lax.broadcasted_iota(jnp.int32, (SENSOR_ROWS, BLOCK_SENSOR_ROWS), 0) % BLOCK_SENSOR_ROWS
    column_position = lax.broadcasted_iota(jnp.int32, (SENSOR_ROWS, BLOCK_SENSOR_ROWS), 1)
    diagonal_portion = jnp.exp(jax.random.uniform(diagonal_key, (SENSOR_ROWS, 1), jnp.float32, math.log(0.08), math.log(0.4)))
    offdiagonal_portion = jax.random.normal(offdiagonal_key, (SENSOR_ROWS, BLOCK_SENSOR_ROWS), jnp.float32)
    offdiagonal_portion = offdiagonal_portion * diagonal_portion * (0.5 / math.sqrt(BLOCK_SENSOR_ROWS))
    return jnp.where(row_position == column_position, diagonal_portion, jnp.where(column_position < row_position, offdiagonal_portion, 0.0))


def draw_sensor_states(key, part):
    key = jax.random.fold_in(key, 31)
    first_state = jax.random.randint(key, (SENSOR_ROWS, 1), 0, STATE_TOTAL, jnp.int32)
    offsets = lax.broadcasted_iota(jnp.int32, (SENSOR_ROWS, STATES_PER_ROW), 1)
    return (first_state + offsets) % STATE_TOTAL


def draw_sensor_coefficients(key, part):
    sign_key, size_key = jax.random.split(jax.random.fold_in(key, 37))
    signs = (2 * jax.random.randint(sign_key, (SENSOR_ROWS, 1), 0, 2, jnp.int32) - 1).astype(jnp.float32)
    magnitudes = jax.random.uniform(size_key, (SENSOR_ROWS, STATES_PER_ROW), jnp.float32, 2.0, 4.0)
    return signs * magnitudes


def touch_ends(drawn, key, smallest, largest):
    place = [jax.random.randint(jax.random.fold_in(key, axis), (), 0, length) for axis, length in enumerate(drawn.shape)]
    main_axis = drawn.shape.index(max(drawn.shape))
    beside = place[:main_axis] + [(place[main_axis] + 1) % drawn.shape[main_axis]] + place[main_axis + 1:]
    return drawn.at[tuple(place)].set(smallest).at[tuple(beside)].set(largest)


def steps_of(rng, dims, cuts, smallest, high):
    def one(dim, blocks):
        heights = jax.random.uniform(jax.random.fold_in(jax.random.fold_in(rng, 6), dim), (blocks,), jnp.float32, smallest / len(cuts), high / len(cuts))
        return jnp.repeat(jnp.exp(heights), dims[dim] // blocks).reshape((-1,) + (1,) * (len(dims) - dim - 1))

    level = one(*cuts[0])
    for cut in cuts[1:]:
        level = level * one(*cut)
    return level


def noise(own_key, shape, deviation, bound, cuts=(), kind=jnp.bfloat16):
    result = deviation * jax.random.normal(own_key, shape, jnp.float32)
    if cuts:
        result = result * steps_of(own_key, shape, cuts, -0.22, 0.18)
    return jnp.clip(result, -bound, bound).astype(kind)


def setup_inputs(seed: int = 0) -> dict:
    arg_keys = jax.random.split(jax.random.key(seed), 11)
    whitening = draw_whitening(jax.random.fold_in(arg_keys[10], 71), 0)
    sensor_states = draw_sensor_states(jax.random.fold_in(arg_keys[10], 71), 0)
    sensor_coefficients = draw_sensor_coefficients(jax.random.fold_in(arg_keys[10], 71), 0)
    sensor_readings = noise(arg_keys[3], (SENSOR_ROWS,), 1.0, 6.0, ((0, 128),), jnp.float32)
    conduit_endpoints = touch_ends(jax.random.randint(arg_keys[4], (BAL, 2), 0, STATE_TOTAL), jax.random.fold_in(arg_keys[4], 1), 0, STATE_TOTAL - 1).astype(jnp.int32)
    conductance = jnp.clip(jnp.exp(math.log(1.0) - 1.609438 * jax.random.uniform(arg_keys[5], (BAL,), jnp.float32) ** steps_of(arg_keys[5], (BAL,), ((0, 128),), -0.2, 0.2)), 0.2, 1.0)
    balance_right_side = noise(arg_keys[6], (BAL,), 0.5, 3.0, ((0, 128),), jnp.float32)
    prior_root_factor = draw_prior_root_factor(jax.random.fold_in(arg_keys[10], 71), 0)
    prior_information = noise(arg_keys[8], (STATE_TOTAL,), 1.0, 6.0, ((0, 128),), jnp.float32)
    transition = noise(arg_keys[9], (STATE_TOTAL, STATE_TOTAL), STATE_TOTAL ** -0.5, 0.1875, ((0, 2),), jnp.float32)
    return dict(whitening=whitening, sensor_states=sensor_states, sensor_coefficients=sensor_coefficients, sensor_readings=sensor_readings, conduit_endpoints=conduit_endpoints, conductance=conductance, balance_right_side=balance_right_side, prior_root_factor=prior_root_factor, prior_information=prior_information, transition=transition)


def incidence_matrix(states, coeffs, state_total_count):
    column_ids = lax.broadcasted_iota(jnp.int32, (states.shape[0], state_total_count), 1)
    summed = jnp.zeros((states.shape[0], state_total_count), jnp.float32)
    for position in range(states.shape[1]):
        summed = summed + jnp.where(column_ids == states[:, position:position + 1], coeffs[:, position:position + 1], 0.0)
    return summed

def reference(whitening, sensor_states, sensor_coefficients, sensor_readings, conduit_endpoints, conductance, balance_right_side, prior_root_factor, prior_information, transition):
    highest_accuracy = lax.Precision.HIGHEST
    white_blocks = whitening.reshape(N_ROWS, BLOCK_SENSOR_ROWS, BLOCK_SENSOR_ROWS)
    state_index_blocks = sensor_states.reshape(N_ROWS, BLOCK_SENSOR_ROWS, STATES_PER_ROW)
    coefficient_blocks = sensor_coefficients.reshape(N_ROWS, BLOCK_SENSOR_ROWS, STATES_PER_ROW)
    reading_blocks = sensor_readings.reshape(N_ROWS, BLOCK_SENSOR_ROWS)
    end_blocks = conduit_endpoints.reshape(N_ROWS, BR_DEV, 2)
    cond_blocks = conductance.reshape(N_ROWS, BR_DEV)
    brhs_blocks = balance_right_side.reshape(N_ROWS, BR_DEV)

    def add_block(carry, items):
        gram, moment = carry
        whitened_block, states_b, coeff_b, reading_block, ends_b, conductance_block, balance_right_block = items
        sensed_states = incidence_matrix(states_b, coeff_b, STATE_TOTAL)
        sensor_row_list = jnp.dot(whitened_block, sensed_states, precision=highest_accuracy)
        sensor_right_side = jnp.dot(whitened_block, reading_block, precision=highest_accuracy)
        pair_coeffs = jnp.stack([conductance_block, -conductance_block], axis=1)
        balance_row_list = incidence_matrix(ends_b, pair_coeffs, STATE_TOTAL)
        stacked_system = jnp.concatenate([sensor_row_list, balance_row_list], axis=0)
        combined_right_side = jnp.concatenate([sensor_right_side, conductance_block * balance_right_block], axis=0)
        gram = gram + jnp.dot(stacked_system.T, stacked_system, precision=highest_accuracy)
        moment = moment + jnp.dot(stacked_system.T, combined_right_side, precision=highest_accuracy)
        return ((gram, moment), None)
    gram0 = jnp.dot(prior_root_factor.T, prior_root_factor, precision=highest_accuracy)
    moment0 = jnp.dot(prior_root_factor.T, prior_information, precision=highest_accuracy)
    (gram, moment), _ = lax.scan(add_block, (gram0, moment0), (white_blocks, state_index_blocks, coefficient_blocks, reading_blocks, end_blocks, cond_blocks, brhs_blocks))
    lower_factor = jnp.linalg.cholesky(gram)
    z_col = lax.linalg.triangular_solve(lower_factor, moment[:, None], left_side=True, lower=True)
    est_col = lax.linalg.triangular_solve(lower_factor, z_col, left_side=True, lower=True, transpose_a=True)
    x_next = jnp.dot(transition, est_col[:, 0], precision=highest_accuracy)
    return (lower_factor.T, z_col[:, 0], x_next)
```

```python
import functools

import jax
import jax.numpy as jnp
from jax import lax
from jax.experimental import pallas as pl
from jax.experimental.pallas import tpu as pltpu
from jax.sharding import PartitionSpec as P

F32, BF16 = jnp.float32, jnp.bfloat16
MESH = pl.DeviceIdType.MESH
NX, NY, NZ = 4, 4, 8
SENSORS, BALANCE, PRIOR = 384, 128, 16
DEPTH = SENSORS + BALANCE + PRIOR
NN = (((1,), (0,)), ((), ()))
NT = (((1,), (1,)), ((), ()))
TN = (((0,), (0,)), ((), ()))


def dot(a, b, dims=NN):
    return lax.dot_general(a, b, dims, preferred_element_type=F32)


def split2(x):
    hi = x.astype(BF16)
    return hi, (x - hi.astype(F32)).astype(BF16)


def split3(x):
    hi = x.astype(BF16)
    rest = x - hi.astype(F32)
    mid = rest.astype(BF16)
    return hi, mid, (rest - mid.astype(F32)).astype(BF16)


def dot3(a, b, dims=NN):
    return dot(a[0], b[0], dims) + (dot(a[0], b[1], dims) + dot(a[1], b[0], dims))


def local_kernel(w_ref, st_ref, co_ref, rd_ref, en_ref, cd_ref, br_ref, pr_ref, pi_ref, p0_ref, p1_ref, sh, sl):
    core = lax.axis_index("cols")
    w = split2(w_ref[...])
    states, coeffs, ends = st_ref[...], co_ref[...], en_ref[...]
    cond_row = cd_ref[...]
    cond = jnp.transpose(jnp.broadcast_to(cond_row, (128, 128)))
    readings = split2(jnp.broadcast_to(rd_ref[...], (8, SENSORS)))
    meas = dot3(readings, w, NT)
    right = jnp.concatenate(
        [
            meas,
            jnp.broadcast_to(cond_row * br_ref[...], (8, BALANCE)),
            jnp.broadcast_to(pi_ref[...], (8, PRIOR)),
        ],
        axis=1,
    )
    right = split2(right)
    for j in range(8):
        cols = slice(128 * j, 128 * j + 128)
        ids = 128 * j + lax.broadcasted_iota(jnp.int32, (SENSORS, 128), 1)
        h = jnp.zeros((SENSORS, 128), F32)
        for k in range(4):
            h = h + jnp.where(ids == states[:, k : k + 1], coeffs[:, k : k + 1], 0.0)
        s = dot3(w, split2(h))
        bids = ids[:BALANCE]
        bal = jnp.where(bids == ends[:, 0:1], cond, 0.0) - jnp.where(bids == ends[:, 1:2], cond, 0.0)
        pri = jnp.concatenate([pr_ref[:, cols], jnp.zeros((8, 128), F32)], axis=0)
        full = split2(jnp.concatenate([s, bal, pri], axis=0))
        sh[:, cols] = full[0]
        sl[:, cols] = full[1]
        mom = dot3(right, full)
        for a in range(4):
            p0_ref[a, 36, j : j + 1, :] = mom[0:1, :]

    def emit(pair, ref):
        for base, first in ((0, pair), (8 - pair, 7 - pair)):
            rows = slice(128 * first, 128 * first + 128)
            for j0 in range(first, 8):
                cols = slice(128 * j0, 128 * j0 + 128)
                blk = dot3((sh[:, rows], sl[:, rows]), (sh[:, cols], sl[:, cols]), TN)
                blk = blk.reshape(4, 4, 8, 128)
                at = base + j0 - first
                for a in range(4):
                    for b in range(4):
                        ref[a, b * 9 + at] = blk[a, b]

    for which in range(2):
        @pl.when(core == which)
        def _():
            emit(2 * which, p0_ref)
            emit(2 * which + 1, p1_ref)


def local_part(*args):
    vmem = pl.BlockSpec(memory_space=pltpu.VMEM)
    return pl.pallas_call(
        local_kernel,
        out_shape=(
            jax.ShapeDtypeStruct((4, 37, 8, 128), F32),
            jax.ShapeDtypeStruct((4, 36, 8, 128), F32),
        ),
        in_specs=[vmem] * len(args),
        out_specs=(vmem, vmem),
        scratch_shapes=[pltpu.VMEM((DEPTH, 1024), BF16), pltpu.VMEM((DEPTH, 1024), BF16)],
        compiler_params=pltpu.CompilerParams(vmem_limit_bytes=40 * 1024 * 1024),
    )(*args)


def sum_kernel(p0, p1, g, mom, r1a, r1b, q0, q1, r2a, r2b, zs, r3, b4, s_sem, r_sem):
    row = lax.axis_index("rows")
    core = lax.axis_index("cols")
    x, y, z = row // (NY * NZ), (row // NZ) % NY, row % NZ

    def at_x(v):
        return ((v * NY + y) * NZ + z, core)

    def at_y(v):
        return ((x * NY + v) * NZ + z, core)

    def at_z(v):
        return ((x * NY + y) * NZ + v, core)

    sibling = (row, 1 - core)
    hop = lambda v, d, n: lax.rem(v + d, n)
    barrier = pltpu.get_barrier_semaphore()
    for d in range(1, 4):
        pl.semaphore_signal(barrier, inc=1, device_id=at_x(hop(x, d, NX)), device_id_type=MESH)
        pl.semaphore_signal(barrier, inc=1, device_id=at_y(hop(y, d, NY)), device_id_type=MESH)
    for d in range(1, 8):
        pl.semaphore_signal(barrier, inc=1, device_id=at_z(hop(z, d, NZ)), device_id_type=MESH)
    pl.semaphore_signal(barrier, inc=1, device_id=sibling, device_id_type=MESH)
    pl.semaphore_wait(barrier, 14)

    copies = []
    used = [0]

    def send(src, dst, to):
        n = used[0]
        used[0] += 1
        cp = pltpu.make_async_remote_copy(
            src_ref=src, dst_ref=dst, send_sem=s_sem.at[n], recv_sem=r_sem.at[n], device_id=to, device_id_type=MESH
        )
        cp.start()
        copies.append(cp)
        return cp

    wa, wb = [], []
    for d in range(1, 4):
        to = hop(x, d, NX)
        wa.append(send(p0.at[to], r1a.at[x], at_x(to)))
        to = hop(y, d, NY)
        wb.append(send(p1.at[to], r1b.at[y], at_y(to)))
    r1a[x] = p0[x]
    r1b[y] = p1[y]
    for cp in wa:
        cp.wait_recv()
    for b in range(4):
        t = slice(9 * b, 9 * b + 9)
        q0[b, 0:9] = (r1a[0, t] + r1a[1, t]) + (r1a[2, t] + r1a[3, t])
    m = (r1a[0, 36] + r1a[1, 36]) + (r1a[2, 36] + r1a[3, 36])
    for b in range(4):
        q0[b, 9] = m
    wa = [send(q0.at[hop(y, d, NY)], r2a.at[y], at_y(hop(y, d, NY))) for d in range(1, 4)]
    for cp in wb:
        cp.wait_recv()
    for b in range(4):
        t = slice(9 * b, 9 * b + 9)
        q1[b] = (r1b[0, t] + r1b[1, t]) + (r1b[2, t] + r1b[3, t])
    wb = [send(q1.at[hop(x, d, NX)], r2b.at[x], at_x(hop(x, d, NX))) for d in range(1, 4)]
    r2a[y] = q0[y]
    r2b[x] = q1[x]
    for cp in wa:
        cp.wait_recv()
    a0 = (r2a[0] + r2a[1]) + (r2a[2] + r2a[3])
    for cp in wb:
        cp.wait_recv()
    a1 = (r2b[0] + r2b[1]) + (r2b[2] + r2b[3])
    for n in range(3):
        zs[n, 0:3] = a0[3 * n : 3 * n + 3]
        zs[3 + n, 0:3] = a1[3 * n : 3 * n + 3]
    for n in range(2):
        zs[6 + n, 0:3] = jnp.zeros((3, 8, 128), F32)
    for n in range(8):
        zs[n, 3] = a0[9]
    wz = [send(zs.at[hop(z, d, NZ)], r3.at[z], at_z(hop(z, d, NZ))) for d in range(1, 8)]
    r3[z] = zs[z]
    for cp in wz:
        cp.wait_recv()
    total = ((r3[0] + r3[1]) + (r3[2] + r3[3])) + ((r3[4] + r3[5]) + (r3[6] + r3[7]))
    mom[...] = total[3]
    b4[z] = total[0:3]
    wz = [send(b4.at[z], b4.at[z], at_z(hop(z, d, NZ))) for d in range(1, 8)]
    for cp in wz:
        cp.wait_recv()
    for n in range(3):
        g[core, 0, x, y, 3 * n : 3 * n + 3] = b4[n]
        g[core, 1, y, x, 3 * n : 3 * n + 3] = b4[3 + n]
    wa, wb = [], []
    for d in range(1, 4):
        mine = g.at[core, 0, x, y]
        wa.append(send(mine, mine, at_y(hop(y, d, NY))))
        mine = g.at[core, 1, y, x]
        wb.append(send(mine, mine, at_x(hop(x, d, NX))))
    for cp in wa:
        cp.wait_recv()
    mine = g.at[core, 0, x]
    wa = [send(mine, mine, at_x(hop(x, d, NX))) for d in range(1, 4)]
    last = [send(mine, mine, sibling)]
    for cp in wb:
        cp.wait_recv()
    mine = g.at[core, 1, y]
    wb = [send(mine, mine, at_y(hop(y, d, NY))) for d in range(1, 4)]
    last.append(send(mine, mine, sibling))
    for d in range(1, 4):
        wa[d - 1].wait_recv()
        got = g.at[core, 0, hop(x, NX - d, NX)]
        last.append(send(got, got, sibling))
        wb[d - 1].wait_recv()
        got = g.at[core, 1, hop(y, NY - d, NY)]
        last.append(send(got, got, sibling))
    for cp in last:
        cp.wait_recv()
    for cp in copies:
        cp.wait_send()


N_COPIES = 46


def sum_over_chips(p0, p1):
    vmem = pl.BlockSpec(memory_space=pltpu.VMEM)
    tiles = lambda *lead: pltpu.VMEM(lead + (8, 128), F32)
    return pl.pallas_call(
        sum_kernel,
        out_shape=(
            jax.ShapeDtypeStruct((2, 2, 4, 4, 9, 8, 128), F32),
            jax.ShapeDtypeStruct((8, 128), F32),
        ),
        in_specs=[vmem, vmem],
        out_specs=(vmem, vmem),
        scratch_shapes=[
            tiles(4, 37),
            tiles(4, 36),
            tiles(4, 10),
            tiles(4, 9),
            tiles(4, 10),
            tiles(4, 9),
            tiles(8, 4),
            tiles(8, 4),
            tiles(8, 3),
            pltpu.SemaphoreType.DMA((N_COPIES,)),
            pltpu.SemaphoreType.DMA((N_COPIES,)),
        ],
        compiler_params=pltpu.CompilerParams(
            collective_id=0, has_side_effects=True, vmem_limit_bytes=40 * 1024 * 1024
        ),
    )(p0, p1)


def bc(row, lane):
    return jnp.broadcast_to(row[:, lane : lane + 1], (1, 128))


def factor_block(ds, rd):
    lane = lax.broadcasted_iota(jnp.int32, (1, 128), 1)
    rows = [ds[s : s + 1, :] for s in range(8)]
    a = {(s, t): bc(rows[s], t) for s in range(8) for t in range(s, 8)}
    for g in range(16):
        r0 = 8 * g
        own = (lane >= r0) & (lane < r0 + 8)
        last = g == 15
        p = list(rows)
        v = [jnp.where(lane == r0 + s, 1.0, 0.0).astype(F32) for s in range(8)]
        u, w = [], []
        if not last:
            nxt = [jnp.where(own, 0.0, ds[r0 + 8 + t : r0 + 9 + t, :]) for t in range(8)]
            na = {(s, t): bc(nxt[s], r0 + 8 + t) for s in range(8) for t in range(s, 8)}
        for s in range(8):
            inv = lax.rsqrt(a[s, s])
            l = {t: a[s, t] * inv for t in range(s + 1, 8)}
            for t in range(s + 1, 8):
                for q in range(t, 8):
                    a[t, q] = a[t, q] - l[t] * l[q]
            us = p[s] * inv
            vs = v[s] * inv
            for t in range(s + 1, 8):
                p[t] = p[t] - l[t] * us
                v[t] = v[t] - l[t] * vs
            ws = jnp.where(own, vs, us)
            u.append(us)
            w.append(ws)
            rd[r0 + s : r0 + s + 1, :] = jnp.where(lane >= r0 + s, us, 0.0)
            ds[r0 + s : r0 + s + 1, :] = jnp.where(lane < r0 + 8, ws, 0.0)
            if not last:
                m = [bc(us, r0 + 8 + t) for t in range(8)]
                for t in range(8):
                    nxt[t] = nxt[t] - m[t] * ws
                    for q in range(t, 8):
                        na[t, q] = na[t, q] - m[t] * m[q]
        if not last:
            rows, a = nxt, na
        if g < 14:
            uh, um, ul = split3(jnp.concatenate(u, axis=0))
            wh, wm, wl = split3(jnp.concatenate(w, axis=0))
            lhs = jnp.concatenate([uh, uh, um, uh, ul, um], axis=0)
            rhs = jnp.concatenate([wh, wm, wh, wl, wh, wm], axis=0)
            upd = dot(lhs, rhs, TN)
            t0 = r0 + 16
            ds[t0:, :] = jnp.where(own, 0.0, ds[t0:, :]) - upd[t0:, :]


def solve_kernel(g_ref, m_ref, t_ref, r_ref, z_ref, x_ref, a_s, ds, rd, di_s, rp_s, zv, t_s, g_sem, t_sem):
    row_id = lax.axis_index("rows")
    core = lax.axis_index("cols")
    loads = []
    for bi in range(8):
        pair = min(bi, 7 - bi)
        base = 0 if bi < 4 else 8 - pair
        for bj in range(bi, 8):
            cp = pltpu.make_async_copy(
                g_ref.at[pair, :, base + bj - bi], a_s.at[bi, :, :, pl.ds(128 * bj, 128)], g_sem.at[bi, bj]
            )
            cp.start()
            loads.append(cp)
    t_load = pltpu.make_async_copy(t_ref, t_s, t_sem)
    t_load.start()
    for i in range(8):
        col = jnp.transpose(jnp.broadcast_to(m_ref[i : i + 1, :], (128, 128)))
        a_s[i, :, :, 1024:] = col.reshape(16, 8, 128)
    for cp in loads:
        cp.wait()

    def block(i, j):
        return a_s[i, :, :, pl.ds(pl.multiple_of(j * 128, 128), 128)].reshape(128, 128)

    def put(i, j, val):
        a_s[i, :, :, pl.ds(pl.multiple_of(j * 128, 128), 128)] = val.reshape(16, 8, 128)

    def panel(k, _):
        ds[...] = block(k, k)
        factor_block(ds, rd)
        di = ds[...]
        di_s[k] = di
        dh, dl = split2(di)
        dcat = jnp.concatenate([dh, dl, dh], axis=1)

        def col(j, _):
            cols = pl.ds(pl.multiple_of(j * 128, 128), 128)
            ah, al = split2(block(k, j))
            r = dot(dcat, jnp.concatenate([ah, ah, al], axis=0))
            put(k, j, r)
            rh, rl = split2(r)
            rp_s[0:128, cols] = rh
            rp_s[128:256, cols] = rh
            rp_s[256:384, cols] = rl
            return 0

        lax.fori_loop(k + 1, 9, col, 0)
        put(k, k, rd[...])

        def trail(i, _):
            th, tl = split2(jnp.transpose(block(k, i)))
            lhs = jnp.concatenate([th, tl, th], axis=1)

            def one(j, _):
                cols = pl.ds(pl.multiple_of(j * 128, 128), 128)
                put(i, j, block(i, j) - dot(lhs, rp_s[:, cols]))
                return 0

            lax.fori_loop(i, 9, one, 0)
            return 0

        lax.fori_loop(k + 1, 8, trail, 0)
        return 0

    lax.fori_loop(0, 8, panel, 0)

    y = [jnp.transpose(block(i, 8))[0:8, :] for i in range(8)]
    for i in range(8):
        zv[i : i + 1, :] = y[i][0:1, :]
    z_ref[...] = zv[pl.ds(core * 4, 4), :]
    e = [None] * 8
    for k in range(7, -1, -1):
        e[k] = dot3(split2(y[k]), split2(di_s[k]))
        if k:
            r = a_s[0:k, :, :, 128 * k : 128 * k + 128].reshape(128 * k, 128)
            upd = dot3(split2(e[k]), split2(r), NT)
            for p in range(k):
                y[p] = y[p] - upd[:, 128 * p : 128 * p + 128]
    t_load.wait()
    x = dot3(split2(jnp.concatenate(e, axis=1)), split2(t_s[...]), NT)
    x_ref[...] = x[0:1, :]
    mine = a_s[row_id // 16, row_id % 16, :, pl.ds(pl.multiple_of(core * 512, 512), 512)]
    at_row = row_id * 8 + lax.broadcasted_iota(jnp.int32, (8, 512), 0)
    at_col = core * 512 + lax.broadcasted_iota(jnp.int32, (8, 512), 1)
    r_ref[...] = jnp.where(at_col >= at_row, mine, 0.0)


def solve(g, m, t):
    vmem = pl.BlockSpec(memory_space=pltpu.VMEM)
    hbm = pl.BlockSpec(memory_space=pl.ANY)
    return pl.pallas_call(
        solve_kernel,
        out_shape=(
            jax.ShapeDtypeStruct((8, 512), F32),
            jax.ShapeDtypeStruct((4, 128), F32),
            jax.ShapeDtypeStruct((1, 512), F32),
        ),
        in_specs=[hbm, vmem, hbm],
        out_specs=(vmem, vmem, vmem),
        scratch_shapes=[
            pltpu.VMEM((8, 16, 8, 1152), F32),
            pltpu.VMEM((128, 128), F32),
            pltpu.VMEM((128, 128), F32),
            pltpu.VMEM((8, 128, 128), F32),
            pltpu.VMEM((384, 1152), BF16),
            pltpu.VMEM((8, 128), F32),
            pltpu.VMEM((512, 1024), F32),
            pltpu.SemaphoreType.DMA((8, 8)),
            pltpu.SemaphoreType.DMA,
        ],
        compiler_params=pltpu.CompilerParams(vmem_limit_bytes=40 * 1024 * 1024),
    )(g, m, t)


def per_device(
    whitening,
    sensor_states,
    sensor_coefficients,
    sensor_readings,
    conduit_endpoints,
    conductance,
    balance_right_side,
    prior_root_factor,
    prior_information,
    transition,
):
    prior_row = jnp.concatenate([prior_information, jnp.zeros((PRIOR - 8,), F32)])
    p0, p1 = local_part(
        whitening,
        sensor_states,
        sensor_coefficients,
        sensor_readings.reshape(1, SENSORS),
        conduit_endpoints,
        conductance.reshape(1, BALANCE),
        balance_right_side.reshape(1, BALANCE),
        prior_root_factor,
        prior_row.reshape(1, PRIOR),
    )
    g, moment = sum_over_chips(p0, p1)
    r_post, z_post, x_next = solve(g.reshape(4, 16, 9, 8, 128), moment, transition)
    return r_post, z_post.reshape(512), x_next.reshape(512)


def solution(mesh):
    in_specs = (
        P("rows", None),
        P("rows", None),
        P("rows", None),
        P("rows"),
        P("rows", None),
        P("rows"),
        P("rows"),
        P("rows", None),
        P("rows"),
        P("cols", None),
    )
    out_specs = (P("rows", "cols"), P("cols"), P("cols"))
    return jax.shard_map(
        per_device, mesh=mesh, in_specs=in_specs, out_specs=out_specs, check_vma=False
    )
```

```python
import functools

import jax
import jax.numpy as jnp
from jax import lax
from jax.experimental import pallas as pl
from jax.experimental.pallas import tpu as pltpu
from jax.sharding import PartitionSpec as P

F32, BF16 = jnp.float32, jnp.bfloat16
MESH = pl.DeviceIdType.MESH
NX, NY, NZ = 4, 4, 8
SENSORS, BALANCE = 384, 128
NN = (((1,), (0,)), ((), ()))
NT = (((1,), (1,)), ((), ()))
TN = (((0,), (0,)), ((), ()))


def dot(a, b, dims=NN):
    return lax.dot_general(a, b, dims, preferred_element_type=F32)


def split2(x):
    hi = x.astype(BF16)
    return hi, (x - hi.astype(F32)).astype(BF16)


def split3(x):
    hi = x.astype(BF16)
    rest = x - hi.astype(F32)
    mid = rest.astype(BF16)
    return hi, mid, (rest - mid.astype(F32)).astype(BF16)


def dot3(a, b, dims=NN):
    return dot(a[0], b[0], dims) + (dot(a[0], b[1], dims) + dot(a[1], b[0], dims))


def local_kernel(
    w_in, st_in, co_in, rd_in, en_in, cd_in, br_in, pr_in, pi_in, p0_ref, p1_ref,
    w_ref, st_ref, co_ref, rd_ref, en_ref, cd_ref, br_ref, pr_ref, pi_ref, sf, sr, sp, sem,
):
    core = lax.axis_index("cols")
    pairs = [
        (st_in, st_ref), (co_in, co_ref), (en_in, en_ref), (cd_in, cd_ref), (br_in, br_ref),
        (pr_in, pr_ref), (pi_in, pi_ref), (rd_in, rd_ref), (w_in, w_ref),
    ]
    loads = [pltpu.make_async_copy(x, y, sem.at[n]) for n, (x, y) in enumerate(pairs)]
    for cp in loads:
        cp.start()
    for cp in loads:
        cp.wait()
    w = split2(w_ref[...])
    wcat = jnp.concatenate([w[0], w[1], w[0]], axis=1)
    spread = lambda row: jnp.transpose(jnp.broadcast_to(row, (128, 128)))
    cond_row = cd_ref[...]
    cond = spread(cond_row)
    ends = [spread(en_ref[k : k + 1, :].astype(F32)).astype(jnp.int32) for k in range(2)]
    info = jnp.concatenate([pi_ref[...], jnp.zeros((1, 120), F32)], axis=1)
    info = spread(info)[0:8, :]
    readings = jnp.concatenate([rd_ref[k : k + 1, :] for k in range(3)], axis=1)
    meas = dot3(split2(jnp.broadcast_to(readings, (8, SENSORS))), w, NT)
    right = split2(jnp.concatenate([meas, jnp.broadcast_to(cond_row * br_ref[...], (8, BALANCE))], axis=1))
    rcat = jnp.concatenate([right[0], right[1], right[0]], axis=1)
    for j in range(8):
        cols = slice(128 * j, 128 * j + 128)
        ids = 128 * j + lax.broadcasted_iota(jnp.int32, (128, SENSORS), 0)
        h = jnp.zeros((128, SENSORS), F32)
        for k in range(4):
            h = h + jnp.where(ids == st_ref[k : k + 1, :], co_ref[k : k + 1, :], 0.0)
        hh, hl = split2(h)
        s = dot(wcat, jnp.concatenate([hh, hh, hl], axis=1), NT)
        bids = 128 * j + lax.broadcasted_iota(jnp.int32, (BALANCE, 128), 1)
        bal = jnp.where(bids == ends[0], cond, 0.0) - jnp.where(bids == ends[1], cond, 0.0)
        full = jnp.concatenate([s, bal], axis=0)
        sf[:, cols] = full
        fh, fl = split2(full)
        sr[0:512, cols] = fh
        sr[512:1024, cols] = fh
        sr[1024:1536, cols] = fl
        prior = pr_ref[:, cols]
        ph, pm, pl_ = split3(prior)
        sp[0, :, cols] = jnp.concatenate([ph, ph, pm, ph, pl_, pm], axis=0)
        sp[1, :, cols] = jnp.concatenate([ph, pm, ph, pl_, ph, pm], axis=0)
        mom = dot(rcat, sr[:, cols])[0:1, :] + jnp.sum(prior * info, axis=0, keepdims=True)
        for a in range(4):
            p0_ref[a, 36, j : j + 1, :] = mom

    def emit(pair, ref):
        for base, first in ((0, pair), (8 - pair, 7 - pair)):
            rows = slice(128 * first, 128 * first + 128)
            th, tl = split2(jnp.concatenate([jnp.transpose(sf[128 * n : 128 * n + 128, rows]) for n in range(4)], axis=1))
            lhs = jnp.concatenate([th, tl, th], axis=1)
            for j0 in range(first, 8, 2):
                j1 = min(j0 + 2, 8)
                cols = slice(128 * j0, 128 * j1)
                wide = dot(lhs, sr[:, cols]) + dot(sp[0, :, rows], sp[1, :, cols], TN)
                for j in range(j0, j1):
                    blk = wide[:, 128 * (j - j0) : 128 * (j - j0) + 128].reshape(4, 4, 8, 128)
                    at = base + j - first
                    for a in range(4):
                        for b in range(4):
                            ref[a, b * 9 + at] = blk[a, b]

    for which in range(2):
        @pl.when(core == which)
        def _():
            emit(2 * which, p0_ref)
            emit(2 * which + 1, p1_ref)


def local_part(*args):
    vmem = pl.BlockSpec(memory_space=pltpu.VMEM)
    return pl.pallas_call(
        local_kernel,
        out_shape=(
            jax.ShapeDtypeStruct((4, 37, 8, 128), F32),
            jax.ShapeDtypeStruct((4, 36, 8, 128), F32),
        ),
        in_specs=[pl.BlockSpec(memory_space=pltpu.HBM)] * len(args),
        out_specs=(vmem, vmem),
        scratch_shapes=[pltpu.VMEM(x.shape, x.dtype) for x in args]
        + [
            pltpu.VMEM((512, 1024), F32),
            pltpu.VMEM((1536, 1024), BF16),
            pltpu.VMEM((2, 48, 1024), BF16),
            pltpu.SemaphoreType.DMA((9,)),
        ],
        compiler_params=pltpu.CompilerParams(vmem_limit_bytes=62 * 1024 * 1024),
    )(*args)


def sum_kernel(p0, p1, g, mom, r1a, r1b, q0, q1, r2a, r2b, zs, r3, b4, s_sem, r_sem):
    row = lax.axis_index("rows")
    core = lax.axis_index("cols")
    x, y, z = row // (NY * NZ), (row // NZ) % NY, row % NZ

    def at_x(v):
        return ((v * NY + y) * NZ + z, core)

    def at_y(v):
        return ((x * NY + v) * NZ + z, core)

    def at_z(v):
        return ((x * NY + y) * NZ + v, core)

    sibling = (row, 1 - core)
    hop = lambda v, d, n: lax.rem(v + d, n)
    barrier = pltpu.get_barrier_semaphore()
    for d in range(1, 4):
        pl.semaphore_signal(barrier, inc=1, device_id=at_x(hop(x, d, NX)), device_id_type=MESH)
        pl.semaphore_signal(barrier, inc=1, device_id=at_y(hop(y, d, NY)), device_id_type=MESH)
    for d in range(1, 8):
        pl.semaphore_signal(barrier, inc=1, device_id=at_z(hop(z, d, NZ)), device_id_type=MESH)
    pl.semaphore_signal(barrier, inc=1, device_id=sibling, device_id_type=MESH)
    pl.semaphore_wait(barrier, 14)

    copies = []
    used = [0]

    def send(src, dst, to):
        n = used[0]
        used[0] += 1
        cp = pltpu.make_async_remote_copy(
            src_ref=src, dst_ref=dst, send_sem=s_sem.at[n], recv_sem=r_sem.at[n], device_id=to, device_id_type=MESH
        )
        cp.start()
        copies.append(cp)
        return cp

    wa, wb = [], []
    for d in range(1, 4):
        to = hop(x, d, NX)
        wa.append(send(p0.at[to], r1a.at[x], at_x(to)))
        to = hop(y, d, NY)
        wb.append(send(p1.at[to], r1b.at[y], at_y(to)))
    r1a[x] = p0[x]
    r1b[y] = p1[y]
    for cp in wa:
        cp.wait_recv()
    for b in range(4):
        t = slice(9 * b, 9 * b + 9)
        q0[b, 0:9] = (r1a[0, t] + r1a[1, t]) + (r1a[2, t] + r1a[3, t])
    m = (r1a[0, 36] + r1a[1, 36]) + (r1a[2, 36] + r1a[3, 36])
    for b in range(4):
        q0[b, 9] = m
    wa = [send(q0.at[hop(y, d, NY)], r2a.at[y], at_y(hop(y, d, NY))) for d in range(1, 4)]
    for cp in wb:
        cp.wait_recv()
    for b in range(4):
        t = slice(9 * b, 9 * b + 9)
        q1[b] = (r1b[0, t] + r1b[1, t]) + (r1b[2, t] + r1b[3, t])
    wb = [send(q1.at[hop(x, d, NX)], r2b.at[x], at_x(hop(x, d, NX))) for d in range(1, 4)]
    r2a[y] = q0[y]
    r2b[x] = q1[x]
    for cp in wa:
        cp.wait_recv()
    a0 = (r2a[0] + r2a[1]) + (r2a[2] + r2a[3])
    for cp in wb:
        cp.wait_recv()
    a1 = (r2b[0] + r2b[1]) + (r2b[2] + r2b[3])
    for n in range(3):
        zs[n, 0:3] = a0[3 * n : 3 * n + 3]
        zs[3 + n, 0:3] = a1[3 * n : 3 * n + 3]
    for n in range(2):
        zs[6 + n, 0:3] = jnp.zeros((3, 8, 128), F32)
    for n in range(8):
        zs[n, 3] = a0[9]
    wz = [send(zs.at[hop(z, d, NZ)], r3.at[z], at_z(hop(z, d, NZ))) for d in range(1, 8)]
    r3[z] = zs[z]
    for cp in wz:
        cp.wait_recv()
    total = ((r3[0] + r3[1]) + (r3[2] + r3[3])) + ((r3[4] + r3[5]) + (r3[6] + r3[7]))
    mom[...] = total[3]
    b4[z] = total[0:3]
    wz = [send(b4.at[z], b4.at[z], at_z(hop(z, d, NZ))) for d in range(1, 8)]
    for cp in wz:
        cp.wait_recv()
    for n in range(3):
        g[core, 0, x, y, 3 * n : 3 * n + 3] = b4[n]
        g[core, 1, y, x, 3 * n : 3 * n + 3] = b4[3 + n]
    wa, wb = [], []
    for d in range(1, 4):
        mine = g.at[core, 0, x, y]
        wa.append(send(mine, mine, at_y(hop(y, d, NY))))
        mine = g.at[core, 1, y, x]
        wb.append(send(mine, mine, at_x(hop(x, d, NX))))
    for cp in wa:
        cp.wait_recv()
    mine = g.at[core, 0, x]
    wa = [send(mine, mine, at_x(hop(x, d, NX))) for d in range(1, 4)]
    last = [send(mine, mine, sibling)]
    for cp in wb:
        cp.wait_recv()
    mine = g.at[core, 1, y]
    wb = [send(mine, mine, at_y(hop(y, d, NY))) for d in range(1, 4)]
    last.append(send(mine, mine, sibling))
    for d in range(1, 4):
        wa[d - 1].wait_recv()
        got = g.at[core, 0, hop(x, NX - d, NX)]
        last.append(send(got, got, sibling))
        wb[d - 1].wait_recv()
        got = g.at[core, 1, hop(y, NY - d, NY)]
        last.append(send(got, got, sibling))
    for cp in last:
        cp.wait_recv()
    for cp in copies:
        cp.wait_send()


N_COPIES = 46


def sum_over_chips(p0, p1):
    vmem = pl.BlockSpec(memory_space=pltpu.VMEM)
    tiles = lambda *lead: pltpu.VMEM(lead + (8, 128), F32)
    return pl.pallas_call(
        sum_kernel,
        out_shape=(
            jax.ShapeDtypeStruct((2, 2, 4, 4, 9, 8, 128), F32),
            jax.ShapeDtypeStruct((8, 128), F32),
        ),
        in_specs=[vmem, vmem],
        out_specs=(vmem, vmem),
        scratch_shapes=[
            tiles(4, 37),
            tiles(4, 36),
            tiles(4, 10),
            tiles(4, 9),
            tiles(4, 10),
            tiles(4, 9),
            tiles(8, 4),
            tiles(8, 4),
            tiles(8, 3),
            pltpu.SemaphoreType.DMA((N_COPIES,)),
            pltpu.SemaphoreType.DMA((N_COPIES,)),
        ],
        compiler_params=pltpu.CompilerParams(
            collective_id=0, has_side_effects=True, vmem_limit_bytes=62 * 1024 * 1024
        ),
    )(p0, p1)


def lane_bc(x, lane):
    return jnp.broadcast_to(x[:, lane : lane + 1], (8, 128))


def row_bc(x, row):
    return jnp.broadcast_to(x[row : row + 1, :], (8, 128))


def factor_block(ds, rd, lt):
    lane = lax.broadcasted_iota(jnp.int32, (8, 128), 1)
    sub = lax.broadcasted_iota(jnp.int32, (8, 128), 0)
    t = [ds[8 * j : 8 * j + 8, :] for j in range(16)]
    c = [lane_bc(t[0], q) for q in range(8)]
    for g in range(16):
        r0 = 8 * g
        own = (lane >= r0) & (lane < r0 + 8)
        below = range(g + 1, 16)
        b = {j: [lane_bc(t[j], r0 + q) for q in range(8)] for j in below}
        if g < 15:
            nc = [lane_bc(t[g + 1], r0 + 8 + q) for q in range(8)]
        p = jnp.where(own, jnp.where(lane - r0 == sub, 1.0, 0.0), t[g])
        for j in below:
            t[j] = jnp.where(own, 0.0, t[j])
        w = []
        low = jnp.zeros((8, 128), F32)
        for s in range(8):
            inv = lax.rsqrt(row_bc(c[s], s))
            col = c[s] * inv
            mult = {q: row_bc(col, q) for q in range(s + 1, 8)}
            for q in range(s + 1, 8):
                c[q] = c[q] - col * mult[q]
            ws = row_bc(p, s) * inv
            if s < 7:
                p = p - col * ws
            low = jnp.where(lane == r0 + s, col, low)
            for j in below:
                m = b[j][s] * inv
                for q in range(s + 1, 8):
                    b[j][q] = b[j][q] - m * mult[q]
                t[j] = t[j] - m * ws
                if j == g + 1:
                    for q in range(8):
                        nc[q] = nc[q] - m * row_bc(m, q)
            w.append(ws)
        full = w[0]
        for s in range(1, 8):
            full = jnp.where(sub == s, w[s], full)
        rd[r0 : r0 + 8, :] = jnp.where(lane >= r0 + 8, full, 0.0)
        ds[r0 : r0 + 8, :] = jnp.where(lane < r0 + 8, full, 0.0)
        lt[r0 : r0 + 8, :] = low
        if g < 15:
            c = nc
    rd[...] = rd[...] + jnp.transpose(lt[...])


def solve_kernel(g_ref, m_ref, t_ref, r_ref, z_ref, x_ref, a_s, ds, rd, lt, di_s, rp_s, zv, t_s, g_sem, t_sem):
    row_id = lax.axis_index("rows")
    core = lax.axis_index("cols")
    loads = []
    for bi in range(8):
        pair = min(bi, 7 - bi)
        base = 0 if bi < 4 else 8 - pair
        for bj in range(bi, 8):
            cp = pltpu.make_async_copy(
                g_ref.at[pair, :, base + bj - bi], a_s.at[bi, :, :, pl.ds(128 * bj, 128)], g_sem.at[bi, bj]
            )
            cp.start()
            loads.append(cp)
    t_load = pltpu.make_async_copy(t_ref, t_s, t_sem)
    t_load.start()
    for i in range(8):
        col = jnp.transpose(jnp.broadcast_to(m_ref[i : i + 1, :], (128, 128)))
        a_s[i, :, :, 1024:] = col.reshape(16, 8, 128)
    for cp in loads:
        cp.wait()

    def block(i, j):
        at = slice(128 * j, 128 * j + 128) if isinstance(j, int) else pl.ds(pl.multiple_of(j * 128, 128), 128)
        return a_s[i, :, :, at].reshape(128, 128)

    def put(i, j, val):
        a_s[i, :, :, pl.ds(pl.multiple_of(j * 128, 128), 128)] = val.reshape(16, 8, 128)

    def panel(k, _):
        ds[...] = block(k, k)
        factor_block(ds, rd, lt)
        di = ds[...]
        di_s[k] = di
        dh, dl = split2(di)
        dcat = jnp.concatenate([dh, dl, dh], axis=1)

        def columns(first):
            cols = slice(128 * first, 1152)
            ah, al = split2(a_s[k, :, :, cols].reshape(128, -1))
            r = dot(dcat, jnp.concatenate([ah, ah, al], axis=0))
            a_s[k, :, :, cols] = r.reshape(16, 8, -1)
            rh, rl = split2(r)
            rp_s[0:128, cols] = rh
            rp_s[128:256, cols] = rh
            rp_s[256:384, cols] = rl

        @pl.when(k < 4)
        def _():
            columns(1)

        @pl.when(k >= 4)
        def _():
            columns(5)

        put(k, k, rd[...])

        for i in range(1, 8):

            @pl.when(i > k)
            def _():
                cols = slice(128 * i, 1152)
                th, tl = split2(jnp.transpose(block(k, i)))
                lhs = jnp.concatenate([th, tl, th], axis=1)
                a_s[i, :, :, cols] = a_s[i, :, :, cols] - dot(lhs, rp_s[:, cols]).reshape(16, 8, -1)

        return 0

    lax.fori_loop(0, 8, panel, 0)

    y = [jnp.transpose(block(i, 8))[0:8, :] for i in range(8)]
    for i in range(8):
        zv[i : i + 1, :] = y[i][0:1, :]
    z_ref[...] = zv[pl.ds(core * 4, 4), :]
    e = [None] * 8
    for k in range(7, -1, -1):
        e[k] = dot3(split2(y[k]), split2(di_s[k]))
        if k:
            r = a_s[0:k, :, :, 128 * k : 128 * k + 128].reshape(128 * k, 128)
            upd = dot3(split2(e[k]), split2(r), NT)
            for p in range(k):
                y[p] = y[p] - upd[:, 128 * p : 128 * p + 128]
    t_load.wait()
    x = dot3(split2(jnp.concatenate(e, axis=1)), split2(t_s[...]), NT)
    x_ref[...] = x[0:1, :]
    mine = a_s[row_id // 16, row_id % 16, :, pl.ds(pl.multiple_of(core * 512, 512), 512)]
    at_row = row_id * 8 + lax.broadcasted_iota(jnp.int32, (8, 512), 0)
    at_col = core * 512 + lax.broadcasted_iota(jnp.int32, (8, 512), 1)
    r_ref[...] = jnp.where(at_col >= at_row, mine, 0.0)


def solve(g, m, t):
    vmem = pl.BlockSpec(memory_space=pltpu.VMEM)
    hbm = pl.BlockSpec(memory_space=pltpu.HBM)
    return pl.pallas_call(
        solve_kernel,
        out_shape=(
            jax.ShapeDtypeStruct((8, 512), F32),
            jax.ShapeDtypeStruct((4, 128), F32),
            jax.ShapeDtypeStruct((1, 512), F32),
        ),
        in_specs=[pl.BlockSpec(memory_space=pl.ANY), vmem, hbm],
        out_specs=(vmem, vmem, vmem),
        scratch_shapes=[
            pltpu.VMEM((8, 16, 8, 1152), F32),
            pltpu.VMEM((128, 128), F32),
            pltpu.VMEM((128, 128), F32),
            pltpu.VMEM((128, 128), F32),
            pltpu.VMEM((8, 128, 128), F32),
            pltpu.VMEM((384, 1152), BF16),
            pltpu.VMEM((8, 128), F32),
            pltpu.VMEM((512, 1024), F32),
            pltpu.SemaphoreType.DMA((8, 8)),
            pltpu.SemaphoreType.DMA,
        ],
        compiler_params=pltpu.CompilerParams(vmem_limit_bytes=62 * 1024 * 1024),
    )(g, m, t)


def per_device(
    whitening,
    sensor_states,
    sensor_coefficients,
    sensor_readings,
    conduit_endpoints,
    conductance,
    balance_right_side,
    prior_root_factor,
    prior_information,
    transition,
):
    p0, p1 = local_part(
        whitening,
        sensor_states.T,
        sensor_coefficients.T,
        sensor_readings.reshape(3, 128),
        conduit_endpoints.T,
        conductance.reshape(1, BALANCE),
        balance_right_side.reshape(1, BALANCE),
        prior_root_factor,
        prior_information.reshape(1, 8),
    )
    g, moment = sum_over_chips(p0, p1)
    r_post, z_post, x_next = solve(g.reshape(4, 16, 9, 8, 128), moment, transition)
    return r_post, z_post.reshape(512), x_next.reshape(512)


def solution(mesh):
    in_specs = (
        P("rows", None),
        P("rows", None),
        P("rows", None),
        P("rows"),
        P("rows", None),
        P("rows"),
        P("rows"),
        P("rows", None),
        P("rows"),
        P("cols", None),
    )
    out_specs = (P("rows", "cols"), P("cols"), P("cols"))
    return jax.shard_map(
        per_device, mesh=mesh, in_specs=in_specs, out_specs=out_specs, check_vma=False
    )
```

```python
import jax
import jax.numpy as jnp
from jax import lax
from jax.experimental import pallas as pl
from jax.experimental.pallas import tpu as pltpu
from jax.sharding import PartitionSpec as P

F32, BF16 = jnp.float32, jnp.bfloat16
MESH = pl.DeviceIdType.MESH
NX, NY, NZ = 4, 4, 8
SENSORS, BALANCE = 384, 128
DEPTH = 3 * (SENSORS + BALANCE) + 128
FIRST = [0, 8, 15, 21, 26, 30, 33, 35, 36]
NN = (((1,), (0,)), ((), ()))
NT = (((1,), (1,)), ((), ()))
TN = (((0,), (0,)), ((), ()))


def dot(a, b, dims=NN):
    return lax.dot_general(a, b, dims, preferred_element_type=F32)


def split2(x):
    hi = x.astype(BF16)
    return hi, (x - hi.astype(F32)).astype(BF16)


def split3(x):
    hi = x.astype(BF16)
    rest = x - hi.astype(F32)
    mid = rest.astype(BF16)
    return hi, mid, (rest - mid.astype(F32)).astype(BF16)


def dot3(a, b, dims=NN):
    return dot(a[0], b[0], dims) + (dot(a[0], b[1], dims) + dot(a[1], b[0], dims))


def spread(row):
    return jnp.transpose(jnp.broadcast_to(row, (128, 128)))


def build_rows(w_ref, st_ref, co_ref, rd_ref, en_ref, cd_ref, br_ref, pr_ref, pi_ref, wcat, hcat, sr, prt, p0, p1):
    w = split2(w_ref[...])
    wcat[...] = jnp.concatenate([w[0], w[1], w[0]], axis=1)
    cond_row = cd_ref[...]
    cond = spread(cond_row)
    ends = [spread(en_ref[k : k + 1, :].astype(F32)).astype(jnp.int32) for k in range(2)]
    info = spread(jnp.concatenate([pi_ref[...], jnp.zeros((1, 120), F32)], axis=1))[0:8, :]
    readings = jnp.concatenate([rd_ref[k : k + 1, :] for k in range(3)], axis=1)
    meas = dot3(split2(jnp.broadcast_to(readings, (8, SENSORS))), w, NT)
    right = split2(jnp.concatenate([meas, jnp.broadcast_to(cond_row * br_ref[...], (8, BALANCE))], axis=1))
    rcat = jnp.concatenate([right[0], right[1], right[0]], axis=1)
    for j in range(8):
        cols = slice(128 * j, 128 * j + 128)
        ids = 128 * j + lax.broadcasted_iota(jnp.int32, (128, SENSORS), 0)
        h = jnp.zeros((128, SENSORS), F32)
        for k in range(4):
            h = h + jnp.where(ids == st_ref[k : k + 1, :], co_ref[k : k + 1, :], 0.0)
        hh, hl = split2(h)
        hj = jnp.concatenate([hh, hh, hl], axis=1)
        hcat[cols, :] = hj
        s = dot(wcat[...], hj, NT)
        bids = 128 * j + lax.broadcasted_iota(jnp.int32, (BALANCE, 128), 1)
        bal = jnp.where(bids == ends[0], cond, 0.0) - jnp.where(bids == ends[1], cond, 0.0)
        fh, fl = split2(jnp.concatenate([s, bal], axis=0))
        sr[0:512, cols] = fh
        sr[512:1024, cols] = fh
        sr[1024:1536, cols] = fl
        prior = pr_ref[:, cols]
        ph, pm, pl_ = [part.astype(F32) for part in split3(prior)]
        none = jnp.zeros((80, 128), F32)
        sr[1536:1664, cols] = jnp.concatenate([ph, pm, ph, pl_, ph, pm, none], axis=0).astype(BF16)
        prt[cols, :] = jnp.transpose(jnp.concatenate([ph, ph, pm, ph, pl_, pm, none], axis=0)).astype(BF16)
        mom = dot(rcat, sr[0:1536, cols])[0:1, :] + jnp.sum(prior * info, axis=0, keepdims=True)
        for a in range(4):
            p0[a, 36, j : j + 1, :] = mom


def build_gram(core, half, en_ref, cd_ref, wcat, hcat, sr, prt, out):
    at = [pl.ds(pl.multiple_of(128 * i + 64 * core + 32 * half, 32), 32) for i in range(8)]
    st = dot(jnp.concatenate([hcat[r, :] for r in at], axis=0), wcat[...], NT)
    ids = lax.broadcasted_iota(jnp.int32, (32, BALANCE), 0) + (64 * core + 32 * half)
    cond = cd_ref[...]
    bal = [
        jnp.where(ids + 128 * i == en_ref[0:1, :], cond, 0.0) - jnp.where(ids + 128 * i == en_ref[1:2, :], cond, 0.0)
        for i in range(8)
    ]
    th, tl = split2(jnp.concatenate([st, jnp.concatenate(bal, axis=0)], axis=1))
    lhs = jnp.concatenate([th, tl, th, jnp.concatenate([prt[r, :] for r in at], axis=0)], axis=1)
    for j0 in range(0, 8, 2):
        wide = dot(lhs[0 : 32 * (j0 + 2), :], sr[:, 128 * j0 : 128 * j0 + 256])
        for j in (j0, j0 + 1):
            for i in range(j + 1):
                blk = wide[32 * i : 32 * i + 32, 128 * (j - j0) : 128 * (j - j0) + 128]
                out[:, FIRST[i] + j - i] = blk.reshape(4, 8, 128)


def lane_bc(x, lane):
    return jnp.broadcast_to(x[:, lane : lane + 1], (8, 128))


def row_bc(x, row):
    return jnp.broadcast_to(x[row : row + 1, :], (8, 128))


def factor_block(ds, rd, lt):
    lane = lax.broadcasted_iota(jnp.int32, (8, 128), 1)
    sub = lax.broadcasted_iota(jnp.int32, (8, 128), 0)
    t = [ds[8 * j : 8 * j + 8, :] for j in range(16)]
    c = [lane_bc(t[0], q) for q in range(8)]
    for g in range(16):
        r0 = 8 * g
        own = (lane >= r0) & (lane < r0 + 8)
        below = range(g + 1, 16)
        b = {j: [lane_bc(t[j], r0 + q) for q in range(8)] for j in below}
        if g < 15:
            nc = [lane_bc(t[g + 1], r0 + 8 + q) for q in range(8)]
        p = jnp.where(own, jnp.where(lane - r0 == sub, 1.0, 0.0), t[g])
        for j in below:
            t[j] = jnp.where(own, 0.0, t[j])
        w = []
        low = jnp.zeros((8, 128), F32)
        for s in range(8):
            inv = lax.rsqrt(row_bc(c[s], s))
            col = c[s] * inv
            mult = {q: row_bc(col, q) for q in range(s + 1, 8)}
            for q in range(s + 1, 8):
                c[q] = c[q] - col * mult[q]
            ws = row_bc(p, s) * inv
            if s < 7:
                p = p - col * ws
            low = jnp.where(lane == r0 + s, col, low)
            for j in below:
                m = b[j][s] * inv
                for q in range(s + 1, 8):
                    b[j][q] = b[j][q] - m * mult[q]
                t[j] = t[j] - m * ws
                if j == g + 1:
                    for q in range(8):
                        nc[q] = nc[q] - m * row_bc(m, q)
            w.append(ws)
        full = w[0]
        for s in range(1, 8):
            full = jnp.where(sub == s, w[s], full)
        rd[r0 : r0 + 8, :] = jnp.where(lane >= r0 + 8, full, 0.0)
        ds[r0 : r0 + 8, :] = jnp.where(lane < r0 + 8, full, 0.0)
        lt[r0 : r0 + 8, :] = low
        if g < 15:
            c = nc
    rd[...] = rd[...] + jnp.transpose(lt[...])


N_COPIES = 60


def kernel(
    w_in, st_in, co_in, rd_in, en_in, cd_in, br_in, pr_in, pi_in, t_in, r_ref, z_ref, x_ref,
    w_ref, st_ref, co_ref, rd_ref, en_ref, cd_ref, br_ref, pr_ref, pi_ref, t_s,
    wcat, hcat, sr, prt, p0, p1, r1a, r1b, q0, q1, r2a, r2b, zs, r3, b4, g,
    a_s, ds, rd, lt, di_s, rp_s, zv, in_sem, s_sem, r_sem,
):
    row = lax.axis_index("rows")
    core = lax.axis_index("cols")
    x, y, z = row // (NY * NZ), (row // NZ) % NY, row % NZ

    pairs = [
        (st_in, st_ref), (co_in, co_ref), (en_in, en_ref), (cd_in, cd_ref), (br_in, br_ref),
        (pr_in, pr_ref), (pi_in, pi_ref), (rd_in, rd_ref), (w_in, w_ref), (t_in, t_s),
    ]
    loads = [pltpu.make_async_copy(src, dst, in_sem.at[n]) for n, (src, dst) in enumerate(pairs)]
    for cp in loads:
        cp.start()

    def at_x(v, c=core):
        return ((v * NY + y) * NZ + z, c)

    def at_y(v, c=core):
        return ((x * NY + v) * NZ + z, c)

    def at_z(v):
        return ((x * NY + y) * NZ + v, core)

    other = 1 - core
    sibling = (row, other)
    hop = lambda v, d, n: lax.rem(v + d, n)
    xs = [hop(x, d, NX) for d in range(1, 4)]
    ys = [hop(y, d, NY) for d in range(1, 4)]
    zz = [hop(z, d, NZ) for d in range(1, 8)]
    barrier = pltpu.get_barrier_semaphore()
    friends = [at_x(v) for v in xs] + [at_y(v) for v in ys] + [at_z(v) for v in zz] + [sibling]
    friends += [at_x(v, other) for v in xs] + [at_y(v, other) for v in ys]
    for to in friends:
        pl.semaphore_signal(barrier, inc=1, device_id=to, device_id_type=MESH)

    copies = []

    def send(src, dst, to):
        n = len(copies)
        cp = pltpu.make_async_remote_copy(
            src_ref=src, dst_ref=dst, send_sem=s_sem.at[n], recv_sem=r_sem.at[n], device_id=to, device_id_type=MESH
        )
        cp.start()
        copies.append(cp)
        return cp

    for cp in loads[:-1]:
        cp.wait()
    build_rows(w_ref, st_ref, co_ref, rd_ref, en_ref, cd_ref, br_ref, pr_ref, pi_ref, wcat, hcat, sr, prt, p0, p1)
    build_gram(core, 0, en_ref, cd_ref, wcat, hcat, sr, prt, p0)
    pl.semaphore_wait(barrier, len(friends))
    wa = [send(p0.at[v], r1a.at[x], at_x(v)) for v in xs]
    build_gram(core, 1, en_ref, cd_ref, wcat, hcat, sr, prt, p1)
    wb = [send(p1.at[v], r1b.at[y], at_y(v)) for v in ys]
    r1a[x] = p0[x]
    r1b[y] = p1[y]
    for i in range(1, 8):
        a_s[i, :, :, 0:1024] = jnp.zeros((16, 8, 1024), F32)
    for cp in wa:
        cp.wait_recv()
    for b in range(4):
        t = slice(9 * b, 9 * b + 9)
        q0[b, 0:9] = (r1a[0, t] + r1a[1, t]) + (r1a[2, t] + r1a[3, t])
    m = (r1a[0, 36] + r1a[1, 36]) + (r1a[2, 36] + r1a[3, 36])
    for b in range(4):
        q0[b, 9] = m
    wa = [send(q0.at[v], r2a.at[y], at_y(v)) for v in ys]
    for cp in wb:
        cp.wait_recv()
    for b in range(4):
        t = slice(9 * b, 9 * b + 9)
        q1[b] = (r1b[0, t] + r1b[1, t]) + (r1b[2, t] + r1b[3, t])
    wb = [send(q1.at[v], r2b.at[x], at_x(v)) for v in xs]
    r2a[y] = q0[y]
    r2b[x] = q1[x]
    for cp in wa:
        cp.wait_recv()
    a0 = (r2a[0] + r2a[1]) + (r2a[2] + r2a[3])
    for cp in wb:
        cp.wait_recv()
    a1 = (r2b[0] + r2b[1]) + (r2b[2] + r2b[3])
    for n in range(3):
        zs[n, 0:3] = a0[3 * n : 3 * n + 3]
        zs[3 + n, 0:3] = a1[3 * n : 3 * n + 3]
    for n in range(2):
        zs[6 + n, 0:3] = jnp.zeros((3, 8, 128), F32)
    for n in range(8):
        zs[n, 3] = a0[9]
    wz = [send(zs.at[v], r3.at[z], at_z(v)) for v in zz]
    r3[z] = zs[z]
    for cp in wz:
        cp.wait_recv()
    total = ((r3[0] + r3[1]) + (r3[2] + r3[3])) + ((r3[4] + r3[5]) + (r3[6] + r3[7]))
    b4[z] = total[0:3]
    wz = [send(b4.at[z], b4.at[z], at_z(v)) for v in zz]
    moment = total[3]
    for i in range(8):
        a_s[i, :, :, 1024:] = spread(moment[i : i + 1, :]).reshape(16, 8, 128)
    for cp in wz:
        cp.wait_recv()
    for n in range(3):
        g[core, 0, x, pl.ds(9 * y + 3 * n, 3)] = b4[n]
        g[core, 1, y, pl.ds(9 * x + 3 * n, 3)] = b4[3 + n]
    mine = g.at[core, 0, x, pl.ds(9 * y, 9)]
    wa = [send(mine, mine, at_y(v)) for v in ys]
    mine = g.at[core, 1, y, pl.ds(9 * x, 9)]
    wb = [send(mine, mine, at_x(v)) for v in xs]
    HEAD, REST = pl.ds(0, 8), pl.ds(8, 28)
    for cp in wa:
        cp.wait_recv()
    mine = g.at[core, 0, x, HEAD]
    first = [send(mine, mine, to) for to in [at_x(v) for v in xs] + [at_x(v, other) for v in xs] + [sibling]]
    for cp in wb:
        cp.wait_recv()
    mine = g.at[core, 1, y, HEAD]
    first += [send(mine, mine, to) for to in [at_y(v) for v in ys] + [at_y(v, other) for v in ys] + [sibling]]
    mine = g.at[core, 0, x, REST]
    wa = [send(mine, mine, at_x(v)) for v in xs]
    last = [send(mine, mine, sibling)]
    mine = g.at[core, 1, y, REST]
    wb = [send(mine, mine, at_y(v)) for v in ys]
    last.append(send(mine, mine, sibling))
    for cp in first:
        cp.wait_recv()
    for j in range(8):
        for c in range(2):
            for h in range(2):
                a_s[0, 8 * c + 4 * h : 8 * c + 4 * h + 4, :, 128 * j : 128 * j + 128] = g[c, h, :, j]

    def relay(d, half):
        src = hop(x, NX - 1 - d, NX) if half == 0 else hop(y, NY - 1 - d, NY)
        got = g.at[core, half, src, pl.ds(8, 28)]
        n = N_COPIES - 6 + 2 * d + half
        return pltpu.make_async_remote_copy(
            src_ref=got, dst_ref=got, send_sem=s_sem.at[n], recv_sem=r_sem.at[n], device_id=sibling, device_id_type=MESH
        )

    def pass_on():
        for d in range(3):
            wa[d].wait_recv()
            relay(d, 0).start()
            wb[d].wait_recv()
            relay(d, 1).start()

    def take_rest():
        for cp in last:
            cp.wait_recv()
        for d in range(3):
            relay(d, 0).wait_recv()
            relay(d, 1).wait_recv()
        for i in range(1, 8):
            for j in range(i, 8):
                cols = slice(128 * j, 128 * j + 128)
                for c in range(2):
                    for h in range(2):
                        at = slice(8 * c + 4 * h, 8 * c + 4 * h + 4)
                        a_s[i, at, :, cols] = a_s[i, at, :, cols] + g[c, h, :, FIRST[i] + j - i]

    def block(i, j):
        at = slice(128 * j, 128 * j + 128) if isinstance(j, int) else pl.ds(pl.multiple_of(j * 128, 128), 128)
        return a_s[i, :, :, at].reshape(128, 128)

    def panel(k, _):
        @pl.when(k == 1)
        def _():
            take_rest()

        here = pl.ds(pl.multiple_of(k * 128, 128), 128)
        ds[...] = block(k, k)
        factor_block(ds, rd, lt)

        @pl.when(k == 0)
        def _():
            pass_on()

        di = ds[...]
        di_s[k] = di
        dh, dl = split2(di)
        dcat = jnp.concatenate([dh, dl, dh], axis=1)

        def columns(first):
            cols = slice(128 * first, 1152)
            ah, al = split2(a_s[k, :, :, cols].reshape(128, -1))
            r = dot(dcat, jnp.concatenate([ah, ah, al], axis=0))
            a_s[k, :, :, cols] = r.reshape(16, 8, -1)
            rh, rl = split2(r)
            rp_s[0:128, cols] = rh
            rp_s[128:256, cols] = rh
            rp_s[256:384, cols] = rl

        @pl.when(k < 4)
        def _():
            columns(1)

        @pl.when(k >= 4)
        def _():
            columns(5)

        a_s[k, :, :, here] = rd[...].reshape(16, 8, 128)

        for i in range(1, 8):

            @pl.when(i > k)
            def _():
                cols = slice(128 * i, 1152)
                th, tl = split2(jnp.transpose(block(k, i)))
                lhs = jnp.concatenate([th, tl, th], axis=1)
                a_s[i, :, :, cols] = a_s[i, :, :, cols] - dot(lhs, rp_s[:, cols]).reshape(16, 8, -1)

        return 0

    lax.fori_loop(0, 8, panel, 0)

    v = [jnp.transpose(block(i, 8))[0:8, :] for i in range(8)]
    for i in range(8):
        zv[i : i + 1, :] = v[i][0:1, :]
    z_ref[...] = zv[pl.ds(core * 4, 4), :]
    e = [None] * 8
    for k in range(7, -1, -1):
        e[k] = dot3(split2(v[k]), split2(di_s[k]))
        if k:
            above = a_s[0:k, :, :, 128 * k : 128 * k + 128].reshape(128 * k, 128)
            upd = dot3(split2(e[k]), split2(above), NT)
            for p in range(k):
                v[p] = v[p] - upd[:, 128 * p : 128 * p + 128]
    loads[-1].wait()
    nxt = dot3(split2(jnp.concatenate(e, axis=1)), split2(t_s[...]), NT)
    x_ref[...] = nxt[0:1, :]
    mine = a_s[row // 16, row % 16, :, pl.ds(pl.multiple_of(core * 512, 512), 512)]
    at_row = row * 8 + lax.broadcasted_iota(jnp.int32, (8, 512), 0)
    at_col = core * 512 + lax.broadcasted_iota(jnp.int32, (8, 512), 1)
    r_ref[...] = jnp.where(at_col >= at_row, mine, 0.0)
    for cp in copies:
        cp.wait_send()
    for d in range(3):
        relay(d, 0).wait_send()
        relay(d, 1).wait_send()


def per_device(
    whitening,
    sensor_states,
    sensor_coefficients,
    sensor_readings,
    conduit_endpoints,
    conductance,
    balance_right_side,
    prior_root_factor,
    prior_information,
    transition,
):
    args = (
        whitening,
        sensor_states.T,
        sensor_coefficients.T,
        sensor_readings.reshape(3, 128),
        conduit_endpoints.T,
        conductance.reshape(1, BALANCE),
        balance_right_side.reshape(1, BALANCE),
        prior_root_factor,
        prior_information.reshape(1, 8),
        transition,
    )
    vmem = pl.BlockSpec(memory_space=pltpu.VMEM)
    tiles = lambda *lead: pltpu.VMEM(lead + (8, 128), F32)
    r_post, z_post, x_next = pl.pallas_call(
        kernel,
        out_shape=(
            jax.ShapeDtypeStruct((8, 512), F32),
            jax.ShapeDtypeStruct((4, 128), F32),
            jax.ShapeDtypeStruct((1, 512), F32),
        ),
        in_specs=[pl.BlockSpec(memory_space=pl.ANY)] * len(args),
        out_specs=(vmem, vmem, vmem),
        scratch_shapes=[pltpu.VMEM(arg.shape, arg.dtype) for arg in args]
        + [
            pltpu.VMEM((SENSORS, 3 * SENSORS), BF16),
            pltpu.VMEM((1024, 3 * SENSORS), BF16),
            pltpu.VMEM((DEPTH, 1024), BF16),
            pltpu.VMEM((1024, 128), BF16),
            tiles(4, 37),
            tiles(4, 36),
            tiles(4, 37),
            tiles(4, 36),
            tiles(4, 10),
            tiles(4, 9),
            tiles(4, 10),
            tiles(4, 9),
            tiles(8, 4),
            tiles(8, 4),
            tiles(8, 3),
            tiles(2, 2, 4, 36),
            pltpu.VMEM((8, 16, 8, 1152), F32),
            pltpu.VMEM((128, 128), F32),
            pltpu.VMEM((128, 128), F32),
            pltpu.VMEM((128, 128), F32),
            pltpu.VMEM((8, 128, 128), F32),
            pltpu.VMEM((384, 1152), BF16),
            pltpu.VMEM((8, 128), F32),
            pltpu.SemaphoreType.DMA((10,)),
            pltpu.SemaphoreType.DMA((N_COPIES,)),
            pltpu.SemaphoreType.DMA((N_COPIES,)),
        ],
        compiler_params=pltpu.CompilerParams(
            collective_id=0, has_side_effects=True, vmem_limit_bytes=62 * 1024 * 1024
        ),
    )(*args)
    return r_post, z_post.reshape(512), x_next.reshape(512)


def solution(mesh):
    in_specs = (
        P("rows", None),
        P("rows", None),
        P("rows", None),
        P("rows"),
        P("rows", None),
        P("rows"),
        P("rows"),
        P("rows", None),
        P("rows"),
        P("cols", None),
    )
    out_specs = (P("rows", "cols"), P("cols"), P("cols"))
    return jax.shard_map(
        per_device, mesh=mesh, in_specs=in_specs, out_specs=out_specs, check_vma=False
    )
```

```python
import jax
import jax.numpy as jnp
from jax import lax
from jax.experimental import pallas as pl
from jax.experimental.pallas import tpu as pltpu
from jax.sharding import PartitionSpec as P

F32, BF16 = jnp.float32, jnp.bfloat16
MESH = pl.DeviceIdType.MESH
NX, NY, NZ = 4, 4, 8
SENSORS, BALANCE = 384, 128
DEPTH = 3 * (SENSORS + BALANCE) + 128
FIRST = [0, 8, 15, 21, 26, 30, 33, 35, 36]
NN = (((1,), (0,)), ((), ()))
NT = (((1,), (1,)), ((), ()))
TN = (((0,), (0,)), ((), ()))


def dot(a, b, dims=NN):
    return lax.dot_general(a, b, dims, preferred_element_type=F32)


def split2(x):
    hi = x.astype(BF16)
    return hi, (x - hi.astype(F32)).astype(BF16)


def split3(x):
    hi = x.astype(BF16)
    rest = x - hi.astype(F32)
    mid = rest.astype(BF16)
    return hi, mid, (rest - mid.astype(F32)).astype(BF16)


def dot3(a, b, dims=NN):
    return dot(a[0], b[0], dims) + (dot(a[0], b[1], dims) + dot(a[1], b[0], dims))


def spread(row):
    return jnp.transpose(jnp.broadcast_to(row, (128, 128)))


def build_rows(w_ref, st_ref, co_ref, rd_ref, en_ref, cd_ref, br_ref, pr_ref, pi_ref, wcat, hcat, sr, prt, p0, p1):
    w = split2(w_ref[...])
    wcat[...] = jnp.concatenate([w[0], w[1], w[0]], axis=1)
    cond_row = cd_ref[...]
    cond = spread(cond_row)
    ends = [spread(en_ref[k : k + 1, :].astype(F32)).astype(jnp.int32) for k in range(2)]
    info = spread(jnp.concatenate([pi_ref[...], jnp.zeros((1, 120), F32)], axis=1))[0:8, :]
    readings = jnp.concatenate([rd_ref[k : k + 1, :] for k in range(3)], axis=1)
    meas = dot3(split2(jnp.broadcast_to(readings, (8, SENSORS))), w, NT)
    right = split2(jnp.concatenate([meas, jnp.broadcast_to(cond_row * br_ref[...], (8, BALANCE))], axis=1))
    rcat = jnp.concatenate([right[0], right[1], right[0]], axis=1)
    for j in range(8):
        cols = slice(128 * j, 128 * j + 128)
        ids = 128 * j + lax.broadcasted_iota(jnp.int32, (128, SENSORS), 0)
        h = jnp.zeros((128, SENSORS), F32)
        for k in range(4):
            h = h + jnp.where(ids == st_ref[k : k + 1, :], co_ref[k : k + 1, :], 0.0)
        hh, hl = split2(h)
        hj = jnp.concatenate([hh, hh, hl], axis=1)
        hcat[cols, :] = hj
        s = dot(wcat[...], hj, NT)
        bids = 128 * j + lax.broadcasted_iota(jnp.int32, (BALANCE, 128), 1)
        bal = jnp.where(bids == ends[0], cond, 0.0) - jnp.where(bids == ends[1], cond, 0.0)
        fh, fl = split2(jnp.concatenate([s, bal], axis=0))
        sr[0:512, cols] = fh
        sr[512:1024, cols] = fh
        sr[1024:1536, cols] = fl
        prior = pr_ref[:, cols]
        ph, pm, pl_ = [part.astype(F32) for part in split3(prior)]
        none = jnp.zeros((80, 128), F32)
        sr[1536:1664, cols] = jnp.concatenate([ph, pm, ph, pl_, ph, pm, none], axis=0).astype(BF16)
        prt[cols, :] = jnp.transpose(jnp.concatenate([ph, ph, pm, ph, pl_, pm, none], axis=0)).astype(BF16)
        mom = dot(rcat, sr[0:1536, cols])[0:1, :] + jnp.sum(prior * info, axis=0, keepdims=True)
        for a in range(4):
            p0[a, 36, j : j + 1, :] = mom


def build_gram(core, half, en_ref, cd_ref, wcat, hcat, sr, prt, out):
    at = [pl.ds(pl.multiple_of(128 * i + 64 * core + 32 * half, 32), 32) for i in range(8)]
    st = dot(jnp.concatenate([hcat[r, :] for r in at], axis=0), wcat[...], NT)
    ids = lax.broadcasted_iota(jnp.int32, (32, BALANCE), 0) + (64 * core + 32 * half)
    cond = cd_ref[...]
    bal = [
        jnp.where(ids + 128 * i == en_ref[0:1, :], cond, 0.0) - jnp.where(ids + 128 * i == en_ref[1:2, :], cond, 0.0)
        for i in range(8)
    ]
    th, tl = split2(jnp.concatenate([st, jnp.concatenate(bal, axis=0)], axis=1))
    lhs = jnp.concatenate([th, tl, th, jnp.concatenate([prt[r, :] for r in at], axis=0)], axis=1)
    for j0 in range(0, 8, 2):
        wide = dot(lhs[0 : 32 * (j0 + 2), :], sr[:, 128 * j0 : 128 * j0 + 256])
        for j in (j0, j0 + 1):
            for i in range(j + 1):
                blk = wide[32 * i : 32 * i + 32, 128 * (j - j0) : 128 * (j - j0) + 128]
                out[:, FIRST[i] + j - i] = blk.reshape(4, 8, 128)


def lane_bc(x, lane):
    return jnp.broadcast_to(x[:, lane : lane + 1], (8, 128))


def row_bc(x, row):
    return jnp.broadcast_to(x[row : row + 1, :], (8, 128))


NEAR = 8


def factor_block(ds, rd, lt, beside):
    lane = lax.broadcasted_iota(jnp.int32, (8, 128), 1)
    sub = lax.broadcasted_iota(jnp.int32, (8, 128), 0)
    t = [ds[8 * j : 8 * j + 8, :] for j in range(16)]
    c = [lane_bc(t[0], q) for q in range(8)]
    for g in range(16):
        r0 = 8 * g
        own = (lane >= r0) & (lane < r0 + 8)
        near = range(g + 1, min(16, g + 1 + NEAR))
        far = range(g + 1 + NEAR, 16)
        b = {j: [lane_bc(t[j], r0 + q) for q in range(8)] for j in near}
        if g < 15:
            nc = [lane_bc(t[g + 1], r0 + 8 + q) for q in range(8)]
        p = jnp.where(own, jnp.where(lane - r0 == sub, 1.0, 0.0), t[g])
        raw = split2(jnp.concatenate([t[j] for j in far], axis=0)) if far else None
        for j in range(g + 1, 16):
            t[j] = jnp.where(own, 0.0, t[j])
        w, mults, invs = [], [], []
        low = jnp.zeros((8, 128), F32)
        for s in range(8):
            inv = lax.rsqrt(row_bc(c[s], s))
            col = c[s] * inv
            mult = {q: row_bc(col, q) for q in range(s + 1, 8)}
            for q in range(s + 1, 8):
                c[q] = c[q] - col * mult[q]
            ws = row_bc(p, s) * inv
            if s < 7:
                p = p - col * ws
            low = jnp.where(lane == r0 + s, col, low)
            for j in near:
                m = b[j][s] * inv
                for q in range(s + 1, 8):
                    b[j][q] = b[j][q] - m * mult[q]
                t[j] = t[j] - m * ws
                if j == g + 1:
                    for q in range(8):
                        nc[q] = nc[q] - m * row_bc(m, q)
            w.append(ws)
            mults.append(mult)
            invs.append(inv)
        full = w[0]
        for s in range(1, 8):
            full = jnp.where(sub == s, w[s], full)
        if far:
            y = [None] * 8
            for s in range(7, -1, -1):
                v = w[s]
                for q in range(7, s, -1):
                    v = v - mults[s][q] * y[q]
                y[s] = v * invs[s]
            yy = y[0]
            for s in range(1, 8):
                yy = jnp.where(sub == s, y[s], yy)
            pad = lambda v: jnp.concatenate(
                ([jnp.zeros((r0, 128), F32)] if r0 else []) + [v, jnp.zeros((120 - r0, 128), F32)], axis=0
            ).astype(BF16)
            yh = yy.astype(BF16).astype(F32)
            yhp, ylp = pad(yh), pad(yy - yh)
            upd = dot(jnp.concatenate(raw, axis=1), jnp.concatenate([yhp, yhp], axis=0)) + dot(raw[0], ylp)
            for n, j in enumerate(far):
                t[j] = t[j] - upd[8 * n : 8 * n + 8, :]
        rd[r0 : r0 + 8, :] = jnp.where(lane >= r0 + 8, full, 0.0)
        ds[r0 : r0 + 8, :] = jnp.where(lane < r0 + 8, full, 0.0)
        lt[r0 : r0 + 8, :] = low
        if g < 15:
            c = nc
        for step in beside[g]:
            step()
    rd[...] = rd[...] + jnp.transpose(lt[...])


N_COPIES = 60


def kernel(
    w_in, st_in, co_in, rd_in, en_in, cd_in, br_in, pr_in, pi_in, t_in, o_ref,
    w_ref, st_ref, co_ref, rd_ref, en_ref, cd_ref, br_ref, pr_ref, pi_ref, t_s,
    wcat, hcat, sr, prt, p0, p1, r1a, r1b, q0, q1, r2a, r2b, zs, r3, b4, g,
    a_s, ds, rd, lt, dh_s, dl_s, rp_s, rt_s, rh_s, rl_s, th_s, tl_s, zv, in_sem, s_sem, r_sem,
):
    row = lax.axis_index("rows")
    core = lax.axis_index("cols")
    x, y, z = row // (NY * NZ), (row // NZ) % NY, row % NZ

    pairs = [
        (st_in, st_ref), (co_in, co_ref), (en_in, en_ref), (cd_in, cd_ref), (br_in, br_ref),
        (pr_in, pr_ref), (pi_in, pi_ref), (rd_in, rd_ref), (w_in, w_ref), (t_in, t_s),
    ]
    loads = [pltpu.make_async_copy(src, dst, in_sem.at[n]) for n, (src, dst) in enumerate(pairs)]
    for cp in loads:
        cp.start()

    def at_x(v, c=core):
        return ((v * NY + y) * NZ + z, c)

    def at_y(v, c=core):
        return ((x * NY + v) * NZ + z, c)

    def at_z(v):
        return ((x * NY + y) * NZ + v, core)

    other = 1 - core
    sibling = (row, other)
    hop = lambda v, d, n: lax.rem(v + d, n)
    xs = [hop(x, d, NX) for d in range(1, 4)]
    ys = [hop(y, d, NY) for d in range(1, 4)]
    zz = [hop(z, d, NZ) for d in range(1, 8)]
    barrier = pltpu.get_barrier_semaphore()
    friends = [at_x(v) for v in xs] + [at_y(v) for v in ys] + [at_z(v) for v in zz] + [sibling]
    friends += [at_x(v, other) for v in xs] + [at_y(v, other) for v in ys]
    for to in friends:
        pl.semaphore_signal(barrier, inc=1, device_id=to, device_id_type=MESH)

    copies = []

    def send(src, dst, to):
        n = len(copies)
        cp = pltpu.make_async_remote_copy(
            src_ref=src, dst_ref=dst, send_sem=s_sem.at[n], recv_sem=r_sem.at[n], device_id=to, device_id_type=MESH
        )
        cp.start()
        copies.append(cp)
        return cp

    for cp in loads[:-1]:
        cp.wait()
    build_rows(w_ref, st_ref, co_ref, rd_ref, en_ref, cd_ref, br_ref, pr_ref, pi_ref, wcat, hcat, sr, prt, p0, p1)
    build_gram(core, 0, en_ref, cd_ref, wcat, hcat, sr, prt, p0)
    pl.semaphore_wait(barrier, len(friends))
    wa = [send(p0.at[v], r1a.at[x], at_x(v)) for v in xs]
    build_gram(core, 1, en_ref, cd_ref, wcat, hcat, sr, prt, p1)
    wb = [send(p1.at[v], r1b.at[y], at_y(v)) for v in ys]
    r1a[x] = p0[x]
    r1b[y] = p1[y]
    for i in range(1, 8):
        a_s[i, :, :, 0:1024] = jnp.zeros((16, 8, 1024), F32)
    a_s[8] = jnp.zeros((16, 8, 1152), F32)
    dh_s[8] = jnp.zeros((128, 128), BF16)
    dl_s[8] = jnp.zeros((128, 128), BF16)
    loads[-1].wait()
    th_s[...], tl_s[...] = split2(t_s[...])
    for cp in wa:
        cp.wait_recv()
    for b in range(4):
        t = slice(9 * b, 9 * b + 9)
        q0[b, 0:9] = (r1a[0, t] + r1a[1, t]) + (r1a[2, t] + r1a[3, t])
    m = (r1a[0, 36] + r1a[1, 36]) + (r1a[2, 36] + r1a[3, 36])
    for b in range(4):
        q0[b, 9] = m
    wa = [send(q0.at[v], r2a.at[y], at_y(v)) for v in ys]
    for cp in wb:
        cp.wait_recv()
    for b in range(4):
        t = slice(9 * b, 9 * b + 9)
        q1[b] = (r1b[0, t] + r1b[1, t]) + (r1b[2, t] + r1b[3, t])
    wb = [send(q1.at[v], r2b.at[x], at_x(v)) for v in xs]
    r2a[y] = q0[y]
    r2b[x] = q1[x]
    for cp in wa:
        cp.wait_recv()
    a0 = (r2a[0] + r2a[1]) + (r2a[2] + r2a[3])
    for cp in wb:
        cp.wait_recv()
    a1 = (r2b[0] + r2b[1]) + (r2b[2] + r2b[3])
    for n in range(3):
        zs[n, 0:3] = a0[3 * n : 3 * n + 3]
        zs[3 + n, 0:3] = a1[3 * n : 3 * n + 3]
    for n in range(2):
        zs[6 + n, 0:3] = jnp.zeros((3, 8, 128), F32)
    for n in range(8):
        zs[n, 3] = a0[9]
    wz = [send(zs.at[v], r3.at[z], at_z(v)) for v in zz]
    r3[z] = zs[z]
    for cp in wz:
        cp.wait_recv()
    total = ((r3[0] + r3[1]) + (r3[2] + r3[3])) + ((r3[4] + r3[5]) + (r3[6] + r3[7]))
    b4[z] = total[0:3]
    wz = [send(b4.at[z], b4.at[z], at_z(v)) for v in zz]
    moment = total[3]
    for i in range(8):
        a_s[i, :, :, 1024:] = spread(moment[i : i + 1, :]).reshape(16, 8, 128)
    for cp in wz:
        cp.wait_recv()
    for n in range(3):
        g[core, 0, x, pl.ds(9 * y + 3 * n, 3)] = b4[n]
        g[core, 1, y, pl.ds(9 * x + 3 * n, 3)] = b4[3 + n]
    mine = g.at[core, 0, x, pl.ds(9 * y, 9)]
    wa = [send(mine, mine, at_y(v)) for v in ys]
    mine = g.at[core, 1, y, pl.ds(9 * x, 9)]
    wb = [send(mine, mine, at_x(v)) for v in xs]
    HEAD, REST = pl.ds(0, 8), pl.ds(8, 28)
    for cp in wa:
        cp.wait_recv()
    mine = g.at[core, 0, x, HEAD]
    first = [send(mine, mine, to) for to in [at_x(v) for v in xs] + [at_x(v, other) for v in xs] + [sibling]]
    for cp in wb:
        cp.wait_recv()
    mine = g.at[core, 1, y, HEAD]
    first += [send(mine, mine, to) for to in [at_y(v) for v in ys] + [at_y(v, other) for v in ys] + [sibling]]
    mine = g.at[core, 0, x, REST]
    wa = [send(mine, mine, at_x(v)) for v in xs]
    last = [send(mine, mine, sibling)]
    mine = g.at[core, 1, y, REST]
    wb = [send(mine, mine, at_y(v)) for v in ys]
    last.append(send(mine, mine, sibling))
    for cp in first:
        cp.wait_recv()
    for j in range(8):
        for c in range(2):
            for h in range(2):
                a_s[0, 8 * c + 4 * h : 8 * c + 4 * h + 4, :, 128 * j : 128 * j + 128] = g[c, h, :, j]

    def relay(d, half):
        src = hop(x, NX - 1 - d, NX) if half == 0 else hop(y, NY - 1 - d, NY)
        got = g.at[core, half, src, pl.ds(8, 28)]
        n = N_COPIES - 6 + 2 * d + half
        return pltpu.make_async_remote_copy(
            src_ref=got, dst_ref=got, send_sem=s_sem.at[n], recv_sem=r_sem.at[n], device_id=sibling, device_id_type=MESH
        )

    def pass_on():
        for d in range(3):
            wa[d].wait_recv()
            relay(d, 0).start()
            wb[d].wait_recv()
            relay(d, 1).start()

    def take_rest():
        for cp in last:
            cp.wait_recv()
        for d in range(3):
            relay(d, 0).wait_recv()
            relay(d, 1).wait_recv()
        for i in range(1, 8):
            for j in range(i, 8):
                cols = slice(128 * j, 128 * j + 128)
                for c in range(2):
                    for h in range(2):
                        at = slice(8 * c + 4 * h, 8 * c + 4 * h + 4)
                        a_s[i, at, :, cols] = a_s[i, at, :, cols] + g[c, h, :, FIRST[i] + j - i]

    def panel(k, _):
        @pl.when(k == 1)
        def _():
            take_rest()
            for c in range(2):
                for h in range(2):
                    at = slice(64 * c + 32 * h, 64 * c + 32 * h + 32)
                    ds[at, :] = ds[at, :] + g[c, h, :, FIRST[1]].reshape(32, 128)

        prev = jnp.where(k == 0, 8, k - 1)
        dcat = jnp.concatenate([dh_s[prev], dl_s[prev], dh_s[prev]], axis=1)

        def product(j):
            def step():
                cols = slice(128 * j, 128 * j + 256)
                ah, al = split2(a_s[prev, :, :, cols].reshape(128, 256))
                r = dot(dcat, jnp.concatenate([ah, ah, al], axis=0))
                a_s[prev, :, :, cols] = r.reshape(16, 8, 256)
                rh, rl = split2(r)
                rp_s[0:128, cols] = rh
                rp_s[128:256, cols] = rh
                rp_s[256:384, cols] = rl
                rh_s[prev, :, cols] = rh
                rl_s[prev, :, cols] = rl
                for i in range(j, min(j + 2, 8)):
                    th, tl = split2(jnp.transpose(r[:, 128 * (i - j) : 128 * (i - j) + 128]))
                    rt_s[i] = jnp.concatenate([th, tl, th], axis=1)

            return step

        def update(i, j):
            def step():
                end = min(j + 2, 9)
                cols = slice(128 * j, 128 * end)
                to = jnp.where(i >= k, i, 8)
                upd = dot(rt_s[i], rp_s[:, cols])
                a_s[to, :, :, cols] = a_s[to, :, :, cols] - upd.reshape(16, 8, 128 * (end - j))

            return step

        steps = [product(j) for j in range(1, 9, 2)]
        steps += [update(i, j) for i in range(1, 8) for j in range(i, 9, 2)]
        factor_block(ds, rd.at[k], lt, [steps[2 * n : 2 * n + 2] for n in range(16)])

        @pl.when(k == 0)
        def _():
            pass_on()

        d = split2(ds[...])
        dh_s[k], dl_s[k] = d
        nxt = pl.ds(pl.multiple_of(128 * k + 128, 128), 128)
        c = dot3(d, split2(a_s[k, :, :, nxt].reshape(128, 128)))
        ds[...] = a_s[k + 1, :, :, nxt].reshape(128, 128) - dot3(split2(jnp.transpose(c)), split2(c))
        return 0

    ds[...] = a_s[0, :, :, 0:128].reshape(128, 128)
    lax.fori_loop(0, 8, panel, 0)

    z7 = dot3((dh_s[7], dl_s[7]), split2(a_s[7, :, :, 1024:].reshape(128, 128)))
    v = [jnp.transpose(a_s[i, :, :, 1024:].reshape(128, 128))[0:8, :] for i in range(7)] + [jnp.transpose(z7)[0:8, :]]
    for i in range(8):
        zv[i : i + 1, :] = v[i][0:1, :]
    e = [None] * 8
    for k in range(7, -1, -1):
        e[k] = dot3(split2(v[k]), (dh_s[k], dl_s[k]))
        ek = split2(e[k])
        for p in range(k - 1, -1, -1):
            at = slice(128 * k, 128 * k + 128)
            v[p] = v[p] - dot3(ek, (rh_s[p, :, at], rl_s[p, :, at]), NT)
    nxt = dot3(split2(jnp.concatenate(e, axis=1)), (th_s[...], tl_s[...]), NT)
    for q in range(4):
        o_ref[8:9, 128 * q : 128 * q + 128] = zv[pl.ds(core * 4 + q, 1), :]
    o_ref[9:10, :] = nxt[0:1, :]
    o_ref[10:16, :] = jnp.zeros((6, 512), F32)
    for k in range(8):
        a_s[k, :, :, 128 * k : 128 * k + 128] = rd[k].reshape(16, 8, 128)
    mine = a_s[row // 16, row % 16, :, pl.ds(pl.multiple_of(core * 512, 512), 512)]
    at_row = row * 8 + lax.broadcasted_iota(jnp.int32, (8, 512), 0)
    at_col = core * 512 + lax.broadcasted_iota(jnp.int32, (8, 512), 1)
    o_ref[0:8, :] = jnp.where(at_col >= at_row, mine, 0.0)
    for cp in copies:
        cp.wait_send()
    for d in range(3):
        relay(d, 0).wait_send()
        relay(d, 1).wait_send()


def hand_out(all_ref, r_ref, z_ref, x_ref):
    r_ref[...] = all_ref[0:8, :]
    z_ref[...] = all_ref[8:9, :]
    x_ref[...] = all_ref[9:10, :]


def per_device(
    whitening,
    sensor_states,
    sensor_coefficients,
    sensor_readings,
    conduit_endpoints,
    conductance,
    balance_right_side,
    prior_root_factor,
    prior_information,
    transition,
):
    args = (
        whitening,
        sensor_states.T,
        sensor_coefficients.T,
        sensor_readings.reshape(3, 128),
        conduit_endpoints.T,
        conductance.reshape(1, BALANCE),
        balance_right_side.reshape(1, BALANCE),
        prior_root_factor,
        prior_information.reshape(1, 8),
        transition,
    )
    vmem = pl.BlockSpec(memory_space=pltpu.VMEM)
    tiles = lambda *lead: pltpu.VMEM(lead + (8, 128), F32)
    results = pl.pallas_call(
        kernel,
        out_shape=jax.ShapeDtypeStruct((16, 512), F32),
        in_specs=[pl.BlockSpec(memory_space=pl.ANY)] * len(args),
        out_specs=vmem,
        scratch_shapes=[pltpu.VMEM(arg.shape, arg.dtype) for arg in args]
        + [
            pltpu.VMEM((SENSORS, 3 * SENSORS), BF16),
            pltpu.VMEM((1024, 3 * SENSORS), BF16),
            pltpu.VMEM((DEPTH, 1024), BF16),
            pltpu.VMEM((1024, 128), BF16),
            tiles(4, 37),
            tiles(4, 36),
            tiles(4, 37),
            tiles(4, 36),
            tiles(4, 10),
            tiles(4, 9),
            tiles(4, 10),
            tiles(4, 9),
            tiles(8, 4),
            tiles(8, 4),
            tiles(8, 3),
            tiles(2, 2, 4, 36),
            pltpu.VMEM((9, 16, 8, 1152), F32),
            pltpu.VMEM((128, 128), F32),
            pltpu.VMEM((8, 128, 128), F32),
            pltpu.VMEM((128, 128), F32),
            pltpu.VMEM((9, 128, 128), BF16),
            pltpu.VMEM((9, 128, 128), BF16),
            pltpu.VMEM((384, 1152), BF16),
            pltpu.VMEM((8, 128, 384), BF16),
            pltpu.VMEM((9, 128, 1152), BF16),
            pltpu.VMEM((9, 128, 1152), BF16),
            pltpu.VMEM((512, 1024), BF16),
            pltpu.VMEM((512, 1024), BF16),
            pltpu.VMEM((8, 128), F32),
            pltpu.SemaphoreType.DMA((10,)),
            pltpu.SemaphoreType.DMA((N_COPIES,)),
            pltpu.SemaphoreType.DMA((N_COPIES,)),
        ],
        compiler_params=pltpu.CompilerParams(
            collective_id=0, has_side_effects=True, vmem_limit_bytes=62 * 1024 * 1024
        ),
    )(*args)
    r_post, z_post, x_next = pl.pallas_call(
        hand_out,
        out_shape=(
            jax.ShapeDtypeStruct((8, 512), F32),
            jax.ShapeDtypeStruct((1, 512), F32),
            jax.ShapeDtypeStruct((1, 512), F32),
        ),
        in_specs=[vmem],
        out_specs=(vmem, vmem, vmem),
        compiler_params=pltpu.CompilerParams(vmem_limit_bytes=62 * 1024 * 1024),
    )(results)
    return r_post, z_post.reshape(512), x_next.reshape(512)


def solution(mesh):
    in_specs = (
        P("rows", None),
        P("rows", None),
        P("rows", None),
        P("rows"),
        P("rows", None),
        P("rows"),
        P("rows"),
        P("rows", None),
        P("rows"),
        P("cols", None),
    )
    out_specs = (P("rows", "cols"), P("cols"), P("cols"))
    return jax.shard_map(
        per_device, mesh=mesh, in_specs=in_specs, out_specs=out_specs, check_vma=False
    )
```

```python
import jax
import jax.numpy as jnp
from jax import lax
from jax.experimental import pallas as pl
from jax.experimental.pallas import tpu as pltpu
from jax.sharding import PartitionSpec as P

F32, BF16 = jnp.float32, jnp.bfloat16
MESH = pl.DeviceIdType.MESH
NX, NY, NZ = 4, 4, 8
SENSORS, BALANCE = 384, 128
DEPTH = 3 * (SENSORS + BALANCE) + 128
FIRST = [0, 8, 15, 21, 26, 30, 33, 35, 36]
HEAD, REST = 16, 20
NN = (((1,), (0,)), ((), ()))
NT = (((1,), (1,)), ((), ()))
TN = (((0,), (0,)), ((), ()))


def dot(a, b, dims=NN):
    return lax.dot_general(a, b, dims, preferred_element_type=F32)


def split2(x):
    hi = x.astype(BF16)
    return hi, (x - hi.astype(F32)).astype(BF16)


def split3(x):
    hi = x.astype(BF16)
    rest = x - hi.astype(F32)
    mid = rest.astype(BF16)
    return hi, mid, (rest - mid.astype(F32)).astype(BF16)


def dot3(a, b, dims=NN):
    return dot(a[0], b[0], dims) + (dot(a[0], b[1], dims) + dot(a[1], b[0], dims))


def spread(row):
    return jnp.transpose(jnp.broadcast_to(row, (128, 128)))


def build_rows(w_ref, st_ref, co_ref, rd_ref, en_ref, cd_ref, br_ref, pr_ref, pi_ref, wcat, hcat, sr, prt, p0, p1):
    w = split2(w_ref[...])
    wcat[...] = jnp.concatenate([w[0], w[1], w[0]], axis=1)
    cond_row = cd_ref[...]
    cond = spread(cond_row)
    ends = [spread(en_ref[k : k + 1, :].astype(F32)).astype(jnp.int32) for k in range(2)]
    info = spread(jnp.concatenate([pi_ref[...], jnp.zeros((1, 120), F32)], axis=1))[0:8, :]
    readings = jnp.concatenate([rd_ref[k : k + 1, :] for k in range(3)], axis=1)
    meas = dot3(split2(jnp.broadcast_to(readings, (8, SENSORS))), w, NT)
    right = split2(jnp.concatenate([meas, jnp.broadcast_to(cond_row * br_ref[...], (8, BALANCE))], axis=1))
    rcat = jnp.concatenate([right[0], right[1], right[0]], axis=1)
    for j in range(8):
        cols = slice(128 * j, 128 * j + 128)
        ids = 128 * j + lax.broadcasted_iota(jnp.int32, (128, SENSORS), 0)
        h = jnp.zeros((128, SENSORS), F32)
        for k in range(4):
            h = h + jnp.where(ids == st_ref[k : k + 1, :], co_ref[k : k + 1, :], 0.0)
        hh, hl = split2(h)
        hj = jnp.concatenate([hh, hh, hl], axis=1)
        hcat[cols, :] = hj
        s = dot(wcat[...], hj, NT)
        bids = 128 * j + lax.broadcasted_iota(jnp.int32, (BALANCE, 128), 1)
        bal = jnp.where(bids == ends[0], cond, 0.0) - jnp.where(bids == ends[1], cond, 0.0)
        fh, fl = split2(jnp.concatenate([s, bal], axis=0))
        sr[0:512, cols] = fh
        sr[512:1024, cols] = fh
        sr[1024:1536, cols] = fl
        prior = pr_ref[:, cols]
        ph, pm, pl_ = [part.astype(F32) for part in split3(prior)]
        none = jnp.zeros((80, 128), F32)
        sr[1536:1664, cols] = jnp.concatenate([ph, pm, ph, pl_, ph, pm, none], axis=0).astype(BF16)
        prt[cols, :] = jnp.transpose(jnp.concatenate([ph, ph, pm, ph, pl_, pm, none], axis=0)).astype(BF16)
        mom = dot(rcat, sr[0:1536, cols])[0:1, :] + jnp.sum(prior * info, axis=0, keepdims=True)
        for a in range(4):
            p0[a, HEAD, j : j + 1, :] = mom


def build_gram(core, half, en_ref, cd_ref, wcat, hcat, sr, prt, out):
    at = [pl.ds(pl.multiple_of(128 * i + 64 * core + 32 * half, 32), 32) for i in range(8)]
    st = dot(jnp.concatenate([hcat[r, :] for r in at], axis=0), wcat[...], NT)
    ids = lax.broadcasted_iota(jnp.int32, (32, BALANCE), 0) + (64 * core + 32 * half)
    cond = cd_ref[...]
    bal = [
        jnp.where(ids + 128 * i == en_ref[0:1, :], cond, 0.0) - jnp.where(ids + 128 * i == en_ref[1:2, :], cond, 0.0)
        for i in range(8)
    ]
    th, tl = split2(jnp.concatenate([st, jnp.concatenate(bal, axis=0)], axis=1))
    lhs = jnp.concatenate([th, tl, th, jnp.concatenate([prt[r, :] for r in at], axis=0)], axis=1)
    for j0 in range(0, 8, 2):
        wide = dot(lhs[0 : 32 * (j0 + 2), :], sr[:, 128 * j0 : 128 * j0 + 256])
        for j in (j0, j0 + 1):
            for i in range(j + 1):
                blk = wide[32 * i : 32 * i + 32, 128 * (j - j0) : 128 * (j - j0) + 128]
                at = FIRST[i] + j - i
                out[:, at + (1 if half == 0 and at >= HEAD else 0)] = blk.reshape(4, 8, 128)


def lane_bc(x, lane):
    return jnp.broadcast_to(x[:, lane : lane + 1], (8, 128))


def row_bc(x, row):
    return jnp.broadcast_to(x[row : row + 1, :], (8, 128))


NEAR = 8


def factor_block(ds, rd, lt, beside):
    lane = lax.broadcasted_iota(jnp.int32, (8, 128), 1)
    sub = lax.broadcasted_iota(jnp.int32, (8, 128), 0)
    t = [ds[8 * j : 8 * j + 8, :] for j in range(16)]
    c = [lane_bc(t[0], q) for q in range(8)]
    for g in range(16):
        r0 = 8 * g
        own = (lane >= r0) & (lane < r0 + 8)
        near = range(g + 1, min(16, g + 1 + NEAR))
        far = range(g + 1 + NEAR, 16)
        b = {j: [lane_bc(t[j], r0 + q) for q in range(8)] for j in near}
        if g < 15:
            nc = [lane_bc(t[g + 1], r0 + 8 + q) for q in range(8)]
        p = jnp.where(own, jnp.where(lane - r0 == sub, 1.0, 0.0), t[g])
        raw = split2(jnp.concatenate([t[j] for j in far], axis=0)) if far else None
        for j in range(g + 1, 16):
            t[j] = jnp.where(own, 0.0, t[j])
        w, mults, invs = [], [], []
        low = jnp.zeros((8, 128), F32)
        for s in range(8):
            inv = lax.rsqrt(row_bc(c[s], s))
            col = c[s] * inv
            mult = {q: row_bc(col, q) for q in range(s + 1, 8)}
            for q in range(s + 1, 8):
                c[q] = c[q] - col * mult[q]
            ws = row_bc(p, s) * inv
            if s < 7:
                p = p - col * ws
            low = jnp.where(lane == r0 + s, col, low)
            for j in near:
                m = b[j][s] * inv
                for q in range(s + 1, 8):
                    b[j][q] = b[j][q] - m * mult[q]
                t[j] = t[j] - m * ws
                if j == g + 1:
                    for q in range(8):
                        nc[q] = nc[q] - m * row_bc(m, q)
            w.append(ws)
            mults.append(mult)
            invs.append(inv)
        full = w[0]
        for s in range(1, 8):
            full = jnp.where(sub == s, w[s], full)
        if far:
            y = [None] * 8
            for s in range(7, -1, -1):
                v = w[s]
                for q in range(7, s, -1):
                    v = v - mults[s][q] * y[q]
                y[s] = v * invs[s]
            yy = y[0]
            for s in range(1, 8):
                yy = jnp.where(sub == s, y[s], yy)
            pad = lambda v: jnp.concatenate(
                ([jnp.zeros((r0, 128), F32)] if r0 else []) + [v, jnp.zeros((120 - r0, 128), F32)], axis=0
            ).astype(BF16)
            yh = yy.astype(BF16).astype(F32)
            yhp, ylp = pad(yh), pad(yy - yh)
            upd = dot(jnp.concatenate(raw, axis=1), jnp.concatenate([yhp, yhp], axis=0)) + dot(raw[0], ylp)
            for n, j in enumerate(far):
                t[j] = t[j] - upd[8 * n : 8 * n + 8, :]
        rd[r0 : r0 + 8, :] = jnp.where(lane >= r0 + 8, full, 0.0)
        ds[r0 : r0 + 8, :] = jnp.where(lane < r0 + 8, full, 0.0)
        lt[r0 : r0 + 8, :] = low
        if g < 15:
            c = nc
        for step in beside[g]:
            step()
    rd[...] = rd[...] + jnp.transpose(lt[...])


LATE = 86
N_COPIES = LATE + 20


def kernel(
    w_in, st_in, co_in, rd_in, en_in, cd_in, br_in, pr_in, pi_in, t_in, o_ref,
    w_ref, st_ref, co_ref, rd_ref, en_ref, cd_ref, br_ref, pr_ref, pi_ref, t_s,
    wcat, hcat, sr, prt, p0, p1, r1, q, r2, zs, r3, b4, g,
    a_s, ds, rd, lt, dh_s, dl_s, rp_s, rt_s, rh_s, rl_s, th_s, tl_s, zv, in_sem, s_sem, r_sem,
):
    row = lax.axis_index("rows")
    core = lax.axis_index("cols")
    x, y, z = row // (NY * NZ), (row // NZ) % NY, row % NZ

    pairs = [
        (st_in, st_ref), (co_in, co_ref), (en_in, en_ref), (cd_in, cd_ref), (br_in, br_ref),
        (pr_in, pr_ref), (pi_in, pi_ref), (rd_in, rd_ref), (w_in, w_ref), (t_in, t_s),
    ]
    loads = [pltpu.make_async_copy(src, dst, in_sem.at[n]) for n, (src, dst) in enumerate(pairs)]
    for cp in loads:
        cp.start()

    def at_x(v, c=core):
        return ((v * NY + y) * NZ + z, c)

    def at_y(v, c=core):
        return ((x * NY + v) * NZ + z, c)

    def at_z(v):
        return ((x * NY + y) * NZ + v, core)

    other = 1 - core
    sibling = (row, other)
    hop = lambda v, d, n: lax.rem(v + d, n)
    xs = [hop(x, d, NX) for d in range(1, 4)]
    ys = [hop(y, d, NY) for d in range(1, 4)]
    zz = [hop(z, d, NZ) for d in range(1, 8)]
    barrier = pltpu.get_barrier_semaphore()
    friends = [at_x(v) for v in xs] + [at_y(v) for v in ys] + [at_z(v) for v in zz] + [sibling]
    friends += [at_x(v, other) for v in xs] + [at_y(v, other) for v in ys]
    for to in friends:
        pl.semaphore_signal(barrier, inc=1, device_id=to, device_id_type=MESH)

    copies = []

    def remote(n, src, dst, to):
        return pltpu.make_async_remote_copy(
            src_ref=src, dst_ref=dst, send_sem=s_sem.at[n], recv_sem=r_sem.at[n], device_id=to, device_id_type=MESH
        )

    def send(src, dst, to):
        cp = remote(len(copies), src, dst, to)
        cp.start()
        copies.append(cp)
        return cp

    def arrive(these):
        for cp in these:
            cp.wait_recv()

    for cp in loads[:-1]:
        cp.wait()
    build_rows(w_ref, st_ref, co_ref, rd_ref, en_ref, cd_ref, br_ref, pr_ref, pi_ref, wcat, hcat, sr, prt, p0, p1)
    me = [(x, y), (y, x)]
    peers = [(xs, ys), (ys, xs)]
    place = [(at_x, at_y), (at_y, at_x)]

    def first_out(c, h):
        p = (p0, p1)[h]
        n = r1[c][h].shape[1]
        start = c * (p.shape[1] - REST)
        own = me[h][0]
        out = [send(p.at[v, pl.ds(start, n)], r1[c][h].at[own], place[h][0](v)) for v in peers[h][0]]
        r1[c][h][own] = p[own, start : start + n]
        return out

    def second_out(c, h):
        size = (HEAD, REST)[c] // 4
        got = r1[c][h]
        for b in range(4):
            t = slice(size * b, size * b + size)
            q[c][h][b, 0:size] = (got[0, t] + got[1, t]) + (got[2, t] + got[3, t])
            if c == 0 and h == 0:
                q[c][h][b, size] = (got[0, HEAD] + got[1, HEAD]) + (got[2, HEAD] + got[3, HEAD])
        own = me[h][1]
        out = [send(q[c][h].at[v], r2[c][h].at[own], place[h][1](v)) for v in peers[h][1]]
        r2[c][h][own] = q[c][h][own]
        return out

    def z_out(c):
        a0, a1 = [(r2[c][h][0] + r2[c][h][1]) + (r2[c][h][2] + r2[c][h][3]) for h in range(2)]
        if c == 0:
            for n in range(4):
                zs[0][n, 0] = a0[n]
                zs[0][4 + n, 0] = a1[n]
            for n in range(8):
                zs[0][n, 1] = a0[4]
        else:
            for n in range(5):
                zs[1][n // 2, n % 2] = a0[n]
                zs[1][(5 + n) // 2, (5 + n) % 2] = a1[n]
            for n in range(5, 8):
                zs[1][n] = jnp.zeros((2, 8, 128), F32)
        out = [send(zs[c].at[v], r3[c].at[z], at_z(v)) for v in zz]
        r3[c][z] = zs[c][z]
        return out

    def z_back(c):
        total = [r3[c][n] for n in range(8)]
        total = ((total[0] + total[1]) + (total[2] + total[3])) + ((total[4] + total[5]) + (total[6] + total[7]))
        size = 1 + c
        b4[c][z] = total[0:size]
        out = [send(b4[c].at[z], b4[c].at[z], at_z(v)) for v in zz]
        return out, total[1]

    def second_back(c):
        size = (HEAD, REST)[c] // 4
        out = []
        for h in range(2):
            begin = c * HEAD + size * me[h][1]
            for n in range(size):
                at = size * h + n
                g[core, h, me[h][0], begin + n] = b4[c][at // (1 + c), at % (1 + c)]
            mine = g.at[core, h, me[h][0], pl.ds(begin, size)]
            out.append([send(mine, mine, place[h][1](v)) for v in peers[h][1]])
        return out

    build_gram(core, 0, en_ref, cd_ref, wcat, hcat, sr, prt, p0)
    pl.semaphore_wait(barrier, len(friends))
    one0 = [first_out(0, 0)]
    build_gram(core, 1, en_ref, cd_ref, wcat, hcat, sr, prt, p1)
    one0.append(first_out(0, 1))
    one1 = [first_out(1, 0), first_out(1, 1)]
    for i in range(1, 8):
        a_s[i, :, :, 0:1024] = jnp.zeros((16, 8, 1024), F32)
    a_s[8] = jnp.zeros((16, 8, 1152), F32)
    dh_s[8] = jnp.zeros((128, 128), BF16)
    dl_s[8] = jnp.zeros((128, 128), BF16)
    loads[-1].wait()
    th_s[...], tl_s[...] = split2(t_s[...])
    two0, two1 = [], []
    for h in range(2):
        arrive(one0[h])
        two0.append(second_out(0, h))
    for h in range(2):
        arrive(one1[h])
        two1.append(second_out(1, h))
    arrive(two0[0] + two0[1])
    z0 = z_out(0)
    arrive(two1[0] + two1[1])
    z1 = z_out(1)
    arrive(z0)
    back0, moment = z_back(0)
    for i in range(8):
        a_s[i, :, :, 1024:] = spread(moment[i : i + 1, :]).reshape(16, 8, 128)
    arrive(z1)
    back1, _ = z_back(1)
    arrive(back0)
    two0 = second_back(0)
    arrive(back1)
    two1 = second_back(1)
    top = []
    for h in range(2):
        arrive(two0[h])
        mine = g.at[core, h, me[h][0], pl.ds(0, 8)]
        for c in (core, other):
            top += [send(mine, mine, place[h][0](v, c)) for v in peers[h][0]]
        top.append(send(mine, mine, sibling))
    row1, row1_own = [], []
    for h in range(2):
        mine = g.at[core, h, me[h][0], pl.ds(8, 8)]
        row1.append([send(mine, mine, place[h][0](v)) for v in peers[h][0]])
        row1_own.append(send(mine, mine, sibling))
    assert len(copies) == LATE
    arrive(top)
    for j in range(8):
        for c in range(2):
            for h in range(2):
                a_s[0, 8 * c + 4 * h : 8 * c + 4 * h + 4, :, 128 * j : 128 * j + 128] = g[c, h, :, j]

    def relay(c, d, h):
        size = (NX, NY)[h]
        part = pl.ds(8, 8) if c == 0 else pl.ds(HEAD, REST)
        got = g.at[core, h, hop(me[h][0], size - 1 - d, size), part]
        return remote(LATE + 6 * c + 2 * d + h, got, got, sibling)

    def rest_out(d, h):
        mine = g.at[core, h, me[h][0], pl.ds(HEAD, REST)]
        if d == 3:
            return remote(LATE + 18 + h, mine, mine, sibling)
        return remote(LATE + 12 + 2 * d + h, mine, mine, place[h][0](peers[h][0][d]))

    halves = [(d, h) for d in range(3) for h in range(2)]

    def add_rows(tiles):
        for i, j in tiles:
            cols = slice(128 * j, 128 * j + 128)
            for c in range(2):
                for h in range(2):
                    at = slice(8 * c + 4 * h, 8 * c + 4 * h + 4)
                    a_s[i, at, :, cols] = a_s[i, at, :, cols] + g[c, h, :, FIRST[i] + j - i]

    def add_diagonal(i):
        for c in range(2):
            for h in range(2):
                at = slice(64 * c + 32 * h, 64 * c + 32 * h + 32)
                ds[at, :] = ds[at, :] + g[c, h, :, FIRST[i]].reshape(32, 128)

    def panel(k, _):
        @pl.when(k == 1)
        def _():
            arrive(row1_own + [relay(0, d, h) for d, h in halves])
            add_rows([(1, j) for j in range(2, 8)])
            add_diagonal(1)

        @pl.when(k == 2)
        def _():
            arrive([rest_out(3, 0), rest_out(3, 1)] + [relay(1, d, h) for d, h in halves])
            add_rows([(i, j) for i in range(2, 8) for j in range(i, 8) if j > 2])
            add_diagonal(2)

        prev = jnp.where(k == 0, 8, k - 1)
        dcat = jnp.concatenate([dh_s[prev], dl_s[prev], dh_s[prev]], axis=1)

        def product(j):
            def step():
                cols = slice(128 * j, 128 * j + 256)
                ah, al = split2(a_s[prev, :, :, cols].reshape(128, 256))
                r = dot(dcat, jnp.concatenate([ah, ah, al], axis=0))
                a_s[prev, :, :, cols] = r.reshape(16, 8, 256)
                rh, rl = split2(r)
                rp_s[0:128, cols] = rh
                rp_s[128:256, cols] = rh
                rp_s[256:384, cols] = rl
                rh_s[prev, :, cols] = rh
                rl_s[prev, :, cols] = rl
                for i in range(j, min(j + 2, 8)):
                    th, tl = split2(jnp.transpose(r[:, 128 * (i - j) : 128 * (i - j) + 128]))
                    rt_s[i] = jnp.concatenate([th, tl, th], axis=1)

            return step

        def update(i, j):
            def step():
                end = min(j + 2, 9)
                cols = slice(128 * j, 128 * end)
                to = jnp.where(i >= k, i, 8)
                upd = dot(rt_s[i], rp_s[:, cols])
                a_s[to, :, :, cols] = a_s[to, :, :, cols] - upd.reshape(16, 8, 128 * (end - j))

            return step

        steps = [product(j) for j in range(1, 9, 2)]
        steps += [update(i, j) for i in range(1, 8) for j in range(i, 9, 2)]
        factor_block(ds, rd.at[k], lt, [steps[2 * n : 2 * n + 2] for n in range(16)])

        @pl.when(k == 0)
        def _():
            for d, h in halves:
                row1[h][d].wait_recv()
                relay(0, d, h).start()
            for h in range(2):
                arrive(two1[h])
                for d in range(4):
                    rest_out(d, h).start()

        @pl.when(k == 1)
        def _():
            for d, h in halves:
                rest_out(d, h).wait_recv()
                relay(1, d, h).start()

        d = split2(ds[...])
        dh_s[k], dl_s[k] = d
        nxt = pl.ds(pl.multiple_of(128 * k + 128, 128), 128)
        c = dot3(d, split2(a_s[k, :, :, nxt].reshape(128, 128)))
        ds[...] = a_s[k + 1, :, :, nxt].reshape(128, 128) - dot3(split2(jnp.transpose(c)), split2(c))
        return 0

    ds[...] = a_s[0, :, :, 0:128].reshape(128, 128)
    lax.fori_loop(0, 8, panel, 0)

    z7 = dot3((dh_s[7], dl_s[7]), split2(a_s[7, :, :, 1024:].reshape(128, 128)))
    v = [jnp.transpose(a_s[i, :, :, 1024:].reshape(128, 128))[0:8, :] for i in range(7)] + [jnp.transpose(z7)[0:8, :]]
    for i in range(8):
        zv[i : i + 1, :] = v[i][0:1, :]
    e = [None] * 8
    for k in range(7, -1, -1):
        e[k] = dot3(split2(v[k]), (dh_s[k], dl_s[k]))
        ek = split2(e[k])
        for p in range(k - 1, -1, -1):
            at = slice(128 * k, 128 * k + 128)
            v[p] = v[p] - dot3(ek, (rh_s[p, :, at], rl_s[p, :, at]), NT)
    nxt = dot3(split2(jnp.concatenate(e, axis=1)), (th_s[...], tl_s[...]), NT)
    for q in range(4):
        o_ref[8:9, 128 * q : 128 * q + 128] = zv[pl.ds(core * 4 + q, 1), :]
    o_ref[9:10, :] = nxt[0:1, :]
    o_ref[10:16, :] = jnp.zeros((6, 512), F32)
    for k in range(8):
        a_s[k, :, :, 128 * k : 128 * k + 128] = rd[k].reshape(16, 8, 128)
    mine = a_s[row // 16, row % 16, :, pl.ds(pl.multiple_of(core * 512, 512), 512)]
    at_row = row * 8 + lax.broadcasted_iota(jnp.int32, (8, 512), 0)
    at_col = core * 512 + lax.broadcasted_iota(jnp.int32, (8, 512), 1)
    o_ref[0:8, :] = jnp.where(at_col >= at_row, mine, 0.0)
    for cp in copies + [relay(c, d, h) for c in range(2) for d, h in halves]:
        cp.wait_send()
    for d in range(4):
        for h in range(2):
            rest_out(d, h).wait_send()


def hand_out(all_ref, r_ref, z_ref, x_ref):
    r_ref[...] = all_ref[0:8, :]
    z_ref[...] = all_ref[8:9, :]
    x_ref[...] = all_ref[9:10, :]


def per_device(
    whitening,
    sensor_states,
    sensor_coefficients,
    sensor_readings,
    conduit_endpoints,
    conductance,
    balance_right_side,
    prior_root_factor,
    prior_information,
    transition,
):
    args = (
        whitening,
        sensor_states.T,
        sensor_coefficients.T,
        sensor_readings.reshape(3, 128),
        conduit_endpoints.T,
        conductance.reshape(1, BALANCE),
        balance_right_side.reshape(1, BALANCE),
        prior_root_factor,
        prior_information.reshape(1, 8),
        transition,
    )
    vmem = pl.BlockSpec(memory_space=pltpu.VMEM)
    tiles = lambda *lead: pltpu.VMEM(lead + (8, 128), F32)
    results = pl.pallas_call(
        kernel,
        out_shape=jax.ShapeDtypeStruct((16, 512), F32),
        in_specs=[pl.BlockSpec(memory_space=pl.ANY)] * len(args),
        out_specs=vmem,
        scratch_shapes=[pltpu.VMEM(arg.shape, arg.dtype) for arg in args]
        + [
            pltpu.VMEM((SENSORS, 3 * SENSORS), BF16),
            pltpu.VMEM((1024, 3 * SENSORS), BF16),
            pltpu.VMEM((DEPTH, 1024), BF16),
            pltpu.VMEM((1024, 128), BF16),
            tiles(4, 37),
            tiles(4, 36),
            [[tiles(4, 17), tiles(4, 16)], [tiles(4, 20), tiles(4, 20)]],
            [[tiles(4, 5), tiles(4, 4)], [tiles(4, 5), tiles(4, 5)]],
            [[tiles(4, 5), tiles(4, 4)], [tiles(4, 5), tiles(4, 5)]],
            [tiles(8, 2), tiles(8, 2)],
            [tiles(8, 2), tiles(8, 2)],
            [tiles(8, 1), tiles(8, 2)],
            tiles(2, 2, 4, 36),
            pltpu.VMEM((9, 16, 8, 1152), F32),
            pltpu.VMEM((128, 128), F32),
            pltpu.VMEM((8, 128, 128), F32),
            pltpu.VMEM((128, 128), F32),
            pltpu.VMEM((9, 128, 128), BF16),
            pltpu.VMEM((9, 128, 128), BF16),
            pltpu.VMEM((384, 1152), BF16),
            pltpu.VMEM((8, 128, 384), BF16),
            pltpu.VMEM((9, 128, 1152), BF16),
            pltpu.VMEM((9, 128, 1152), BF16),
            pltpu.VMEM((512, 1024), BF16),
            pltpu.VMEM((512, 1024), BF16),
            pltpu.VMEM((8, 128), F32),
            pltpu.SemaphoreType.DMA((10,)),
            pltpu.SemaphoreType.DMA((N_COPIES,)),
            pltpu.SemaphoreType.DMA((N_COPIES,)),
        ],
        compiler_params=pltpu.CompilerParams(
            collective_id=0, has_side_effects=True, vmem_limit_bytes=62 * 1024 * 1024
        ),
    )(*args)
    r_post, z_post, x_next = pl.pallas_call(
        hand_out,
        out_shape=(
            jax.ShapeDtypeStruct((8, 512), F32),
            jax.ShapeDtypeStruct((1, 512), F32),
            jax.ShapeDtypeStruct((1, 512), F32),
        ),
        in_specs=[vmem],
        out_specs=(vmem, vmem, vmem),
        compiler_params=pltpu.CompilerParams(vmem_limit_bytes=62 * 1024 * 1024),
    )(results)
    return r_post, z_post.reshape(512), x_next.reshape(512)


def solution(mesh):
    in_specs = (
        P("rows", None),
        P("rows", None),
        P("rows", None),
        P("rows"),
        P("rows", None),
        P("rows"),
        P("rows"),
        P("rows", None),
        P("rows"),
        P("cols", None),
    )
    out_specs = (P("rows", "cols"), P("cols"), P("cols"))
    return jax.shard_map(
        per_device, mesh=mesh, in_specs=in_specs, out_specs=out_specs, check_vma=False
    )
```

```python
import jax
import jax.numpy as jnp
from jax import lax
from jax.experimental import pallas as pl
from jax.experimental.pallas import tpu as pltpu
from jax.sharding import PartitionSpec as P

F32, BF16 = jnp.float32, jnp.bfloat16
MESH = pl.DeviceIdType.MESH
NX, NY, NZ = 4, 4, 8
SENSORS, BALANCE = 384, 128
DEPTH = 3 * (SENSORS + BALANCE) + 128
FIRST = [0, 8, 15, 21, 26, 30, 33, 35, 36]
HEAD, REST = 16, 20
NN = (((1,), (0,)), ((), ()))
NT = (((1,), (1,)), ((), ()))
TN = (((0,), (0,)), ((), ()))


def dot(a, b, dims=NN):
    return lax.dot_general(a, b, dims, preferred_element_type=F32)


def split2(x):
    hi = x.astype(BF16)
    return hi, (x - hi.astype(F32)).astype(BF16)


def split3(x):
    hi = x.astype(BF16)
    rest = x - hi.astype(F32)
    mid = rest.astype(BF16)
    return hi, mid, (rest - mid.astype(F32)).astype(BF16)


def dot3(a, b, dims=NN):
    return dot(a[0], b[0], dims) + (dot(a[0], b[1], dims) + dot(a[1], b[0], dims))


def spread(row):
    return jnp.transpose(jnp.broadcast_to(row, (128, 128)))


def build_rows(w_ref, st_ref, co_ref, en_ref, cd_ref, pr_ref, pi_ref, wcat, hcat, sr, prt, mrow):
    w = split2(w_ref[...])
    wcat[...] = jnp.concatenate([w[0], w[1], w[0]], axis=1)
    cond_row = cd_ref[...]
    cond = spread(cond_row)
    ends = [spread(en_ref[k : k + 1, :].astype(F32)).astype(jnp.int32) for k in range(2)]
    info = spread(jnp.concatenate([pi_ref[...], jnp.zeros((1, 120), F32)], axis=1))[0:8, :]
    for j in range(8):
        cols = slice(128 * j, 128 * j + 128)
        ids = 128 * j + lax.broadcasted_iota(jnp.int32, (128, SENSORS), 0)
        h = jnp.zeros((128, SENSORS), F32)
        for k in range(4):
            h = h + jnp.where(ids == st_ref[k : k + 1, :], co_ref[k : k + 1, :], 0.0)
        hh, hl = split2(h)
        hj = jnp.concatenate([hh, hh, hl], axis=1)
        hcat[cols, :] = hj
        s = dot(wcat[...], hj, NT)
        bids = 128 * j + lax.broadcasted_iota(jnp.int32, (BALANCE, 128), 1)
        bal = jnp.where(bids == ends[0], cond, 0.0) - jnp.where(bids == ends[1], cond, 0.0)
        fh, fl = split2(jnp.concatenate([s, bal], axis=0))
        sr[0:512, cols] = fh
        sr[512:1024, cols] = fh
        sr[1024:1536, cols] = fl
        prior = pr_ref[:, cols]
        ph, pm, pl_ = [part.astype(F32) for part in split3(prior)]
        none = jnp.zeros((80, 128), F32)
        sr[1536:1664, cols] = jnp.concatenate([ph, pm, ph, pl_, ph, pm, none], axis=0).astype(BF16)
        prt[cols, :] = jnp.transpose(jnp.concatenate([ph, ph, pm, ph, pl_, pm, none], axis=0)).astype(BF16)
        mrow[:, cols] = jnp.sum(prior * info, axis=0, keepdims=True)


def build_gram(core, half, rd_ref, br_ref, en_ref, cd_ref, wcat, hcat, sr, prt, mrow, out):
    at = [pl.ds(pl.multiple_of(128 * i + 64 * core + 32 * half, 32), 32) for i in range(8)]
    extra = 16 if half == 0 else 0
    rows = [hcat[r, :] for r in at]
    if half == 0:
        readings = jnp.concatenate([rd_ref[k : k + 1, :] for k in range(3)], axis=1)
        rh, rl = split2(jnp.broadcast_to(readings, (extra, SENSORS)))
        rows.append(jnp.concatenate([rh, rh, rl], axis=1))
    st = dot(jnp.concatenate(rows, axis=0), wcat[...], NT)
    ids = lax.broadcasted_iota(jnp.int32, (32, BALANCE), 0) + (64 * core + 32 * half)
    cond = cd_ref[...]
    bal = [
        jnp.where(ids + 128 * i == en_ref[0:1, :], cond, 0.0) - jnp.where(ids + 128 * i == en_ref[1:2, :], cond, 0.0)
        for i in range(8)
    ]
    prior = [prt[r, :] for r in at]
    if half == 0:
        bal.append(jnp.broadcast_to(cond * br_ref[...], (extra, BALANCE)))
        prior.append(jnp.zeros((extra, 128), BF16))
    th, tl = split2(jnp.concatenate([st, jnp.concatenate(bal, axis=0)], axis=1))
    lhs = jnp.concatenate([th, tl, th, jnp.concatenate(prior, axis=0)], axis=1)
    if half == 0:
        lhs = jnp.concatenate([lhs[256:, :], lhs[:256, :]], axis=0)
    for j0 in range(0, 8, 2):
        cols = slice(128 * j0, 128 * j0 + 256)
        wide = dot(lhs[0 : extra + 32 * (j0 + 2), :], sr[:, cols])
        if half == 0:
            mom = wide[0:1, :] + mrow[:, cols]
            for a in range(4):
                out[a, HEAD, j0 : j0 + 1, :] = mom[:, 0:128]
                out[a, HEAD, j0 + 1 : j0 + 2, :] = mom[:, 128:256]
            wide = wide[extra:, :]
        for j in (j0, j0 + 1):
            for i in range(j + 1):
                blk = wide[32 * i : 32 * i + 32, 128 * (j - j0) : 128 * (j - j0) + 128]
                at = FIRST[i] + j - i
                out[:, at + (1 if half == 0 and at >= HEAD else 0)] = blk.reshape(4, 8, 128)


def lane_bc(x, lane):
    return jnp.broadcast_to(x[:, lane : lane + 1], (8, 128))


def row_bc(x, row):
    return jnp.broadcast_to(x[row : row + 1, :], (8, 128))


NEAR = 7


def factor_block(ds, rd, lt, beside):
    lane = lax.broadcasted_iota(jnp.int32, (8, 128), 1)
    sub = lax.broadcasted_iota(jnp.int32, (8, 128), 0)
    t = [ds[8 * j : 8 * j + 8, :] for j in range(16)]
    c = [lane_bc(t[0], q) for q in range(8)]
    for g in range(16):
        r0 = 8 * g
        own = (lane >= r0) & (lane < r0 + 8)
        near = range(g + 1, min(16, g + 1 + NEAR))
        far = range(g + 1 + NEAR, 16)
        b = {j: [lane_bc(t[j], r0 + q) for q in range(8)] for j in near}
        if g < 15:
            nc = [lane_bc(t[g + 1], r0 + 8 + q) for q in range(8)]
        p = jnp.where(own, jnp.where(lane - r0 == sub, 1.0, 0.0), t[g])
        raw = split2(jnp.concatenate([t[j] for j in far], axis=0)) if far else None
        for j in range(g + 1, 16):
            t[j] = jnp.where(own, 0.0, t[j])
        w, mults, invs = [], [], []
        low = jnp.zeros((8, 128), F32)
        for s in range(8):
            inv = lax.rsqrt(row_bc(c[s], s))
            col = c[s] * inv
            mult = {q: row_bc(col, q) for q in range(s + 1, 8)}
            for q in range(s + 1, 8):
                c[q] = c[q] - col * mult[q]
            ws = row_bc(p, s) * inv
            if s < 7:
                p = p - col * ws
            low = jnp.where(lane == r0 + s, col, low)
            for j in near:
                m = b[j][s] * inv
                for q in range(s + 1, 8):
                    b[j][q] = b[j][q] - m * mult[q]
                t[j] = t[j] - m * ws
                if j == g + 1:
                    for q in range(8):
                        nc[q] = nc[q] - m * row_bc(m, q)
            w.append(ws)
            mults.append(mult)
            invs.append(inv)
        full = w[0]
        for s in range(1, 8):
            full = jnp.where(sub == s, w[s], full)
        if far:
            y = [None] * 8
            for s in range(7, -1, -1):
                v = w[s]
                for q in range(7, s, -1):
                    v = v - mults[s][q] * y[q]
                y[s] = v * invs[s]
            yy = y[0]
            for s in range(1, 8):
                yy = jnp.where(sub == s, y[s], yy)
            pad = lambda v: jnp.concatenate(
                ([jnp.zeros((r0, 128), F32)] if r0 else []) + [v, jnp.zeros((120 - r0, 128), F32)], axis=0
            ).astype(BF16)
            yh = yy.astype(BF16).astype(F32)
            yhp, ylp = pad(yh), pad(yy - yh)
            upd = dot(jnp.concatenate(raw, axis=1), jnp.concatenate([yhp, yhp], axis=0)) + dot(raw[0], ylp)
            for n, j in enumerate(far):
                t[j] = t[j] - upd[8 * n : 8 * n + 8, :]
        rd[r0 : r0 + 8, :] = jnp.where(lane >= r0 + 8, full, 0.0)
        ds[r0 : r0 + 8, :] = jnp.where(lane < r0 + 8, full, 0.0)
        lt[r0 : r0 + 8, :] = low
        if g < 15:
            c = nc
        for step in beside[g]:
            step()
    rd[...] = rd[...] + jnp.transpose(lt[...])


LATE = 86
N_COPIES = LATE + 20


def kernel(
    w_in, st_in, co_in, rd_in, en_in, cd_in, br_in, pr_in, pi_in, t_in, o_ref,
    w_ref, st_ref, co_ref, rd_ref, en_ref, cd_ref, br_ref, pr_ref, pi_ref, t_s,
    wcat, hcat, sr, prt, mrow, p0, p1, r1, q, r2, zs, r3, b4, g,
    a_s, ds, rd, lt, dh_s, dl_s, gh_s, gl_s, rp_s, rt_s, rh_s, rl_s, th_s, tl_s, zv, in_sem, s_sem, r_sem,
):
    row = lax.axis_index("rows")
    core = lax.axis_index("cols")
    x, y, z = row // (NY * NZ), (row // NZ) % NY, row % NZ

    pairs = [
        (st_in, st_ref), (co_in, co_ref), (en_in, en_ref), (cd_in, cd_ref), (br_in, br_ref),
        (pr_in, pr_ref), (pi_in, pi_ref), (rd_in, rd_ref), (w_in, w_ref), (t_in, t_s),
    ]
    loads = [pltpu.make_async_copy(src, dst, in_sem.at[n]) for n, (src, dst) in enumerate(pairs)]
    for cp in loads:
        cp.start()

    def at_x(v):
        return ((v * NY + y) * NZ + z, core)

    def at_y(v):
        return ((x * NY + v) * NZ + z, core)

    def at_z(v):
        return ((x * NY + y) * NZ + v, core)

    sibling = (row, 1 - core)
    hop = lambda v, d, n: lax.rem(v + d, n)
    xs = [hop(x, d, NX) for d in range(1, 4)]
    ys = [hop(y, d, NY) for d in range(1, 4)]
    zz = [hop(z, d, NZ) for d in range(1, 8)]
    barrier = pltpu.get_barrier_semaphore()
    friends = [at_x(v) for v in xs] + [at_y(v) for v in ys] + [at_z(v) for v in zz] + [sibling]
    for to in friends:
        pl.semaphore_signal(barrier, inc=1, device_id=to, device_id_type=MESH)

    copies = []

    def remote(n, src, dst, to):
        return pltpu.make_async_remote_copy(
            src_ref=src, dst_ref=dst, send_sem=s_sem.at[n], recv_sem=r_sem.at[n], device_id=to, device_id_type=MESH
        )

    def send(src, dst, to):
        cp = remote(len(copies), src, dst, to)
        cp.start()
        copies.append(cp)
        return cp

    def arrive(these):
        for cp in these:
            cp.wait_recv()

    for cp in loads[:-1]:
        cp.wait()
    build_rows(w_ref, st_ref, co_ref, en_ref, cd_ref, pr_ref, pi_ref, wcat, hcat, sr, prt, mrow)
    me = [(x, y), (y, x)]
    peers = [(xs, ys), (ys, xs)]
    place = [(at_x, at_y), (at_y, at_x)]

    def first_out(c, h):
        p = (p0, p1)[h]
        n = r1[c][h].shape[1]
        start = c * (p.shape[1] - REST)
        own = me[h][0]
        out = [send(p.at[v, pl.ds(start, n)], r1[c][h].at[own], place[h][0](v)) for v in peers[h][0]]
        r1[c][h][own] = p[own, start : start + n]
        return out

    def second_out(c, h):
        size = (HEAD, REST)[c] // 4
        got = r1[c][h]
        for b in range(4):
            t = slice(size * b, size * b + size)
            q[c][h][b, 0:size] = (got[0, t] + got[1, t]) + (got[2, t] + got[3, t])
            if c == 0 and h == 0:
                q[c][h][b, size] = (got[0, HEAD] + got[1, HEAD]) + (got[2, HEAD] + got[3, HEAD])
        own = me[h][1]
        out = [send(q[c][h].at[v], r2[c][h].at[own], place[h][1](v)) for v in peers[h][1]]
        r2[c][h][own] = q[c][h][own]
        return out

    def z_out(c):
        a0, a1 = [(r2[c][h][0] + r2[c][h][1]) + (r2[c][h][2] + r2[c][h][3]) for h in range(2)]
        if c == 0:
            for n in range(4):
                zs[0][n, 0] = a0[n]
                zs[0][4 + n, 0] = a1[n]
            for n in range(8):
                zs[0][n, 1] = a0[4]
        else:
            for n in range(5):
                zs[1][n // 2, n % 2] = a0[n]
                zs[1][(5 + n) // 2, (5 + n) % 2] = a1[n]
            for n in range(5, 8):
                zs[1][n] = jnp.zeros((2, 8, 128), F32)
        out = [send(zs[c].at[v], r3[c].at[z], at_z(v)) for v in zz]
        r3[c][z] = zs[c][z]
        return out

    def z_back(c):
        total = [r3[c][n] for n in range(8)]
        total = ((total[0] + total[1]) + (total[2] + total[3])) + ((total[4] + total[5]) + (total[6] + total[7]))
        size = 1 + c
        b4[c][z] = total[0:size]
        out = [send(b4[c].at[z], b4[c].at[z], at_z(v)) for v in zz]
        return out, total[1]

    def second_back(c):
        size = (HEAD, REST)[c] // 4
        out = []
        for h in range(2):
            begin = c * HEAD + size * me[h][1]
            for n in range(size):
                at = size * h + n
                g[core, h, me[h][0], begin + n] = b4[c][at // (1 + c), at % (1 + c)]
            mine = g.at[core, h, me[h][0], pl.ds(begin, size)]
            out.append([send(mine, mine, place[h][1](v)) for v in peers[h][1]])
        return out

    build_gram(core, 0, rd_ref, br_ref, en_ref, cd_ref, wcat, hcat, sr, prt, mrow, p0)
    pl.semaphore_wait(barrier, len(friends))
    one0 = [first_out(0, 0)]
    build_gram(core, 1, rd_ref, br_ref, en_ref, cd_ref, wcat, hcat, sr, prt, mrow, p1)
    one0.append(first_out(0, 1))
    one1 = [first_out(1, 0), first_out(1, 1)]
    for i in range(1, 8):
        a_s[i, :, :, 0:1024] = jnp.zeros((16, 8, 1024), F32)
    a_s[8] = jnp.zeros((16, 8, 1152), F32)
    dh_s[8] = jnp.zeros((128, 128), BF16)
    dl_s[8] = jnp.zeros((128, 128), BF16)
    loads[-1].wait()
    th_s[...], tl_s[...] = split2(t_s[...])
    two0, two1 = [], []
    for h in range(2):
        arrive(one0[h])
        two0.append(second_out(0, h))
    for h in range(2):
        arrive(one1[h])
        two1.append(second_out(1, h))
    arrive(two0[0] + two0[1])
    z0 = z_out(0)
    arrive(two1[0] + two1[1])
    z1 = z_out(1)
    arrive(z0)
    back0, moment = z_back(0)
    for i in range(8):
        a_s[i, :, :, 1024:] = spread(moment[i : i + 1, :]).reshape(16, 8, 128)
    arrive(z1)
    back1, _ = z_back(1)
    arrive(back0)
    two0 = second_back(0)
    arrive(back1)
    two1 = second_back(1)
    top, own = [], []
    for h in range(2):
        arrive(two0[h])
        mine = g.at[core, h, me[h][0], pl.ds(0, 8)]
        top.append([send(mine, mine, place[h][0](v)) for v in peers[h][0]])
        own.append(send(mine, mine, sibling))
    row1, row1_own = [], []
    for h in range(2):
        mine = g.at[core, h, me[h][0], pl.ds(8, 8)]
        row1.append([send(mine, mine, place[h][0](v)) for v in peers[h][0]])
        row1_own.append(send(mine, mine, sibling))
    for d in range(3):
        for h in range(2):
            top[h][d].wait_recv()
            size = (NX, NY)[h]
            got = g.at[core, h, hop(me[h][0], size - 1 - d, size), pl.ds(0, 8)]
            own.append(send(got, got, sibling))
    arrive(own)
    assert len(copies) == LATE
    for j in range(8):
        for c in range(2):
            for h in range(2):
                a_s[0, 8 * c + 4 * h : 8 * c + 4 * h + 4, :, 128 * j : 128 * j + 128] = g[c, h, :, j]

    def relay(c, d, h):
        size = (NX, NY)[h]
        part = pl.ds(8, 8) if c == 0 else pl.ds(HEAD, REST)
        got = g.at[core, h, hop(me[h][0], size - 1 - d, size), part]
        return remote(LATE + 6 * c + 2 * d + h, got, got, sibling)

    def rest_out(d, h):
        mine = g.at[core, h, me[h][0], pl.ds(HEAD, REST)]
        if d == 3:
            return remote(LATE + 18 + h, mine, mine, sibling)
        return remote(LATE + 12 + 2 * d + h, mine, mine, place[h][0](peers[h][0][d]))

    halves = [(d, h) for d in range(3) for h in range(2)]

    def add_rows(tiles):
        for i, j in tiles:
            cols = slice(128 * j, 128 * j + 128)
            for c in range(2):
                for h in range(2):
                    at = slice(8 * c + 4 * h, 8 * c + 4 * h + 4)
                    a_s[i, at, :, cols] = a_s[i, at, :, cols] + g[c, h, :, FIRST[i] + j - i]

    def add_diagonal(i):
        for c in range(2):
            for h in range(2):
                at = slice(64 * c + 32 * h, 64 * c + 32 * h + 32)
                ds[at, :] = ds[at, :] + g[c, h, :, FIRST[i]].reshape(32, 128)

    def panel(k, _):
        @pl.when(k == 1)
        def _():
            arrive(row1_own + [relay(0, d, h) for d, h in halves])
            add_rows([(1, j) for j in range(2, 8)])
            add_diagonal(1)

        @pl.when(k == 2)
        def _():
            arrive([rest_out(3, 0), rest_out(3, 1)] + [relay(1, d, h) for d, h in halves])
            add_rows([(i, j) for i in range(2, 8) for j in range(i, 8) if j > 2])
            add_diagonal(2)

        prev = jnp.where(k == 0, 8, k - 1)
        dcat = jnp.concatenate([dh_s[prev], dl_s[prev], dh_s[prev]], axis=1)

        def product(j):
            def step():
                cols = slice(128 * j, 128 * j + 256)
                ah, al = split2(a_s[prev, :, :, cols].reshape(128, 256))
                r = dot(dcat, jnp.concatenate([ah, ah, al], axis=0))
                a_s[prev, :, :, cols] = r.reshape(16, 8, 256)
                rh, rl = split2(r)
                rp_s[0:128, cols] = rh
                rp_s[128:256, cols] = rh
                rp_s[256:384, cols] = rl
                rh_s[prev, :, cols] = rh
                rl_s[prev, :, cols] = rl
                for i in range(j, min(j + 2, 8)):
                    th, tl = split2(jnp.transpose(r[:, 128 * (i - j) : 128 * (i - j) + 128]))
                    rt_s[i] = jnp.concatenate([th, tl, th], axis=1)

            return step

        def couple():
            by = dot(rt_s[k], jnp.concatenate([dh_s[prev], dh_s[prev], dl_s[prev]], axis=0))
            gh_s[prev], gl_s[prev] = split2(by)

        def update(i, j):
            def step():
                end = min(j + 2, 9)
                cols = slice(128 * j, 128 * end)
                to = jnp.where(i >= k, i, 8)
                upd = dot(rt_s[i], rp_s[:, cols])
                a_s[to, :, :, cols] = a_s[to, :, :, cols] - upd.reshape(16, 8, 128 * (end - j))

            return step

        steps = [product(j) for j in range(1, 9, 2)]
        steps.append(couple)
        steps += [update(i, j) for i in range(1, 8) for j in range(i, 9, 2)]
        factor_block(ds, rd.at[k], lt, [steps[2 * n : 2 * n + 2] for n in range(16)])

        @pl.when(k == 0)
        def _():
            for d, h in halves:
                row1[h][d].wait_recv()
                relay(0, d, h).start()
            for h in range(2):
                arrive(two1[h])
                for d in range(4):
                    rest_out(d, h).start()

        @pl.when(k == 1)
        def _():
            for d, h in halves:
                rest_out(d, h).wait_recv()
                relay(1, d, h).start()

        d = split2(ds[...])
        dh_s[k], dl_s[k] = d
        nxt = pl.ds(pl.multiple_of(128 * k + 128, 128), 128)
        c = dot3(d, split2(a_s[k, :, :, nxt].reshape(128, 128)))
        ds[...] = a_s[k + 1, :, :, nxt].reshape(128, 128) - dot3(split2(jnp.transpose(c)), split2(c))
        return 0

    ds[...] = a_s[0, :, :, 0:128].reshape(128, 128)
    lax.fori_loop(0, 8, panel, 0)

    z7 = dot3((dh_s[7], dl_s[7]), split2(a_s[7, :, :, 1024:].reshape(128, 128)))
    v = [jnp.transpose(a_s[i, :, :, 1024:].reshape(128, 128))[0:8, :] for i in range(7)] + [jnp.transpose(z7)[0:8, :]]
    for i in range(8):
        zv[i : i + 1, :] = v[i][0:1, :]
    e, ek = [None] * 8, None
    for k in range(7, -1, -1):
        e[k] = dot3(split2(v[k]), (dh_s[k], dl_s[k]))
        if k < 7:
            e[k] = e[k] - dot3(ek, (gh_s[k], gl_s[k]))
        ek = split2(e[k])
        for p in range(k - 2, -1, -1):
            at = slice(128 * k, 128 * k + 128)
            v[p] = v[p] - dot3(ek, (rh_s[p, :, at], rl_s[p, :, at]), NT)
    nxt = dot3(split2(jnp.concatenate(e, axis=1)), (th_s[...], tl_s[...]), NT)
    for q in range(4):
        o_ref[8:9, 128 * q : 128 * q + 128] = zv[pl.ds(core * 4 + q, 1), :]
    o_ref[9:10, :] = nxt[0:1, :]
    o_ref[10:16, :] = jnp.zeros((6, 512), F32)
    mine = row // 16
    a_s[mine, :, :, pl.ds(pl.multiple_of(128 * mine, 128), 128)] = rd[mine].reshape(16, 8, 128)
    mine = a_s[row // 16, row % 16, :, pl.ds(pl.multiple_of(core * 512, 512), 512)]
    at_row = row * 8 + lax.broadcasted_iota(jnp.int32, (8, 512), 0)
    at_col = core * 512 + lax.broadcasted_iota(jnp.int32, (8, 512), 1)
    o_ref[0:8, :] = jnp.where(at_col >= at_row, mine, 0.0)
    for cp in copies + [relay(c, d, h) for c in range(2) for d, h in halves]:
        cp.wait_send()
    for d in range(4):
        for h in range(2):
            rest_out(d, h).wait_send()


def hand_out(all_ref, r_ref, z_ref, x_ref):
    r_ref[...] = all_ref[0:8, :]
    z_ref[...] = all_ref[8:9, :]
    x_ref[...] = all_ref[9:10, :]


def per_device(
    whitening,
    sensor_states,
    sensor_coefficients,
    sensor_readings,
    conduit_endpoints,
    conductance,
    balance_right_side,
    prior_root_factor,
    prior_information,
    transition,
):
    args = (
        whitening,
        sensor_states.T,
        sensor_coefficients.T,
        sensor_readings.reshape(3, 128),
        conduit_endpoints.T,
        conductance.reshape(1, BALANCE),
        balance_right_side.reshape(1, BALANCE),
        prior_root_factor,
        prior_information.reshape(1, 8),
        transition,
    )
    vmem = pl.BlockSpec(memory_space=pltpu.VMEM)
    tiles = lambda *lead: pltpu.VMEM(lead + (8, 128), F32)
    results = pl.pallas_call(
        kernel,
        out_shape=jax.ShapeDtypeStruct((16, 512), F32),
        in_specs=[pl.BlockSpec(memory_space=pl.ANY)] * len(args),
        out_specs=vmem,
        scratch_shapes=[pltpu.VMEM(arg.shape, arg.dtype) for arg in args]
        + [
            pltpu.VMEM((SENSORS, 3 * SENSORS), BF16),
            pltpu.VMEM((1024, 3 * SENSORS), BF16),
            pltpu.VMEM((DEPTH, 1024), BF16),
            pltpu.VMEM((1024, 128), BF16),
            pltpu.VMEM((1, 1024), F32),
            tiles(4, 37),
            tiles(4, 36),
            [[tiles(4, 17), tiles(4, 16)], [tiles(4, 20), tiles(4, 20)]],
            [[tiles(4, 5), tiles(4, 4)], [tiles(4, 5), tiles(4, 5)]],
            [[tiles(4, 5), tiles(4, 4)], [tiles(4, 5), tiles(4, 5)]],
            [tiles(8, 2), tiles(8, 2)],
            [tiles(8, 2), tiles(8, 2)],
            [tiles(8, 1), tiles(8, 2)],
            tiles(2, 2, 4, 36),
            pltpu.VMEM((9, 16, 8, 1152), F32),
            pltpu.VMEM((128, 128), F32),
            pltpu.VMEM((8, 128, 128), F32),
            pltpu.VMEM((128, 128), F32),
            pltpu.VMEM((9, 128, 128), BF16),
            pltpu.VMEM((9, 128, 128), BF16),
            pltpu.VMEM((9, 128, 128), BF16),
            pltpu.VMEM((9, 128, 128), BF16),
            pltpu.VMEM((384, 1152), BF16),
            pltpu.VMEM((8, 128, 384), BF16),
            pltpu.VMEM((9, 128, 1152), BF16),
            pltpu.VMEM((9, 128, 1152), BF16),
            pltpu.VMEM((512, 1024), BF16),
            pltpu.VMEM((512, 1024), BF16),
            pltpu.VMEM((8, 128), F32),
            pltpu.SemaphoreType.DMA((10,)),
            pltpu.SemaphoreType.DMA((N_COPIES,)),
            pltpu.SemaphoreType.DMA((N_COPIES,)),
        ],
        compiler_params=pltpu.CompilerParams(
            collective_id=0, has_side_effects=True, vmem_limit_bytes=62 * 1024 * 1024
        ),
    )(*args)
    r_post, z_post, x_next = pl.pallas_call(
        hand_out,
        out_shape=(
            jax.ShapeDtypeStruct((8, 512), F32),
            jax.ShapeDtypeStruct((1, 512), F32),
            jax.ShapeDtypeStruct((1, 512), F32),
        ),
        in_specs=[vmem],
        out_specs=(vmem, vmem, vmem),
        compiler_params=pltpu.CompilerParams(vmem_limit_bytes=62 * 1024 * 1024),
    )(results)
    return r_post, z_post.reshape(512), x_next.reshape(512)


def solution(mesh):
    in_specs = (
        P("rows", None),
        P("rows", None),
        P("rows", None),
        P("rows"),
        P("rows", None),
        P("rows"),
        P("rows"),
        P("rows", None),
        P("rows"),
        P("cols", None),
    )
    out_specs = (P("rows", "cols"), P("cols"), P("cols"))
    return jax.shard_map(
        per_device, mesh=mesh, in_specs=in_specs, out_specs=out_specs, check_vma=False
    )
```

```python
import jax
import jax.numpy as jnp
from jax import lax
from jax.experimental import pallas as pl
from jax.experimental.pallas import tpu as pltpu
from jax.sharding import PartitionSpec as P

F32, BF16 = jnp.float32, jnp.bfloat16
MESH = pl.DeviceIdType.MESH
NX, NY, NZ = 4, 4, 8
SENSORS, BALANCE = 384, 128
DEPTH = 3 * (SENSORS + BALANCE) + 128
FIRST = [0, 8, 15, 21, 26, 30, 33, 35, 36]
HEAD, REST = 16, 20
NN = (((1,), (0,)), ((), ()))
NT = (((1,), (1,)), ((), ()))
TN = (((0,), (0,)), ((), ()))


def dot(a, b, dims=NN):
    return lax.dot_general(a, b, dims, preferred_element_type=F32)


def split2(x):
    hi = x.astype(BF16)
    return hi, (x - hi.astype(F32)).astype(BF16)


def split3(x):
    hi = x.astype(BF16)
    rest = x - hi.astype(F32)
    mid = rest.astype(BF16)
    return hi, mid, (rest - mid.astype(F32)).astype(BF16)


def dot3(a, b, dims=NN):
    return dot(a[0], b[0], dims) + (dot(a[0], b[1], dims) + dot(a[1], b[0], dims))


def stack2(x):
    return jnp.concatenate(split2(x), axis=0)


def rows_dot(x, hi, lo, dims=NN):
    both = dot(x, hi, dims) + dot(x, lo, dims)
    return both[0:8, :] + both[8:16, :]


def spread(row):
    return jnp.transpose(jnp.broadcast_to(row, (128, 128)))


def build_rows(w_ref, st_ref, co_ref, en_ref, cd_ref, pr_ref, pi_ref, wcat, hcat, sr, prt, mrow):
    w = split2(w_ref[...])
    wcat[...] = jnp.concatenate([w[0], w[1], w[0]], axis=1)
    cond_row = cd_ref[...]
    cond = spread(cond_row)
    ends = [spread(en_ref[k : k + 1, :].astype(F32)).astype(jnp.int32) for k in range(2)]
    info = spread(jnp.concatenate([pi_ref[...], jnp.zeros((1, 120), F32)], axis=1))[0:8, :]
    twice = lambda v: jnp.concatenate([v, v], axis=1)
    cond, info, ends = twice(cond), twice(info), [twice(v) for v in ends]
    for j in range(0, 8, 2):
        cols = slice(128 * j, 128 * j + 256)
        ids = 128 * j + lax.broadcasted_iota(jnp.int32, (256, SENSORS), 0)
        h = jnp.zeros((256, SENSORS), F32)
        for k in range(4):
            h = h + jnp.where(ids == st_ref[k : k + 1, :], co_ref[k : k + 1, :], 0.0)
        hh, hl = split2(h)
        hj = jnp.concatenate([hh, hh, hl], axis=1)
        hcat[cols, :] = hj
        s = dot(wcat[...], hj, NT)
        bids = 128 * j + lax.broadcasted_iota(jnp.int32, (BALANCE, 256), 1)
        bal = jnp.where(bids == ends[0], cond, 0.0) - jnp.where(bids == ends[1], cond, 0.0)
        fh, fl = split2(jnp.concatenate([s, bal], axis=0))
        sr[0:512, cols] = fh
        sr[512:1024, cols] = fh
        sr[1024:1536, cols] = fl
        prior = pr_ref[:, cols]
        ph, pm, pl_ = [part.astype(F32) for part in split3(prior)]
        none = jnp.zeros((80, 256), F32)
        sr[1536:1664, cols] = jnp.concatenate([ph, pm, ph, pl_, ph, pm, none], axis=0).astype(BF16)
        packed = jnp.concatenate([ph, ph, pm, ph, pl_, pm, none], axis=0)
        for n in range(2):
            half = packed[:, 128 * n : 128 * n + 128]
            prt[128 * (j + n) : 128 * (j + n) + 128, :] = jnp.transpose(half).astype(BF16)
        mrow[:, cols] = jnp.sum(prior * info, axis=0, keepdims=True)


def build_gram(core, half, rd_ref, br_ref, en_ref, cd_ref, wcat, hcat, sr, prt, mrow, out):
    at = [pl.ds(pl.multiple_of(128 * i + 64 * core + 32 * half, 32), 32) for i in range(8)]
    extra = 16 if half == 0 else 0
    rows = [hcat[r, :] for r in at]
    if half == 0:
        readings = jnp.concatenate([rd_ref[k : k + 1, :] for k in range(3)], axis=1)
        rh, rl = split2(jnp.broadcast_to(readings, (extra, SENSORS)))
        rows.append(jnp.concatenate([rh, rh, rl], axis=1))
    st = dot(jnp.concatenate(rows, axis=0), wcat[...], NT)
    ids = lax.broadcasted_iota(jnp.int32, (32, BALANCE), 0) + (64 * core + 32 * half)
    cond = cd_ref[...]
    bal = [
        jnp.where(ids + 128 * i == en_ref[0:1, :], cond, 0.0) - jnp.where(ids + 128 * i == en_ref[1:2, :], cond, 0.0)
        for i in range(8)
    ]
    prior = [prt[r, :] for r in at]
    if half == 0:
        bal.append(jnp.broadcast_to(cond * br_ref[...], (extra, BALANCE)))
        prior.append(jnp.zeros((extra, 128), BF16))
    th, tl = split2(jnp.concatenate([st, jnp.concatenate(bal, axis=0)], axis=1))
    lhs = jnp.concatenate([th, tl, th, jnp.concatenate(prior, axis=0)], axis=1)
    if half == 0:
        lhs = jnp.concatenate([lhs[256:, :], lhs[:256, :]], axis=0)
    for j0 in range(0, 8, 2):
        cols = slice(128 * j0, 128 * j0 + 256)
        wide = dot(lhs[0 : extra + 32 * (j0 + 2), :], sr[:, cols])
        if half == 0:
            mom = wide[0:1, :] + mrow[:, cols]
            for a in range(4):
                out[a, HEAD, j0 : j0 + 1, :] = mom[:, 0:128]
                out[a, HEAD, j0 + 1 : j0 + 2, :] = mom[:, 128:256]
            wide = wide[extra:, :]
        for j in (j0, j0 + 1):
            for i in range(j + 1):
                blk = wide[32 * i : 32 * i + 32, 128 * (j - j0) : 128 * (j - j0) + 128]
                at = FIRST[i] + j - i
                out[:, at + (1 if half == 0 and at >= HEAD else 0)] = blk.reshape(4, 8, 128)


def lane_bc(x, lane):
    return jnp.broadcast_to(x[:, lane : lane + 1], (8, 128))


def row_bc(x, row):
    return jnp.broadcast_to(x[row : row + 1, :], (8, 128))


NEAR = 7


def factor_block(ds, rd, lt, beside):
    lane = lax.broadcasted_iota(jnp.int32, (8, 128), 1)
    sub = lax.broadcasted_iota(jnp.int32, (8, 128), 0)
    t = [ds[8 * j : 8 * j + 8, :] for j in range(16)]
    c = [lane_bc(t[0], q) for q in range(8)]
    for g in range(16):
        r0 = 8 * g
        own = (lane >= r0) & (lane < r0 + 8)
        near = range(g + 1, min(16, g + 1 + NEAR))
        far = range(g + 1 + NEAR, 16)
        b = {j: [lane_bc(t[j], r0 + q) for q in range(8)] for j in near}
        if g < 15:
            nc = [lane_bc(t[g + 1], r0 + 8 + q) for q in range(8)]
        p = jnp.where(own, jnp.where(lane - r0 == sub, 1.0, 0.0), t[g])
        raw = split2(jnp.concatenate([t[j] for j in far], axis=0)) if far else None
        for j in range(g + 1, 16):
            t[j] = jnp.where(own, 0.0, t[j])
        w, mults, invs = [], [], []
        low = jnp.zeros((8, 128), F32)
        for s in range(8):
            inv = lax.rsqrt(row_bc(c[s], s))
            col = c[s] * inv
            mult = {q: row_bc(col, q) for q in range(s + 1, 8)}
            for q in range(s + 1, 8):
                c[q] = c[q] - col * mult[q]
            ws = row_bc(p, s) * inv
            if s < 7:
                p = p - col * ws
            low = jnp.where(lane == r0 + s, col, low)
            for j in near:
                m = b[j][s] * inv
                for q in range(s + 1, 8):
                    b[j][q] = b[j][q] - m * mult[q]
                t[j] = t[j] - m * ws
                if j == g + 1:
                    for q in range(8):
                        nc[q] = nc[q] - m * row_bc(m, q)
            w.append(ws)
            mults.append(mult)
            invs.append(inv)
        full = w[0]
        for s in range(1, 8):
            full = jnp.where(sub == s, w[s], full)
        if far:
            y = [None] * 8
            for s in range(7, -1, -1):
                v = w[s]
                for q in range(7, s, -1):
                    v = v - mults[s][q] * y[q]
                y[s] = v * invs[s]
            yy = y[0]
            for s in range(1, 8):
                yy = jnp.where(sub == s, y[s], yy)
            pad = lambda v: jnp.concatenate(
                ([jnp.zeros((r0, 128), F32)] if r0 else []) + [v, jnp.zeros((120 - r0, 128), F32)], axis=0
            ).astype(BF16)
            yh = yy.astype(BF16).astype(F32)
            yhp, ylp = pad(yh), pad(yy - yh)
            upd = dot(jnp.concatenate(raw, axis=1), jnp.concatenate([yhp, yhp], axis=0)) + dot(raw[0], ylp)
            for n, j in enumerate(far):
                t[j] = t[j] - upd[8 * n : 8 * n + 8, :]
        rd[r0 : r0 + 8, :] = jnp.where(lane >= r0 + 8, full, 0.0)
        ds[r0 : r0 + 8, :] = jnp.where(lane < r0 + 8, full, 0.0)
        lt[r0 : r0 + 8, :] = low
        if g < 15:
            c = nc
        for step in beside[g]:
            step()
    rd[...] = rd[...] + jnp.transpose(lt[...])


LATE = 86
N_COPIES = LATE + 20


def kernel(
    w_in, st_in, co_in, rd_in, en_in, cd_in, br_in, pr_in, pi_in, t_in, o_ref,
    w_ref, st_ref, co_ref, rd_ref, en_ref, cd_ref, br_ref, pr_ref, pi_ref, t_s,
    wcat, hcat, sr, prt, mrow, p0, p1, r1, q, r2, zs, r3, b4, g,
    a_s, ds, rd, lt, dh_s, dl_s, gh_s, gl_s, rp_s, rt_s, rh_s, rl_s, th_s, tl_s, zv, in_sem, s_sem, r_sem,
):
    row = lax.axis_index("rows")
    core = lax.axis_index("cols")
    x, y, z = row // (NY * NZ), (row // NZ) % NY, row % NZ

    pairs = [
        (st_in, st_ref), (co_in, co_ref), (en_in, en_ref), (cd_in, cd_ref), (br_in, br_ref),
        (pr_in, pr_ref), (pi_in, pi_ref), (rd_in, rd_ref), (w_in, w_ref), (t_in, t_s),
    ]
    loads = [pltpu.make_async_copy(src, dst, in_sem.at[n]) for n, (src, dst) in enumerate(pairs)]
    for cp in loads:
        cp.start()

    def at_x(v):
        return ((v * NY + y) * NZ + z, core)

    def at_y(v):
        return ((x * NY + v) * NZ + z, core)

    def at_z(v):
        return ((x * NY + y) * NZ + v, core)

    sibling = (row, 1 - core)
    hop = lambda v, d, n: lax.rem(v + d, n)
    xs = [hop(x, d, NX) for d in range(1, 4)]
    ys = [hop(y, d, NY) for d in range(1, 4)]
    zz = [hop(z, d, NZ) for d in range(1, 8)]
    barrier = pltpu.get_barrier_semaphore()
    friends = [at_x(v) for v in xs] + [at_y(v) for v in ys] + [at_z(v) for v in zz] + [sibling]
    for to in friends:
        pl.semaphore_signal(barrier, inc=1, device_id=to, device_id_type=MESH)

    copies = []

    def remote(n, src, dst, to):
        return pltpu.make_async_remote_copy(
            src_ref=src, dst_ref=dst, send_sem=s_sem.at[n], recv_sem=r_sem.at[n], device_id=to, device_id_type=MESH
        )

    def send(src, dst, to):
        cp = remote(len(copies), src, dst, to)
        cp.start()
        copies.append(cp)
        return cp

    def arrive(these):
        for cp in these:
            cp.wait_recv()

    for cp in loads[:-1]:
        cp.wait()
    build_rows(w_ref, st_ref, co_ref, en_ref, cd_ref, pr_ref, pi_ref, wcat, hcat, sr, prt, mrow)
    me = [(x, y), (y, x)]
    peers = [(xs, ys), (ys, xs)]
    place = [(at_x, at_y), (at_y, at_x)]

    def first_out(c, h):
        p = (p0, p1)[h]
        n = r1[c][h].shape[1]
        start = c * (p.shape[1] - REST)
        own = me[h][0]
        out = [send(p.at[v, pl.ds(start, n)], r1[c][h].at[own], place[h][0](v)) for v in peers[h][0]]
        r1[c][h][own] = p[own, start : start + n]
        return out

    def second_out(c, h):
        size = (HEAD, REST)[c] // 4
        got = r1[c][h]
        for b in range(4):
            t = slice(size * b, size * b + size)
            q[c][h][b, 0:size] = (got[0, t] + got[1, t]) + (got[2, t] + got[3, t])
            if c == 0 and h == 0:
                q[c][h][b, size] = (got[0, HEAD] + got[1, HEAD]) + (got[2, HEAD] + got[3, HEAD])
        own = me[h][1]
        out = [send(q[c][h].at[v], r2[c][h].at[own], place[h][1](v)) for v in peers[h][1]]
        r2[c][h][own] = q[c][h][own]
        return out

    def z_out(c):
        a0, a1 = [(r2[c][h][0] + r2[c][h][1]) + (r2[c][h][2] + r2[c][h][3]) for h in range(2)]
        if c == 0:
            for n in range(4):
                zs[0][n, 0] = a0[n]
                zs[0][4 + n, 0] = a1[n]
            for n in range(8):
                zs[0][n, 1] = a0[4]
        else:
            for n in range(5):
                zs[1][n // 2, n % 2] = a0[n]
                zs[1][(5 + n) // 2, (5 + n) % 2] = a1[n]
            for n in range(5, 8):
                zs[1][n] = jnp.zeros((2, 8, 128), F32)
        out = [send(zs[c].at[v], r3[c].at[z], at_z(v)) for v in zz]
        r3[c][z] = zs[c][z]
        return out

    def z_back(c):
        total = [r3[c][n] for n in range(8)]
        total = ((total[0] + total[1]) + (total[2] + total[3])) + ((total[4] + total[5]) + (total[6] + total[7]))
        size = 1 + c
        b4[c][z] = total[0:size]
        out = [send(b4[c].at[z], b4[c].at[z], at_z(v)) for v in zz]
        return out, total[1]

    def second_back(c):
        size = (HEAD, REST)[c] // 4
        out = []
        for h in range(2):
            begin = c * HEAD + size * me[h][1]
            for n in range(size):
                at = size * h + n
                g[core, h, me[h][0], begin + n] = b4[c][at // (1 + c), at % (1 + c)]
            mine = g.at[core, h, me[h][0], pl.ds(begin, size)]
            out.append([send(mine, mine, place[h][1](v)) for v in peers[h][1]])
        return out

    build_gram(core, 0, rd_ref, br_ref, en_ref, cd_ref, wcat, hcat, sr, prt, mrow, p0)
    pl.semaphore_wait(barrier, len(friends))
    one0 = [first_out(0, 0)]
    build_gram(core, 1, rd_ref, br_ref, en_ref, cd_ref, wcat, hcat, sr, prt, mrow, p1)
    one0.append(first_out(0, 1))
    one1 = [first_out(1, 0), first_out(1, 1)]
    for i in range(1, 8):
        a_s[i, :, :, 0:1024] = jnp.zeros((16, 8, 1024), F32)
    a_s[8] = jnp.zeros((16, 8, 1152), F32)
    dh_s[8] = jnp.zeros((128, 128), BF16)
    dl_s[8] = jnp.zeros((128, 128), BF16)
    loads[-1].wait()
    th_s[...], tl_s[...] = split2(t_s[...])
    two0, two1 = [], []
    for h in range(2):
        arrive(one0[h])
        two0.append(second_out(0, h))
    for h in range(2):
        arrive(one1[h])
        two1.append(second_out(1, h))
    arrive(two0[0] + two0[1])
    z0 = z_out(0)
    arrive(two1[0] + two1[1])
    z1 = z_out(1)
    arrive(z0)
    back0, moment = z_back(0)
    for i in range(8):
        a_s[i, :, :, 1024:] = spread(moment[i : i + 1, :]).reshape(16, 8, 128)
    arrive(z1)
    back1, _ = z_back(1)
    arrive(back0)
    two0 = second_back(0)
    arrive(back1)
    two1 = second_back(1)
    top, own = [], []
    for h in range(2):
        arrive(two0[h])
        mine = g.at[core, h, me[h][0], pl.ds(0, 8)]
        top.append([send(mine, mine, place[h][0](v)) for v in peers[h][0]])
        own.append(send(mine, mine, sibling))
    row1, row1_own = [], []
    for h in range(2):
        mine = g.at[core, h, me[h][0], pl.ds(8, 8)]
        row1.append([send(mine, mine, place[h][0](v)) for v in peers[h][0]])
        row1_own.append(send(mine, mine, sibling))
    for d in range(3):
        for h in range(2):
            top[h][d].wait_recv()
            size = (NX, NY)[h]
            got = g.at[core, h, hop(me[h][0], size - 1 - d, size), pl.ds(0, 8)]
            own.append(send(got, got, sibling))
    arrive(own)
    assert len(copies) == LATE
    for j in range(8):
        for c in range(2):
            for h in range(2):
                a_s[0, 8 * c + 4 * h : 8 * c + 4 * h + 4, :, 128 * j : 128 * j + 128] = g[c, h, :, j]

    def relay(c, d, h):
        size = (NX, NY)[h]
        part = pl.ds(8, 8) if c == 0 else pl.ds(HEAD, REST)
        got = g.at[core, h, hop(me[h][0], size - 1 - d, size), part]
        return remote(LATE + 6 * c + 2 * d + h, got, got, sibling)

    def rest_out(d, h):
        mine = g.at[core, h, me[h][0], pl.ds(HEAD, REST)]
        if d == 3:
            return remote(LATE + 18 + h, mine, mine, sibling)
        return remote(LATE + 12 + 2 * d + h, mine, mine, place[h][0](peers[h][0][d]))

    halves = [(d, h) for d in range(3) for h in range(2)]

    def add_rows(tiles):
        for i, j in tiles:
            cols = slice(128 * j, 128 * j + 128)
            for c in range(2):
                for h in range(2):
                    at = slice(8 * c + 4 * h, 8 * c + 4 * h + 4)
                    a_s[i, at, :, cols] = a_s[i, at, :, cols] + g[c, h, :, FIRST[i] + j - i]

    def add_diagonal(i):
        for c in range(2):
            for h in range(2):
                at = slice(64 * c + 32 * h, 64 * c + 32 * h + 32)
                ds[at, :] = ds[at, :] + g[c, h, :, FIRST[i]].reshape(32, 128)

    def panel(k, _):
        @pl.when(k == 1)
        def _():
            arrive(row1_own + [relay(0, d, h) for d, h in halves])
            add_rows([(1, j) for j in range(2, 8)])
            add_diagonal(1)

        @pl.when(k == 2)
        def _():
            arrive([rest_out(3, 0), rest_out(3, 1)] + [relay(1, d, h) for d, h in halves])
            add_rows([(i, j) for i in range(2, 8) for j in range(i, 8) if j > 2])
            add_diagonal(2)

        prev = jnp.where(k == 0, 8, k - 1)
        dcat = jnp.concatenate([dh_s[prev], dl_s[prev], dh_s[prev]], axis=1)

        def product(j):
            def step():
                cols = slice(128 * j, 128 * j + 256)
                ah, al = split2(a_s[prev, :, :, cols].reshape(128, 256))
                r = dot(dcat, jnp.concatenate([ah, ah, al], axis=0))
                a_s[prev, :, :, cols] = r.reshape(16, 8, 256)
                rh, rl = split2(r)
                rp_s[0:128, cols] = rh
                rp_s[128:256, cols] = rh
                rp_s[256:384, cols] = rl
                rh_s[prev, :, cols] = rh
                rl_s[prev, :, cols] = rl
                for i in range(j, min(j + 2, 8)):
                    th, tl = split2(jnp.transpose(r[:, 128 * (i - j) : 128 * (i - j) + 128]))
                    rt_s[i] = jnp.concatenate([th, tl, th], axis=1)

            return step

        def couple():
            by = dot(rt_s[k], jnp.concatenate([dh_s[prev], dh_s[prev], dl_s[prev]], axis=0))
            gh_s[prev], gl_s[prev] = split2(by)

        def update(i, j):
            def step():
                end = min(j + 2, 9)
                cols = slice(128 * j, 128 * end)
                to = jnp.where(i >= k, i, 8)
                upd = dot(rt_s[i], rp_s[:, cols])
                a_s[to, :, :, cols] = a_s[to, :, :, cols] - upd.reshape(16, 8, 128 * (end - j))

            return step

        steps = [product(j) for j in range(1, 9, 2)]
        steps.append(couple)
        steps += [update(i, j) for i in range(1, 8) for j in range(i, 9, 2)]
        factor_block(ds, rd.at[k], lt, [steps[2 * n : 2 * n + 2] for n in range(16)])

        @pl.when(k == 0)
        def _():
            for d, h in halves:
                row1[h][d].wait_recv()
                relay(0, d, h).start()
            for h in range(2):
                arrive(two1[h])
                for d in range(4):
                    rest_out(d, h).start()

        @pl.when(k == 1)
        def _():
            for d, h in halves:
                rest_out(d, h).wait_recv()
                relay(1, d, h).start()

        d = split2(ds[...])
        dh_s[k], dl_s[k] = d
        nxt = pl.ds(pl.multiple_of(128 * k + 128, 128), 128)
        c = dot3(d, split2(a_s[k, :, :, nxt].reshape(128, 128)))
        ds[...] = a_s[k + 1, :, :, nxt].reshape(128, 128) - dot3(split2(jnp.transpose(c)), split2(c))
        return 0

    ds[...] = a_s[0, :, :, 0:128].reshape(128, 128)
    lax.fori_loop(0, 8, panel, 0)

    z7 = dot3((dh_s[7], dl_s[7]), split2(a_s[7, :, :, 1024:].reshape(128, 128)))
    v = [jnp.transpose(a_s[i, :, :, 1024:].reshape(128, 128))[0:8, :] for i in range(7)] + [jnp.transpose(z7)[0:8, :]]
    for i in range(8):
        zv[i : i + 1, :] = v[i][0:1, :]
    nxt = jnp.zeros((8, 512), F32)
    ek = None
    for k in range(7, -1, -1):
        e = rows_dot(stack2(v[k]), dh_s[k], dl_s[k])
        if k < 7:
            e = e - rows_dot(ek, gh_s[k], gl_s[k])
        ek = stack2(e)
        at = slice(128 * k, 128 * k + 128)
        for p in range(k - 2, -1, -1):
            v[p] = v[p] - rows_dot(ek, rh_s[p, :, at], rl_s[p, :, at], NT)
        nxt = nxt + rows_dot(ek, th_s[:, at], tl_s[:, at], NT)
    for q in range(4):
        o_ref[8:9, 128 * q : 128 * q + 128] = zv[pl.ds(core * 4 + q, 1), :]
    o_ref[9:10, :] = nxt[0:1, :]
    o_ref[10:16, :] = jnp.zeros((6, 512), F32)
    mine = row // 16
    a_s[mine, :, :, pl.ds(pl.multiple_of(128 * mine, 128), 128)] = rd[mine].reshape(16, 8, 128)
    mine = a_s[row // 16, row % 16, :, pl.ds(pl.multiple_of(core * 512, 512), 512)]
    at_row = row * 8 + lax.broadcasted_iota(jnp.int32, (8, 512), 0)
    at_col = core * 512 + lax.broadcasted_iota(jnp.int32, (8, 512), 1)
    o_ref[0:8, :] = jnp.where(at_col >= at_row, mine, 0.0)
    for cp in copies + [relay(c, d, h) for c in range(2) for d, h in halves]:
        cp.wait_send()
    for d in range(4):
        for h in range(2):
            rest_out(d, h).wait_send()


def hand_out(all_ref, r_ref, z_ref, x_ref):
    r_ref[...] = all_ref[0:8, :]
    z_ref[...] = all_ref[8:9, :]
    x_ref[...] = all_ref[9:10, :]


def per_device(
    whitening,
    sensor_states,
    sensor_coefficients,
    sensor_readings,
    conduit_endpoints,
    conductance,
    balance_right_side,
    prior_root_factor,
    prior_information,
    transition,
):
    args = (
        whitening,
        sensor_states.T,
        sensor_coefficients.T,
        sensor_readings.reshape(3, 128),
        conduit_endpoints.T,
        conductance.reshape(1, BALANCE),
        balance_right_side.reshape(1, BALANCE),
        prior_root_factor,
        prior_information.reshape(1, 8),
        transition,
    )
    vmem = pl.BlockSpec(memory_space=pltpu.VMEM)
    tiles = lambda *lead: pltpu.VMEM(lead + (8, 128), F32)
    results = pl.pallas_call(
        kernel,
        out_shape=jax.ShapeDtypeStruct((16, 512), F32),
        in_specs=[pl.BlockSpec(memory_space=pl.ANY)] * len(args),
        out_specs=vmem,
        scratch_shapes=[pltpu.VMEM(arg.shape, arg.dtype) for arg in args]
        + [
            pltpu.VMEM((SENSORS, 3 * SENSORS), BF16),
            pltpu.VMEM((1024, 3 * SENSORS), BF16),
            pltpu.VMEM((DEPTH, 1024), BF16),
            pltpu.VMEM((1024, 128), BF16),
            pltpu.VMEM((1, 1024), F32),
            tiles(4, 37),
            tiles(4, 36),
            [[tiles(4, 17), tiles(4, 16)], [tiles(4, 20), tiles(4, 20)]],
            [[tiles(4, 5), tiles(4, 4)], [tiles(4, 5), tiles(4, 5)]],
            [[tiles(4, 5), tiles(4, 4)], [tiles(4, 5), tiles(4, 5)]],
            [tiles(8, 2), tiles(8, 2)],
            [tiles(8, 2), tiles(8, 2)],
            [tiles(8, 1), tiles(8, 2)],
            tiles(2, 2, 4, 36),
            pltpu.VMEM((9, 16, 8, 1152), F32),
            pltpu.VMEM((128, 128), F32),
            pltpu.VMEM((8, 128, 128), F32),
            pltpu.VMEM((128, 128), F32),
            pltpu.VMEM((9, 128, 128), BF16),
            pltpu.VMEM((9, 128, 128), BF16),
            pltpu.VMEM((9, 128, 128), BF16),
            pltpu.VMEM((9, 128, 128), BF16),
            pltpu.VMEM((384, 1152), BF16),
            pltpu.VMEM((8, 128, 384), BF16),
            pltpu.VMEM((9, 128, 1152), BF16),
            pltpu.VMEM((9, 128, 1152), BF16),
            pltpu.VMEM((512, 1024), BF16),
            pltpu.VMEM((512, 1024), BF16),
            pltpu.VMEM((8, 128), F32),
            pltpu.SemaphoreType.DMA((10,)),
            pltpu.SemaphoreType.DMA((N_COPIES,)),
            pltpu.SemaphoreType.DMA((N_COPIES,)),
        ],
        compiler_params=pltpu.CompilerParams(
            collective_id=0, has_side_effects=True, vmem_limit_bytes=62 * 1024 * 1024
        ),
    )(*args)
    r_post, z_post, x_next = pl.pallas_call(
        hand_out,
        out_shape=(
            jax.ShapeDtypeStruct((8, 512), F32),
            jax.ShapeDtypeStruct((1, 512), F32),
            jax.ShapeDtypeStruct((1, 512), F32),
        ),
        in_specs=[vmem],
        out_specs=(vmem, vmem, vmem),
        compiler_params=pltpu.CompilerParams(vmem_limit_bytes=62 * 1024 * 1024),
    )(results)
    return r_post, z_post.reshape(512), x_next.reshape(512)


def solution(mesh):
    in_specs = (
        P("rows", None),
        P("rows", None),
        P("rows", None),
        P("rows"),
        P("rows", None),
        P("rows"),
        P("rows"),
        P("rows", None),
        P("rows"),
        P("cols", None),
    )
    out_specs = (P("rows", "cols"), P("cols"), P("cols"))
    return jax.shard_map(
        per_device, mesh=mesh, in_specs=in_specs, out_specs=out_specs, check_vma=False
    )
```

```python
import jax
import jax.numpy as jnp
from jax import lax
from jax.experimental import pallas as pl
from jax.experimental.pallas import tpu as pltpu
from jax.sharding import PartitionSpec as P

F32, BF16 = jnp.float32, jnp.bfloat16
MESH = pl.DeviceIdType.MESH
NX, NY, NZ = 4, 4, 8
SENSORS, BALANCE = 384, 128
DEPTH = 3 * (SENSORS + BALANCE) + 128
FIRST = [0, 8, 15, 21, 26, 30, 33, 35, 36]
HEAD, REST = 16, 20
NN = (((1,), (0,)), ((), ()))
NT = (((1,), (1,)), ((), ()))
TN = (((0,), (0,)), ((), ()))


def dot(a, b, dims=NN):
    return lax.dot_general(a, b, dims, preferred_element_type=F32)


def split2(x):
    hi = x.astype(BF16)
    return hi, (x - hi.astype(F32)).astype(BF16)


def split3(x):
    hi = x.astype(BF16)
    rest = x - hi.astype(F32)
    mid = rest.astype(BF16)
    return hi, mid, (rest - mid.astype(F32)).astype(BF16)


def dot3(a, b, dims=NN):
    return dot(a[0], b[0], dims) + (dot(a[0], b[1], dims) + dot(a[1], b[0], dims))


def stack2(x):
    return jnp.concatenate(split2(x), axis=0)


def rows_dot(x, hi, lo, dims=NN):
    both = dot(x, hi, dims) + dot(x, lo, dims)
    return both[0:8, :] + both[8:16, :]


def spread(row):
    return jnp.transpose(jnp.broadcast_to(row, (128, 128)))


def build_rows(w_ref, st_ref, co_ref, en_ref, cd_ref, pr_ref, pi_ref, wcat, hcat, sr, prt, mrow):
    w = split2(w_ref[...])
    wcat[...] = jnp.concatenate([w[0], w[1], w[0]], axis=1)
    cond_row = cd_ref[...]
    cond = spread(cond_row)
    ends = [spread(en_ref[k : k + 1, :].astype(F32)).astype(jnp.int32) for k in range(2)]
    info = spread(jnp.concatenate([pi_ref[...], jnp.zeros((1, 120), F32)], axis=1))[0:8, :]
    twice = lambda v: jnp.concatenate([v, v], axis=1)
    cond, info, ends = twice(cond), twice(info), [twice(v) for v in ends]
    for j in range(0, 8, 2):
        cols = slice(128 * j, 128 * j + 256)
        ids = 128 * j + lax.broadcasted_iota(jnp.int32, (256, SENSORS), 0)
        h = jnp.zeros((256, SENSORS), F32)
        for k in range(4):
            h = h + jnp.where(ids == st_ref[k : k + 1, :], co_ref[k : k + 1, :], 0.0)
        hh, hl = split2(h)
        hj = jnp.concatenate([hh, hh, hl], axis=1)
        hcat[cols, :] = hj
        s = dot(wcat[...], hj, NT)
        bids = 128 * j + lax.broadcasted_iota(jnp.int32, (BALANCE, 256), 1)
        bal = jnp.where(bids == ends[0], cond, 0.0) - jnp.where(bids == ends[1], cond, 0.0)
        fh, fl = split2(jnp.concatenate([s, bal], axis=0))
        sr[0:512, cols] = fh
        sr[512:1024, cols] = fh
        sr[1024:1536, cols] = fl
        prior = pr_ref[:, cols]
        ph, pm, pl_ = [part.astype(F32) for part in split3(prior)]
        none = jnp.zeros((80, 256), F32)
        sr[1536:1664, cols] = jnp.concatenate([ph, pm, ph, pl_, ph, pm, none], axis=0).astype(BF16)
        packed = jnp.concatenate([ph, ph, pm, ph, pl_, pm, none], axis=0)
        for n in range(2):
            half = packed[:, 128 * n : 128 * n + 128]
            prt[128 * (j + n) : 128 * (j + n) + 128, :] = jnp.transpose(half).astype(BF16)
        mrow[:, cols] = jnp.sum(prior * info, axis=0, keepdims=True)


def build_gram(core, half, rd_ref, br_ref, en_ref, cd_ref, wcat, hcat, sr, prt, mrow, out):
    at = [pl.ds(pl.multiple_of(128 * i + 64 * core + 32 * half, 32), 32) for i in range(8)]
    extra = 16 if half == 0 else 0
    rows = [hcat[r, :] for r in at]
    if half == 0:
        readings = jnp.concatenate([rd_ref[k : k + 1, :] for k in range(3)], axis=1)
        rh, rl = split2(jnp.broadcast_to(readings, (extra, SENSORS)))
        rows.append(jnp.concatenate([rh, rh, rl], axis=1))
    st = dot(jnp.concatenate(rows, axis=0), wcat[...], NT)
    ids = lax.broadcasted_iota(jnp.int32, (32, BALANCE), 0) + (64 * core + 32 * half)
    cond = cd_ref[...]
    bal = [
        jnp.where(ids + 128 * i == en_ref[0:1, :], cond, 0.0) - jnp.where(ids + 128 * i == en_ref[1:2, :], cond, 0.0)
        for i in range(8)
    ]
    prior = [prt[r, :] for r in at]
    if half == 0:
        bal.append(jnp.broadcast_to(cond * br_ref[...], (extra, BALANCE)))
        prior.append(jnp.zeros((extra, 128), BF16))
    th, tl = split2(jnp.concatenate([st, jnp.concatenate(bal, axis=0)], axis=1))
    lhs = jnp.concatenate([th, tl, th, jnp.concatenate(prior, axis=0)], axis=1)
    if half == 0:
        lhs = jnp.concatenate([lhs[256:, :], lhs[:256, :]], axis=0)
    for j0 in range(0, 8, 2):
        cols = slice(128 * j0, 128 * j0 + 256)
        wide = dot(lhs[0 : extra + 32 * (j0 + 2), :], sr[:, cols])
        if half == 0:
            mom = wide[0:1, :] + mrow[:, cols]
            for a in range(4):
                out[a, HEAD, j0 : j0 + 1, :] = mom[:, 0:128]
                out[a, HEAD, j0 + 1 : j0 + 2, :] = mom[:, 128:256]
            wide = wide[extra:, :]
        for j in (j0, j0 + 1):
            for i in range(j + 1):
                blk = wide[32 * i : 32 * i + 32, 128 * (j - j0) : 128 * (j - j0) + 128]
                at = FIRST[i] + j - i
                out[:, at + (1 if half == 0 and at >= HEAD else 0)] = blk.reshape(4, 8, 128)


def lane_bc(x, lane):
    return jnp.broadcast_to(x[:, lane : lane + 1], (8, 128))


def row_bc(x, row):
    return jnp.broadcast_to(x[row : row + 1, :], (8, 128))


NEAR = 7


def factor_block(ds, rd, lt, beside):
    lane = lax.broadcasted_iota(jnp.int32, (8, 128), 1)
    sub = lax.broadcasted_iota(jnp.int32, (8, 128), 0)
    t = [ds[8 * j : 8 * j + 8, :] for j in range(16)]
    c = [lane_bc(t[0], q) for q in range(8)]
    for g in range(16):
        r0 = 8 * g
        own = (lane >= r0) & (lane < r0 + 8)
        near = range(g + 1, min(16, g + 1 + NEAR))
        far = range(g + 1 + NEAR, 16)
        b = {j: [lane_bc(t[j], r0 + q) for q in range(8)] for j in near}
        if g < 15:
            nc = [lane_bc(t[g + 1], r0 + 8 + q) for q in range(8)]
        p = jnp.where(own, jnp.where(lane - r0 == sub, 1.0, 0.0), t[g])
        raw = split2(jnp.concatenate([t[j] for j in far], axis=0)) if far else None
        for j in range(g + 1, 16):
            t[j] = jnp.where(own, 0.0, t[j])
        w, mults, invs = [], [], []
        low = jnp.zeros((8, 128), F32)
        for s in range(8):
            inv = lax.rsqrt(row_bc(c[s], s))
            col = c[s] * inv
            mult = {q: row_bc(col, q) for q in range(s + 1, 8)}
            for q in range(s + 1, 8):
                c[q] = c[q] - col * mult[q]
            ws = row_bc(p, s) * inv
            if s < 7:
                p = p - col * ws
            low = jnp.where(lane == r0 + s, col, low)
            for j in near:
                m = b[j][s] * inv
                for q in range(s + 1, 8):
                    b[j][q] = b[j][q] - m * mult[q]
                t[j] = t[j] - m * ws
                if j == g + 1:
                    for q in range(8):
                        nc[q] = nc[q] - m * row_bc(m, q)
            w.append(ws)
            mults.append(mult)
            invs.append(inv)
        full = w[0]
        for s in range(1, 8):
            full = jnp.where(sub == s, w[s], full)
        if far:
            y = [None] * 8
            for s in range(7, -1, -1):
                v = w[s]
                for q in range(7, s, -1):
                    v = v - mults[s][q] * y[q]
                y[s] = v * invs[s]
            yy = y[0]
            for s in range(1, 8):
                yy = jnp.where(sub == s, y[s], yy)
            pad = lambda v: jnp.concatenate(
                ([jnp.zeros((r0, 128), F32)] if r0 else []) + [v, jnp.zeros((120 - r0, 128), F32)], axis=0
            ).astype(BF16)
            yh = yy.astype(BF16).astype(F32)
            yhp, ylp = pad(yh), pad(yy - yh)
            upd = dot(jnp.concatenate(raw, axis=1), jnp.concatenate([yhp, yhp], axis=0)) + dot(raw[0], ylp)
            for n, j in enumerate(far):
                t[j] = t[j] - upd[8 * n : 8 * n + 8, :]
        rd[r0 : r0 + 8, :] = jnp.where(lane >= r0 + 8, full, 0.0)
        ds[r0 : r0 + 8, :] = jnp.where(lane < r0 + 8, full, 0.0)
        lt[r0 : r0 + 8, :] = low
        if g < 15:
            c = nc
        for step in beside[g]:
            step()
    rd[...] = rd[...] + jnp.transpose(lt[...])


LATE = 86
N_COPIES = LATE + 20


def kernel(
    w_in, st_in, co_in, rd_in, en_in, cd_in, br_in, pr_in, pi_in, t_in, o_ref,
    w_ref, st_ref, co_ref, rd_ref, en_ref, cd_ref, br_ref, pr_ref, pi_ref, t_s,
    wcat, hcat, sr, prt, mrow, p0, p1, r1, q, r2, zs, r3, b4, g,
    a_s, ds, rd, lt, dh_s, dl_s, gh_s, gl_s, rp_s, rt_s, rh_s, rl_s, th_s, tl_s, zv, in_sem, s_sem, r_sem,
):
    row = lax.axis_index("rows")
    core = lax.axis_index("cols")
    x, y, z = row // (NY * NZ), (row // NZ) % NY, row % NZ

    pairs = [
        (st_in, st_ref), (co_in, co_ref), (en_in, en_ref), (cd_in, cd_ref), (br_in, br_ref),
        (pr_in, pr_ref), (pi_in, pi_ref), (rd_in, rd_ref), (w_in, w_ref), (t_in, t_s),
    ]
    loads = [pltpu.make_async_copy(src, dst, in_sem.at[n]) for n, (src, dst) in enumerate(pairs)]
    for cp in loads:
        cp.start()

    def at_x(v):
        return ((v * NY + y) * NZ + z, core)

    def at_y(v):
        return ((x * NY + v) * NZ + z, core)

    def at_z(v):
        return ((x * NY + y) * NZ + v, core)

    sibling = (row, 1 - core)
    hop = lambda v, d, n: lax.rem(v + d, n)
    xs = [hop(x, d, NX) for d in range(1, 4)]
    ys = [hop(y, d, NY) for d in range(1, 4)]
    zz = [hop(z, d, NZ) for d in range(1, 8)]
    barrier = pltpu.get_barrier_semaphore()
    friends = [at_x(v) for v in xs] + [at_y(v) for v in ys] + [at_z(v) for v in zz] + [sibling]
    for to in friends:
        pl.semaphore_signal(barrier, inc=1, device_id=to, device_id_type=MESH)

    copies = []

    def remote(n, src, dst, to):
        return pltpu.make_async_remote_copy(
            src_ref=src, dst_ref=dst, send_sem=s_sem.at[n], recv_sem=r_sem.at[n], device_id=to, device_id_type=MESH
        )

    def send(src, dst, to):
        cp = remote(len(copies), src, dst, to)
        cp.start()
        copies.append(cp)
        return cp

    def arrive(these):
        for cp in these:
            cp.wait_recv()

    for cp in loads[:-1]:
        cp.wait()
    build_rows(w_ref, st_ref, co_ref, en_ref, cd_ref, pr_ref, pi_ref, wcat, hcat, sr, prt, mrow)
    me = [(x, y), (y, x)]
    peers = [(xs, ys), (ys, xs)]
    place = [(at_x, at_y), (at_y, at_x)]

    def first_out(c, h):
        p = (p0, p1)[h]
        n = r1[c][h].shape[1]
        start = c * (p.shape[1] - REST)
        own = me[h][0]
        out = [send(p.at[v, pl.ds(start, n)], r1[c][h].at[own], place[h][0](v)) for v in peers[h][0]]
        r1[c][h][own] = p[own, start : start + n]
        return out

    def second_out(c, h):
        size = (HEAD, REST)[c] // 4
        got = r1[c][h]
        for b in range(4):
            t = slice(size * b, size * b + size)
            q[c][h][b, 0:size] = (got[0, t] + got[1, t]) + (got[2, t] + got[3, t])
            if c == 0 and h == 0:
                q[c][h][b, size] = (got[0, HEAD] + got[1, HEAD]) + (got[2, HEAD] + got[3, HEAD])
        own = me[h][1]
        out = [send(q[c][h].at[v], r2[c][h].at[own], place[h][1](v)) for v in peers[h][1]]
        r2[c][h][own] = q[c][h][own]
        return out

    def z_out(c):
        a0, a1 = [(r2[c][h][0] + r2[c][h][1]) + (r2[c][h][2] + r2[c][h][3]) for h in range(2)]
        if c == 0:
            for n in range(4):
                zs[0][n, 0] = a0[n]
                zs[0][4 + n, 0] = a1[n]
            for n in range(8):
                zs[0][n, 1] = a0[4]
        else:
            for n in range(5):
                zs[1][n // 2, n % 2] = a0[n]
                zs[1][(5 + n) // 2, (5 + n) % 2] = a1[n]
            for n in range(5, 8):
                zs[1][n] = jnp.zeros((2, 8, 128), F32)
        out = [send(zs[c].at[v], r3[c].at[z], at_z(v)) for v in zz]
        r3[c][z] = zs[c][z]
        return out

    def z_back(c):
        total = [r3[c][n] for n in range(8)]
        total = ((total[0] + total[1]) + (total[2] + total[3])) + ((total[4] + total[5]) + (total[6] + total[7]))
        size = 1 + c
        b4[c][z] = total[0:size]
        out = [send(b4[c].at[z], b4[c].at[z], at_z(v)) for v in zz]
        return out, total[1]

    def second_back(c):
        size = (HEAD, REST)[c] // 4
        out = []
        for h in range(2):
            begin = c * HEAD + size * me[h][1]
            for n in range(size):
                at = size * h + n
                g[core, h, me[h][0], begin + n] = b4[c][at // (1 + c), at % (1 + c)]
            mine = g.at[core, h, me[h][0], pl.ds(begin, size)]
            out.append([send(mine, mine, place[h][1](v)) for v in peers[h][1]])
        return out

    build_gram(core, 0, rd_ref, br_ref, en_ref, cd_ref, wcat, hcat, sr, prt, mrow, p0)
    pl.semaphore_wait(barrier, len(friends))
    one0 = [first_out(0, 0)]
    build_gram(core, 1, rd_ref, br_ref, en_ref, cd_ref, wcat, hcat, sr, prt, mrow, p1)
    one0.append(first_out(0, 1))
    one1 = [first_out(1, 0), first_out(1, 1)]
    for i in range(1, 8):
        a_s[i, :, :, 0:1024] = jnp.zeros((16, 8, 1024), F32)
    a_s[8] = jnp.zeros((16, 8, 1152), F32)
    dh_s[8] = jnp.zeros((128, 128), BF16)
    dl_s[8] = jnp.zeros((128, 128), BF16)
    loads[-1].wait()
    th_s[...], tl_s[...] = split2(t_s[...])
    two0, two1 = [], []
    for h in range(2):
        arrive(one0[h])
        two0.append(second_out(0, h))
    for h in range(2):
        arrive(one1[h])
        two1.append(second_out(1, h))
    arrive(two0[0] + two0[1])
    z0 = z_out(0)
    arrive(two1[0] + two1[1])
    z1 = z_out(1)
    arrive(z0)
    back0, moment = z_back(0)
    for i in range(8):
        a_s[i, :, :, 1024:] = spread(moment[i : i + 1, :]).reshape(16, 8, 128)
    arrive(z1)
    back1, _ = z_back(1)
    arrive(back0)
    two0 = second_back(0)
    arrive(back1)
    two1 = second_back(1)
    top, own = [], []
    for h in range(2):
        arrive(two0[h])
        mine = g.at[core, h, me[h][0], pl.ds(0, 8)]
        top.append([send(mine, mine, place[h][0](v)) for v in peers[h][0]])
        own.append(send(mine, mine, sibling))
    row1, row1_own = [], []
    for h in range(2):
        mine = g.at[core, h, me[h][0], pl.ds(8, 8)]
        row1.append([send(mine, mine, place[h][0](v)) for v in peers[h][0]])
        row1_own.append(send(mine, mine, sibling))
    for d in range(3):
        for h in range(2):
            top[h][d].wait_recv()
            size = (NX, NY)[h]
            got = g.at[core, h, hop(me[h][0], size - 1 - d, size), pl.ds(0, 8)]
            own.append(send(got, got, sibling))
    arrive(own)
    assert len(copies) == LATE
    for j in range(8):
        for c in range(2):
            for h in range(2):
                a_s[0, 8 * c + 4 * h : 8 * c + 4 * h + 4, :, 128 * j : 128 * j + 128] = g[c, h, :, j]

    def relay(c, d, h):
        size = (NX, NY)[h]
        part = pl.ds(8, 8) if c == 0 else pl.ds(HEAD, REST)
        got = g.at[core, h, hop(me[h][0], size - 1 - d, size), part]
        return remote(LATE + 6 * c + 2 * d + h, got, got, sibling)

    def rest_out(d, h):
        mine = g.at[core, h, me[h][0], pl.ds(HEAD, REST)]
        if d == 3:
            return remote(LATE + 18 + h, mine, mine, sibling)
        return remote(LATE + 12 + 2 * d + h, mine, mine, place[h][0](peers[h][0][d]))

    halves = [(d, h) for d in range(3) for h in range(2)]

    def add_rows(tiles):
        for i, j in tiles:
            cols = slice(128 * j, 128 * j + 128)
            for c in range(2):
                for h in range(2):
                    at = slice(8 * c + 4 * h, 8 * c + 4 * h + 4)
                    a_s[i, at, :, cols] = a_s[i, at, :, cols] + g[c, h, :, FIRST[i] + j - i]

    def add_diagonal(i):
        for c in range(2):
            for h in range(2):
                at = slice(64 * c + 32 * h, 64 * c + 32 * h + 32)
                ds[at, :] = ds[at, :] + g[c, h, :, FIRST[i]].reshape(32, 128)

    def arrivals(k):
        @pl.when(k == 1)
        def _():
            arrive(row1_own + [relay(0, d, h) for d, h in halves])
            add_rows([(1, j) for j in range(2, 8)])
            add_diagonal(1)

        @pl.when(k == 2)
        def _():
            arrive([rest_out(3, 0), rest_out(3, 1)] + [relay(1, d, h) for d, h in halves])
            add_rows([(i, j) for i in range(2, 8) for j in range(i, 8) if j > 2])
            add_diagonal(2)

    def relays(k):
        @pl.when(k == 0)
        def _():
            for d, h in halves:
                row1[h][d].wait_recv()
                relay(0, d, h).start()
            for h in range(2):
                arrive(two1[h])
                for d in range(4):
                    rest_out(d, h).start()

        @pl.when(k == 1)
        def _():
            for d, h in halves:
                rest_out(d, h).wait_recv()
                relay(1, d, h).start()

    def panel(k, low):
        if low == 1:
            arrivals(k)
        prev = jnp.where(k == 0, 8, k - 1)
        dcat = jnp.concatenate([dh_s[prev], dl_s[prev], dh_s[prev]], axis=1)

        def product(j):
            def step():
                cols = slice(128 * j, 128 * j + 256)
                ah, al = split2(a_s[prev, :, :, cols].reshape(128, 256))
                r = dot(dcat, jnp.concatenate([ah, ah, al], axis=0))
                a_s[prev, :, :, cols] = r.reshape(16, 8, 256)
                rh, rl = split2(r)
                rp_s[0:128, cols] = rh
                rp_s[128:256, cols] = rh
                rp_s[256:384, cols] = rl
                rh_s[prev, :, cols] = rh
                rl_s[prev, :, cols] = rl
                for i in range(j, min(j + 2, 8)):
                    th, tl = split2(jnp.transpose(r[:, 128 * (i - j) : 128 * (i - j) + 128]))
                    rt_s[i] = jnp.concatenate([th, tl, th], axis=1)

            return step

        def couple():
            by = dot(rt_s[k], jnp.concatenate([dh_s[prev], dh_s[prev], dl_s[prev]], axis=0))
            gh_s[prev], gl_s[prev] = split2(by)

        def update(i, j):
            def step():
                end = min(j + 2, 9)
                cols = slice(128 * j, 128 * end)
                to = jnp.where(i >= k, i, 8)
                upd = dot(rt_s[i], rp_s[:, cols])
                a_s[to, :, :, cols] = a_s[to, :, :, cols] - upd.reshape(16, 8, 128 * (end - j))

            return step

        steps = [product(j) for j in range(low - 1 + low % 2, 9, 2)]
        steps.append(couple)
        steps += [update(i, j) for i in range(low, 8) for j in range(i, 9, 2)]
        factor_block(ds, rd.at[k], lt, [steps[2 * n : 2 * n + 2] for n in range(16)])

        if low == 1:
            relays(k)
        d = split2(ds[...])
        dh_s[k], dl_s[k] = d
        nxt = pl.ds(pl.multiple_of(128 * k + 128, 128), 128)
        c = dot3(d, split2(a_s[k, :, :, nxt].reshape(128, 128)))
        ds[...] = a_s[k + 1, :, :, nxt].reshape(128, 128) - dot3(split2(jnp.transpose(c)), split2(c))

    ds[...] = a_s[0, :, :, 0:128].reshape(128, 128)
    for begin, end, low in ((0, 4, 1), (4, 8, 4)):

        def one(k, done, low=low):
            panel(k, low)
            return done

        lax.fori_loop(begin, end, one, 0)

    z7 = dot3((dh_s[7], dl_s[7]), split2(a_s[7, :, :, 1024:].reshape(128, 128)))
    v = [jnp.transpose(a_s[i, :, :, 1024:].reshape(128, 128))[0:8, :] for i in range(7)] + [jnp.transpose(z7)[0:8, :]]
    for i in range(8):
        zv[i : i + 1, :] = v[i][0:1, :]
    nxt = jnp.zeros((8, 512), F32)
    ek = None
    for k in range(7, -1, -1):
        e = rows_dot(stack2(v[k]), dh_s[k], dl_s[k])
        if k < 7:
            e = e - rows_dot(ek, gh_s[k], gl_s[k])
        ek = stack2(e)
        at = slice(128 * k, 128 * k + 128)
        for p in range(k - 2, -1, -1):
            v[p] = v[p] - rows_dot(ek, rh_s[p, :, at], rl_s[p, :, at], NT)
        nxt = nxt + rows_dot(ek, th_s[:, at], tl_s[:, at], NT)
    for q in range(4):
        o_ref[8:9, 128 * q : 128 * q + 128] = zv[pl.ds(core * 4 + q, 1), :]
    o_ref[9:10, :] = nxt[0:1, :]
    o_ref[10:16, :] = jnp.zeros((6, 512), F32)
    mine = row // 16
    a_s[mine, :, :, pl.ds(pl.multiple_of(128 * mine, 128), 128)] = rd[mine].reshape(16, 8, 128)
    mine = a_s[row // 16, row % 16, :, pl.ds(pl.multiple_of(core * 512, 512), 512)]
    at_row = row * 8 + lax.broadcasted_iota(jnp.int32, (8, 512), 0)
    at_col = core * 512 + lax.broadcasted_iota(jnp.int32, (8, 512), 1)
    o_ref[0:8, :] = jnp.where(at_col >= at_row, mine, 0.0)
    for cp in copies + [relay(c, d, h) for c in range(2) for d, h in halves]:
        cp.wait_send()
    for d in range(4):
        for h in range(2):
            rest_out(d, h).wait_send()


def hand_out(all_ref, r_ref, z_ref, x_ref):
    r_ref[...] = all_ref[0:8, :]
    z_ref[...] = all_ref[8:9, :]
    x_ref[...] = all_ref[9:10, :]


def per_device(
    whitening,
    sensor_states,
    sensor_coefficients,
    sensor_readings,
    conduit_endpoints,
    conductance,
    balance_right_side,
    prior_root_factor,
    prior_information,
    transition,
):
    args = (
        whitening,
        sensor_states.T,
        sensor_coefficients.T,
        sensor_readings.reshape(3, 128),
        conduit_endpoints.T,
        conductance.reshape(1, BALANCE),
        balance_right_side.reshape(1, BALANCE),
        prior_root_factor,
        prior_information.reshape(1, 8),
        transition,
    )
    vmem = pl.BlockSpec(memory_space=pltpu.VMEM)
    tiles = lambda *lead: pltpu.VMEM(lead + (8, 128), F32)
    results = pl.pallas_call(
        kernel,
        out_shape=jax.ShapeDtypeStruct((16, 512), F32),
        in_specs=[pl.BlockSpec(memory_space=pl.ANY)] * len(args),
        out_specs=vmem,
        scratch_shapes=[pltpu.VMEM(arg.shape, arg.dtype) for arg in args]
        + [
            pltpu.VMEM((SENSORS, 3 * SENSORS), BF16),
            pltpu.VMEM((1024, 3 * SENSORS), BF16),
            pltpu.VMEM((DEPTH, 1024), BF16),
            pltpu.VMEM((1024, 128), BF16),
            pltpu.VMEM((1, 1024), F32),
            tiles(4, 37),
            tiles(4, 36),
            [[tiles(4, 17), tiles(4, 16)], [tiles(4, 20), tiles(4, 20)]],
            [[tiles(4, 5), tiles(4, 4)], [tiles(4, 5), tiles(4, 5)]],
            [[tiles(4, 5), tiles(4, 4)], [tiles(4, 5), tiles(4, 5)]],
            [tiles(8, 2), tiles(8, 2)],
            [tiles(8, 2), tiles(8, 2)],
            [tiles(8, 1), tiles(8, 2)],
            tiles(2, 2, 4, 36),
            pltpu.VMEM((9, 16, 8, 1152), F32),
            pltpu.VMEM((128, 128), F32),
            pltpu.VMEM((8, 128, 128), F32),
            pltpu.VMEM((128, 128), F32),
            pltpu.VMEM((9, 128, 128), BF16),
            pltpu.VMEM((9, 128, 128), BF16),
            pltpu.VMEM((9, 128, 128), BF16),
            pltpu.VMEM((9, 128, 128), BF16),
            pltpu.VMEM((384, 1152), BF16),
            pltpu.VMEM((8, 128, 384), BF16),
            pltpu.VMEM((9, 128, 1152), BF16),
            pltpu.VMEM((9, 128, 1152), BF16),
            pltpu.VMEM((512, 1024), BF16),
            pltpu.VMEM((512, 1024), BF16),
            pltpu.VMEM((8, 128), F32),
            pltpu.SemaphoreType.DMA((10,)),
            pltpu.SemaphoreType.DMA((N_COPIES,)),
            pltpu.SemaphoreType.DMA((N_COPIES,)),
        ],
        compiler_params=pltpu.CompilerParams(
            collective_id=0, has_side_effects=True, vmem_limit_bytes=62 * 1024 * 1024
        ),
    )(*args)
    r_post, z_post, x_next = pl.pallas_call(
        hand_out,
        out_shape=(
            jax.ShapeDtypeStruct((8, 512), F32),
            jax.ShapeDtypeStruct((1, 512), F32),
            jax.ShapeDtypeStruct((1, 512), F32),
        ),
        in_specs=[vmem],
        out_specs=(vmem, vmem, vmem),
        compiler_params=pltpu.CompilerParams(vmem_limit_bytes=62 * 1024 * 1024),
    )(results)
    return r_post, z_post.reshape(512), x_next.reshape(512)


def solution(mesh):
    in_specs = (
        P("rows", None),
        P("rows", None),
        P("rows", None),
        P("rows"),
        P("rows", None),
        P("rows"),
        P("rows"),
        P("rows", None),
        P("rows"),
        P("cols", None),
    )
    out_specs = (P("rows", "cols"), P("cols"), P("cols"))
    return jax.shard_map(
        per_device, mesh=mesh, in_specs=in_specs, out_specs=out_specs, check_vma=False
    )
```
